32 devices in a mesh: view: 8 (over z, core), tile: 4 (over y, x).
Axes of the slice: x: 2, y: 2, z: 4, core: 2. Of those that a mesh axis runs over, the one named last changes fastest.
Arguments:
- params: float32 [59, 32768], P(None, ('view', 'tile')), may hold values from -25 to 25, as said below
- first: float32 [59, 32768], P(None, ('view', 'tile')), may hold values from -0.3 to 0.3
- second: float32 [59, 32768], P(None, ('view', 'tile')), may hold values from 0.0001 to 0.01
- visible: int32 [8, 2048], P(None, ('view', 'tile')), may hold values from 0 to 1023, as said below
- cameras: float32 [8, 11], replicated, as said below
- tile_lists: int32 [8, 8, 1024], P('view', 'tile'), may hold values from 0 to 2047
- tile_blocks: int32 [8, 8], P('view', 'tile'), may hold values from 1 to 8, as said below
- targets: float32 [8, 3, 2048], P('view', None, 'tile'), may hold values from 0 to 1
Outputs:
- new_params: float32 [59, 32768], P(None, ('view', 'tile'))
- new_first: float32 [59, 32768], P(None, ('view', 'tile'))
- new_second: float32 [59, 32768], P(None, ('view', 'tile'))
- rendered: float32 [8, 3, 2048], P('view', None, 'tile')
The draws below stay inside these ranges and needn't reach their ends.
Inputs may be any that keep to these rules, and one draw needn't show every extreme that they name: `visible`: for each view and each owner (a run of 64 entries), distinct local columns of that owner. `tile_blocks`: number of live blocks of 128 entries at the head of each tile's list; the first tile of every view has all 8. `params`: rows 0 to 2 in -25 to 25; rows 3 to 5 in -6 to 2.5; row 6 in 1 to 2; rows 7 to 9 in -1 to 1; row 10 in -7.5 to -5.5; rows 11 to 58 in -1.2 to 1.2. `cameras`: column 0 in 0.5 to 1, columns 1 to 3 in -1 to 1, columns 4 and 5 in -0.3 to 0.3, column 6 in 6 to 9; focal lengths 0.7 to 1.1 times the larger side of the window of 128 by 16 pixels; the principal point within 8 pixels of the window's middle.
All inputs are finite; a program needn't handle non-finite values.
Results may differ from the reference program's by a relative error of at most 0.0003.
Values sent between devices are 32-bit elements; how exact they have to be, the bound alone decides.
A program may use at most 128 MiB of HBM per device.

```python
import math
import jax
import jax.numpy as jnp
from jax import lax

PARAMS = 59
SIDE = 16
PIX = 256
BLOCK = 128
BLOCKS = 8
WIN_COLS = 8
G_DEV = 1024
VIS_OWN = 64
TILES_DEV = 2
VIEWS = 8
OWNERS = 32
G_ALL = 32768
V_VIEW = 2048
TILES = 8
LIST = 1024
N_TILE = 4


reach_float = (2.0, 6.0, 20.0, 60.0)


reach_whole = (2, 6, 20, 60)


def window_sides():
    return (SIDE * WIN_COLS, SIDE * ((TILES + WIN_COLS - 1) // WIN_COLS))


def turn_matrix(real_part, axis_one, axis_two, axis_three):
    inverse = jax.lax.rsqrt(real_part * real_part + axis_one * axis_one + axis_two * axis_two + axis_three * axis_three)
    real_unit = real_part * inverse
    unit_one = axis_one * inverse
    unit_two = axis_two * inverse
    unit_three = axis_three * inverse
    return ((1.0 - 2.0 * (unit_two * unit_two + unit_three * unit_three), 2.0 * (unit_one * unit_two - real_unit * unit_three), 2.0 * (unit_one * unit_three + real_unit * unit_two)), (2.0 * (unit_one * unit_two + real_unit * unit_three), 1.0 - 2.0 * (unit_one * unit_one + unit_three * unit_three), 2.0 * (unit_two * unit_three - real_unit * unit_one)), (2.0 * (unit_one * unit_three - real_unit * unit_two), 2.0 * (unit_two * unit_three + real_unit * unit_one), 1.0 - 2.0 * (unit_one * unit_one + unit_two * unit_two)))


def camera_table(key):
    keys = jax.random.split(jax.random.fold_in(key, 11), 6)
    width, height = window_sides()
    larger = 1.0 * max(width, height)
    real_part = jax.random.uniform(keys[0], (VIEWS, 1), jnp.float32, 0.5, 1.0)
    axes_part = jax.random.uniform(keys[1], (VIEWS, 3), jnp.float32, -1.0, 1.0)
    shift_side = jax.random.uniform(keys[2], (VIEWS, 2), jnp.float32, -0.3, 0.3)
    shift_depth = jax.random.uniform(keys[3], (VIEWS, 1), jnp.float32, 6.0, 9.0)
    focal = jax.random.uniform(keys[4], (VIEWS, 2), jnp.float32, 0.7, 1.1) * larger
    centre = jnp.array([0.5 * width, 0.5 * height], jnp.float32) + jax.random.uniform(keys[5], (VIEWS, 2), jnp.float32, -8.0, 8.0)
    return jnp.concatenate([real_part, axes_part, shift_side, shift_depth, focal, centre], axis=1)


def layout(key):
    keys = jax.random.split(jax.random.fold_in(key, 12), 5)
    width, height = window_sides()
    shuffled = jax.vmap(lambda single: jax.random.permutation(single, G_DEV))(jax.random.split(keys[0], OWNERS)).astype(jnp.int32)
    across = jax.random.randint(keys[1], (VIEWS, V_VIEW), 0, width, jnp.int32)
    downward = jax.random.randint(keys[2], (VIEWS, V_VIEW), 0, height, jnp.int32)
    kinds = jax.random.randint(keys[3], (VIEWS, V_VIEW), 0, 4, jnp.int32)
    depth_rank = jax.vmap(lambda single: jax.random.permutation(single, V_VIEW))(jax.random.split(keys[4], VIEWS)).astype(jnp.int32)
    return (shuffled, across, downward, kinds, depth_rank)


def draw_cameras(key, part):
    return camera_table(key)


def draw_visible(key, part):
    shuffled, across, downward, kinds, depth_rank = layout(key)
    chosen = shuffled[:, :VIEWS * VIS_OWN].reshape(OWNERS, VIEWS, VIS_OWN)
    return jnp.transpose(chosen, (1, 0, 2)).reshape(VIEWS, OWNERS * VIS_OWN).astype(jnp.int32)


def draw_tile_lists(key, part):
    shuffled, across, downward, kinds, depth_rank = layout(key)
    tie_keys = jax.random.split(jax.random.fold_in(key, 15), VIEWS)
    reach_table = jnp.array(reach_whole, jnp.int32)
    tiles = jnp.arange(TILES, dtype=jnp.int32)
    left_edge = (SIDE * (tiles % WIN_COLS))[:, None]
    top_edge = (SIDE * (tiles // WIN_COLS))[:, None]

    def one_view(inputs):
        row_x, row_y, row_kind, row_rank, tie_key = inputs
        gap_x = jnp.maximum(jnp.maximum(left_edge - row_x[None, :], row_x[None, :] - (left_edge + SIDE - 1)), 0)
        gap_y = jnp.maximum(jnp.maximum(top_edge - row_y[None, :], row_y[None, :] - (top_edge + SIDE - 1)), 0)
        reach = jnp.take(reach_table, row_kind)
        nearness = jnp.minimum((gap_x * gap_x + gap_y * gap_y) * 64 // (reach * reach)[None, :], 16383)
        ties = jax.random.randint(tie_key, (TILES, V_VIEW), 0, 32768, jnp.int32)
        order = jnp.argsort(nearness * 32768 + ties, axis=1, stable=True)[:, :LIST]
        depth = jnp.take(row_rank, order)
        resort = jnp.argsort(depth, axis=1, stable=True)
        return jnp.take_along_axis(order, resort, axis=1).astype(jnp.int32)
    return lax.map(one_view, (across, downward, kinds, depth_rank, tie_keys)).astype(jnp.int32)


def draw_params(key, part):
    shuffled, across, downward, kinds, depth_rank = layout(key)
    cameras = camera_table(key)
    keys = jax.random.split(jax.random.fold_in(key, 13), 8)
    slot_of = jnp.argsort(shuffled, axis=1).reshape(-1).astype(jnp.int32)
    column = jnp.arange(G_ALL, dtype=jnp.int32)
    owner_index = column // G_DEV
    per_view = OWNERS // VIEWS
    is_seen = slot_of < VIEWS * VIS_OWN
    row_index = owner_index % per_view * (VIEWS * VIS_OWN) + owner_index // per_view * VIS_OWN + slot_of % VIS_OWN
    view_index = jnp.where(is_seen, slot_of // VIS_OWN, 0)
    row_index = jnp.where(is_seen, row_index, column % V_VIEW)
    spot_x = across[view_index, row_index].astype(jnp.float32) + jax.random.uniform(keys[0], (G_ALL,), jnp.float32, 0.0, 1.0)
    spot_y = downward[view_index, row_index].astype(jnp.float32) + jax.random.uniform(keys[1], (G_ALL,), jnp.float32, 0.0, 1.0)
    depth = 5.0 + 5.0 * (depth_rank[view_index, row_index].astype(jnp.float32) + 0.5) / V_VIEW
    camera = cameras[view_index]
    turn = turn_matrix(camera[:, 0], camera[:, 1], camera[:, 2], camera[:, 3])
    local_point = ((spot_x - camera[:, 9]) * depth / camera[:, 7] - camera[:, 4], (spot_y - camera[:, 10]) * depth / camera[:, 8] - camera[:, 5], depth - camera[:, 6])
    position = jnp.stack([turn[0][axis_at] * local_point[0] + turn[1][axis_at] * local_point[1] + turn[2][axis_at] * local_point[2] for axis_at in range(3)])
    reach = jnp.take(jnp.array(reach_float, jnp.float32), kinds[view_index, row_index]) * jnp.exp(jax.random.uniform(keys[2], (G_ALL,), jnp.float32, -0.2231, 0.2231))
    base_scale = jnp.log(reach * depth / jnp.sqrt(camera[:, 7] * camera[:, 8]))
    scales = base_scale[None, :] + jax.random.uniform(keys[3], (3, G_ALL), jnp.float32, -0.15, 0.15)
    opacity = jax.random.uniform(keys[4], (1, G_ALL), jnp.float32, -7.5, -5.5)
    colour = jnp.clip(0.3 * jax.random.normal(keys[5], (48, G_ALL), jnp.float32), -1.2, 1.2)
    real_part = jax.random.uniform(keys[6], (1, G_ALL), jnp.float32, 1.0, 2.0)
    others = jax.random.uniform(keys[7], (3, G_ALL), jnp.float32, -1.0, 1.0)
    return jnp.concatenate([position, scales, real_part, others, opacity, colour], axis=0)


def draw_tile_blocks(key, part):
    keys = jax.random.split(jax.random.fold_in(key, 14), 3)
    counts = jax.random.randint(keys[0], (VIEWS, TILES), 1, BLOCKS + 1, jnp.int32)
    others = jax.random.randint(keys[1], (VIEWS, TILES), 1, BLOCKS + 1, jnp.int32)
    heavy = jax.random.randint(keys[2], (VIEWS, TILES // TILES_DEV, 1), 0, 2, jnp.int32)
    heavy = jnp.broadcast_to(heavy, (VIEWS, TILES // TILES_DEV, TILES_DEV)).reshape(VIEWS, TILES)
    counts = jnp.where(heavy > 0, jnp.maximum(counts, others), jnp.minimum(counts, others))
    return counts.at[:, 0].set(BLOCKS).astype(jnp.int32)


def block_levels(key, shape, pieces, least, largest):
    def one(dim, blocks):
        heights = jax.random.uniform(jax.random.fold_in(jax.random.fold_in(key, 6), dim), (blocks,), jnp.float32, least / len(pieces), largest / len(pieces))
        return jnp.repeat(jnp.exp(heights), shape[dim] // blocks).reshape((-1,) + (1,) * (len(shape) - dim - 1))

    factor_of = one(*pieces[0])
    for cut in pieces[1:]:
        factor_of = factor_of * one(*cut)
    return factor_of


def centred(own_key, dims, scale, limit, cuts=(), held_as=jnp.bfloat16):
    level = block_levels(own_key, dims, cuts, -0.22, 0.18) if cuts else 1.0
    drawn = jax.random.normal(own_key, dims, jnp.float32) * scale * level
    return jnp.minimum(jnp.maximum(drawn, -limit), limit).astype(held_as)


def setup_inputs(seed: int = 0) -> dict:
    key_list = jax.random.split(jax.random.key(seed), 9)
    return {
        "params": draw_params(jax.random.fold_in(key_list[8], 71), 0),
        "first": centred(key_list[1], (PARAMS, G_ALL), 0.05, 0.3, ((1, 32),), jnp.float32),
        "second": jnp.clip(jnp.exp(math.log(0.01) - 4.6051702 * jax.random.uniform(key_list[2], (PARAMS, G_ALL), jnp.float32) ** block_levels(key_list[2], (PARAMS, G_ALL), ((1, 32),), -0.2, 0.2)), 0.0001, 0.01),
        "visible": draw_visible(jax.random.fold_in(key_list[8], 71), 0),
        "cameras": draw_cameras(jax.random.fold_in(key_list[8], 71), 0),
        "tile_lists": draw_tile_lists(jax.random.fold_in(key_list[8], 71), 0),
        "tile_blocks": draw_tile_blocks(jax.random.fold_in(key_list[8], 71), 0),
        "targets": jnp.clip(1.0 * jax.random.uniform(key_list[7], (VIEWS, 3, TILES * PIX), jnp.float32) ** block_levels(key_list[7], (VIEWS, 3, TILES * PIX), ((0, 8), (2, 4)), -0.2, 0.2), 0.0, 1.0),
    }


harm_zero = 0.28209479177387814
harm_one = 0.4886025119029199
harm_two = (1.0925484305920792, -1.0925484305920792, 0.31539156525252005, -1.0925484305920792, 0.5462742152960396)
harm_three = (-0.5900435899266435, 2.890611442640554, -0.4570457994644658, 0.3731763325901154, -0.4570457994644658, 1.445305721320277, -0.5900435899266435)
learn_rate = 0.05
beta_first = 0.9
beta_second = 0.999
adam_eps = 1e-08
blur_add = 0.3

def rotation(real_part, axis_one, axis_two, axis_three):
    inverse = lax.rsqrt(real_part * real_part + axis_one * axis_one + axis_two * axis_two + axis_three * axis_three)
    real_unit = real_part * inverse
    unit_one = axis_one * inverse
    unit_two = axis_two * inverse
    unit_three = axis_three * inverse
    return ((1.0 - 2.0 * (unit_two * unit_two + unit_three * unit_three), 2.0 * (unit_one * unit_two - real_unit * unit_three), 2.0 * (unit_one * unit_three + real_unit * unit_two)), (2.0 * (unit_one * unit_two + real_unit * unit_three), 1.0 - 2.0 * (unit_one * unit_one + unit_three * unit_three), 2.0 * (unit_two * unit_three - real_unit * unit_one)), (2.0 * (unit_one * unit_three - real_unit * unit_two), 2.0 * (unit_two * unit_three + real_unit * unit_one), 1.0 - 2.0 * (unit_one * unit_one + unit_two * unit_two)))

def harmonics(first_dir, second_dir, third_dir):
    sq_first = first_dir * first_dir
    sq_second = second_dir * second_dir
    sq_third = third_dir * third_dir
    return [harm_zero, -harm_one * second_dir, harm_one * third_dir, -harm_one * first_dir, harm_two[0] * first_dir * second_dir, harm_two[1] * second_dir * third_dir, harm_two[2] * (2.0 * sq_third - sq_first - sq_second), harm_two[3] * first_dir * third_dir, harm_two[4] * (sq_first - sq_second), harm_three[0] * second_dir * (3.0 * sq_first - sq_second), harm_three[1] * first_dir * second_dir * third_dir, harm_three[2] * second_dir * (4.0 * sq_third - sq_first - sq_second), harm_three[3] * third_dir * (2.0 * sq_third - 3.0 * sq_first - 3.0 * sq_second), harm_three[4] * first_dir * (4.0 * sq_third - sq_first - sq_second), harm_three[5] * third_dir * (sq_first - sq_second), harm_three[6] * first_dir * (sq_first - 3.0 * sq_second)]

def project(raw, camera):
    camera_turn = rotation(camera[0], camera[1], camera[2], camera[3])
    shift_vec = (camera[4], camera[5], camera[6])
    focal_x = camera[7]
    focal_y = camera[8]
    position = (raw[0], raw[1], raw[2])
    viewed = [camera_turn[across][0] * position[0] + camera_turn[across][1] * position[1] + camera_turn[across][2] * position[2] + shift_vec[across] for across in range(3)]
    inverse = 1.0 / viewed[2]
    mean_x = focal_x * viewed[0] * inverse + camera[9]
    mean_y = focal_y * viewed[1] * inverse + camera[10]
    gauss_turn = rotation(raw[6], raw[7], raw[8], raw[9])
    stretch = [jnp.exp(raw[3 + column]) for column in range(3)]
    jac_xx = focal_x * inverse
    jac_xz = -focal_x * viewed[0] * inverse * inverse
    jac_yy = focal_y * inverse
    jac_yz = -focal_y * viewed[1] * inverse * inverse
    leading_x = [jac_xx * camera_turn[0][column] + jac_xz * camera_turn[2][column] for column in range(3)]
    leading_y = [jac_yy * camera_turn[1][column] + jac_yz * camera_turn[2][column] for column in range(3)]
    axes_x = [(leading_x[0] * gauss_turn[0][column] + leading_x[1] * gauss_turn[1][column] + leading_x[2] * gauss_turn[2][column]) * stretch[column] for column in range(3)]
    axes_y = [(leading_y[0] * gauss_turn[0][column] + leading_y[1] * gauss_turn[1][column] + leading_y[2] * gauss_turn[2][column]) * stretch[column] for column in range(3)]
    cov_xx = axes_x[0] * axes_x[0] + axes_x[1] * axes_x[1] + axes_x[2] * axes_x[2] + blur_add
    cov_xy = axes_x[0] * axes_y[0] + axes_x[1] * axes_y[1] + axes_x[2] * axes_y[2]
    cov_yy = axes_y[0] * axes_y[0] + axes_y[1] * axes_y[1] + axes_y[2] * axes_y[2] + blur_add
    determ = cov_xx * cov_yy - cov_xy * cov_xy
    opacity = jax.nn.sigmoid(raw[10])
    camera_eye = [-(camera_turn[0][column] * shift_vec[0] + camera_turn[1][column] * shift_vec[1] + camera_turn[2][column] * shift_vec[2]) for column in range(3)]
    offset = [position[column] - camera_eye[column] for column in range(3)]
    length = lax.rsqrt(offset[0] * offset[0] + offset[1] * offset[1] + offset[2] * offset[2])
    harmonic_terms = harmonics(offset[0] * length, offset[1] * length, offset[2] * length)
    colours = []
    for channel in range(3):
        total = 0.5 + jnp.zeros_like(opacity)
        for harmonic in range(16):
            total = total + raw[11 + 16 * channel + harmonic] * harmonic_terms[harmonic]
        colours.append(total)
    return jnp.stack([mean_x, mean_y, cov_yy / determ, -cov_xy / determ, cov_xx / determ, opacity] + colours)

def composite(rows, anchor_x, anchor_y, count, lazy):
    pixel = jnp.arange(PIX, dtype=jnp.int32)
    pixel_x = (anchor_x + (pixel % SIDE).astype(jnp.float32) + 0.5)[:, None]
    pixel_y = (anchor_y + (pixel // SIDE).astype(jnp.float32) + 0.5)[:, None]
    ahead = (lax.broadcasted_iota(jnp.int32, (BLOCK, BLOCK), 0) < lax.broadcasted_iota(jnp.int32, (BLOCK, BLOCK), 1)).astype(jnp.float32)
    current = (jnp.zeros((PIX,), jnp.float32), jnp.zeros((3, PIX), jnp.float32))
    for block in range(rows.shape[1] // BLOCK):
        piece = rows[:, block * BLOCK:(block + 1) * BLOCK]
        live = (block < count).astype(jnp.float32)

        def advance(holder, piece=piece, live=live):
            carried, image = holder
            delta_x = pixel_x - piece[0][None, :]
            delta_y = pixel_y - piece[1][None, :]
            power = piece[2][None, :] * delta_x * delta_x + 2.0 * piece[3][None, :] * delta_x * delta_y + piece[4][None, :] * delta_y * delta_y
            alpha = piece[5][None, :] * jnp.exp(-0.5 * power) * live
            decay = jnp.log1p(-alpha)
            before = jnp.dot(decay, ahead, precision=lax.Precision.HIGHEST, preferred_element_type=jnp.float32) + carried[:, None]
            weight = alpha * jnp.exp(before)
            image = image + lax.dot_general(piece[6:9], weight, (((1,), (1,)), ((), ())), precision=lax.Precision.HIGHEST, preferred_element_type=jnp.float32)
            return (carried + lax.optimization_barrier(jnp.sum(decay, axis=1)), image)
        if lazy:
            current = lax.cond(block < count, advance, lambda holder: holder, current)
        else:
            current = advance(current)
    return current[1]

def reference(params, first, second, visible, cameras, tile_lists, tile_blocks, targets):
    places = jnp.arange(V_VIEW, dtype=jnp.int32)
    within = places % VIS_OWN
    source_view = places // VIS_OWN % VIEWS
    source_tile = places // (VIEWS * VIS_OWN)
    owner = source_view * N_TILE + source_tile

    def one_view(carry, view):
        grad_total, hits = carry
        local = jnp.take(visible[view], owner * VIS_OWN + within)
        columns = (owner * G_DEV + local).astype(jnp.int32)
        raw = jnp.take(params, columns, axis=1)
        camera = cameras[view]
        projected, pullback = jax.vjp(lambda source: project(source, camera), raw)

        def one_tile(tile_index):
            listed = tile_lists[view, tile_index]
            rows = jnp.take(projected, listed, axis=1)
            anchor_x = (tile_index % WIN_COLS * SIDE).astype(jnp.float32)
            anchor_y = (tile_index // WIN_COLS * SIDE).astype(jnp.float32)
            count = tile_blocks[view, tile_index]
            image, pull = jax.vjp(lambda source: composite(source, anchor_x, anchor_y, count, False), rows)
            goal = lax.dynamic_slice_in_dim(targets[view], tile_index * PIX, PIX, 1)
            rows_grad, = pull(2.0 * (image - goal))
            return (image, rows_grad)
        images, row_grads = lax.map(one_tile, jnp.arange(TILES, dtype=jnp.int32))
        flat = tile_lists[view].reshape(-1)
        spread = jnp.transpose(row_grads, (1, 0, 2)).reshape(9, -1)
        projected_grad = jnp.zeros((9, V_VIEW), jnp.float32).at[:, flat].add(spread)
        raw_grad, = pullback(projected_grad)
        grad_total = grad_total.at[:, columns].add(raw_grad)
        hits = hits.at[columns].add(1.0)
        return ((grad_total, hits), jnp.transpose(images, (1, 0, 2)).reshape(3, TILES * PIX))
    start = (jnp.zeros((PARAMS, G_ALL), jnp.float32), jnp.zeros((G_ALL,), jnp.float32))
    (grad, hits), rendered = lax.scan(one_view, start, jnp.arange(VIEWS, dtype=jnp.int32))
    seen = (hits > 0.5)[None, :]
    moved_first = beta_first * first + (1.0 - beta_first) * grad
    moved_second = beta_second * second + (1.0 - beta_second) * grad * grad
    moved_params = params - learn_rate * moved_first / (jnp.sqrt(moved_second) + adam_eps)
    new_first = jnp.where(seen, moved_first, first)
    new_second = jnp.where(seen, moved_second, second)
    new_params = jnp.where(seen, moved_params, params)
    return (new_params, new_first, new_second, rendered)
```

```python
import functools

import jax
import jax.numpy as jnp
from jax import lax
from jax.experimental import pallas as pl
from jax.experimental.pallas import tpu as pltpu
from jax.sharding import PartitionSpec as P

SIDE = 16
PIX = 256
BLOCK = 128
WIN_COLS = 8
SUBS = 8
MESH = pl.DeviceIdType.MESH
VMEM = pl.BlockSpec(memory_space=pltpu.VMEM)
SMEM = pl.BlockSpec(memory_space=pltpu.SMEM)
LIMIT = 48 * 1024 * 1024


harm_zero = 0.28209479177387814
harm_one = 0.4886025119029199
harm_two = (
    1.0925484305920792,
    -1.0925484305920792,
    0.31539156525252005,
    -1.0925484305920792,
    0.5462742152960396,
)
harm_three = (
    -0.5900435899266435,
    2.890611442640554,
    -0.4570457994644658,
    0.3731763325901154,
    -0.4570457994644658,
    1.445305721320277,
    -0.5900435899266435,
)
learn_rate = 0.05
beta_first = 0.9
beta_second = 0.999
adam_eps = 1e-08
blur_add = 0.3


def rotation(real_part, axis_one, axis_two, axis_three):
    inverse = lax.rsqrt(
        real_part * real_part + axis_one * axis_one + axis_two * axis_two + axis_three * axis_three
    )
    real_unit = real_part * inverse
    unit_one = axis_one * inverse
    unit_two = axis_two * inverse
    unit_three = axis_three * inverse
    return (
        (
            1.0 - 2.0 * (unit_two * unit_two + unit_three * unit_three),
            2.0 * (unit_one * unit_two - real_unit * unit_three),
            2.0 * (unit_one * unit_three + real_unit * unit_two),
        ),
        (
            2.0 * (unit_one * unit_two + real_unit * unit_three),
            1.0 - 2.0 * (unit_one * unit_one + unit_three * unit_three),
            2.0 * (unit_two * unit_three - real_unit * unit_one),
        ),
        (
            2.0 * (unit_one * unit_three - real_unit * unit_two),
            2.0 * (unit_two * unit_three + real_unit * unit_one),
            1.0 - 2.0 * (unit_one * unit_one + unit_two * unit_two),
        ),
    )


def harmonics(first_dir, second_dir, third_dir):
    sq_first = first_dir * first_dir
    sq_second = second_dir * second_dir
    sq_third = third_dir * third_dir
    return [
        harm_zero,
        -harm_one * second_dir,
        harm_one * third_dir,
        -harm_one * first_dir,
        harm_two[0] * first_dir * second_dir,
        harm_two[1] * second_dir * third_dir,
        harm_two[2] * (2.0 * sq_third - sq_first - sq_second),
        harm_two[3] * first_dir * third_dir,
        harm_two[4] * (sq_first - sq_second),
        harm_three[0] * second_dir * (3.0 * sq_first - sq_second),
        harm_three[1] * first_dir * second_dir * third_dir,
        harm_three[2] * second_dir * (4.0 * sq_third - sq_first - sq_second),
        harm_three[3] * third_dir * (2.0 * sq_third - 3.0 * sq_first - 3.0 * sq_second),
        harm_three[4] * first_dir * (4.0 * sq_third - sq_first - sq_second),
        harm_three[5] * third_dir * (sq_first - sq_second),
        harm_three[6] * first_dir * (sq_first - 3.0 * sq_second),
    ]


def project(raw, camera):
    camera_turn = rotation(camera[0], camera[1], camera[2], camera[3])
    shift_vec = (camera[4], camera[5], camera[6])
    focal_x = camera[7]
    focal_y = camera[8]
    position = (raw[0], raw[1], raw[2])
    viewed = [
        camera_turn[across][0] * position[0]
        + camera_turn[across][1] * position[1]
        + camera_turn[across][2] * position[2]
        + shift_vec[across]
        for across in range(3)
    ]
    inverse = 1.0 / viewed[2]
    mean_x = focal_x * viewed[0] * inverse + camera[9]
    mean_y = focal_y * viewed[1] * inverse + camera[10]
    gauss_turn = rotation(raw[6], raw[7], raw[8], raw[9])
    stretch = [jnp.exp(raw[3 + column]) for column in range(3)]
    jac_xx = focal_x * inverse
    jac_xz = -focal_x * viewed[0] * inverse * inverse
    jac_yy = focal_y * inverse
    jac_yz = -focal_y * viewed[1] * inverse * inverse
    leading_x = [
        jac_xx * camera_turn[0][column] + jac_xz * camera_turn[2][column] for column in range(3)
    ]
    leading_y = [
        jac_yy * camera_turn[1][column] + jac_yz * camera_turn[2][column] for column in range(3)
    ]
    axes_x = [
        (
            leading_x[0] * gauss_turn[0][column]
            + leading_x[1] * gauss_turn[1][column]
            + leading_x[2] * gauss_turn[2][column]
        )
        * stretch[column]
        for column in range(3)
    ]
    axes_y = [
        (
            leading_y[0] * gauss_turn[0][column]
            + leading_y[1] * gauss_turn[1][column]
            + leading_y[2] * gauss_turn[2][column]
        )
        * stretch[column]
        for column in range(3)
    ]
    cov_xx = axes_x[0] * axes_x[0] + axes_x[1] * axes_x[1] + axes_x[2] * axes_x[2] + blur_add
    cov_xy = axes_x[0] * axes_y[0] + axes_x[1] * axes_y[1] + axes_x[2] * axes_y[2]
    cov_yy = axes_y[0] * axes_y[0] + axes_y[1] * axes_y[1] + axes_y[2] * axes_y[2] + blur_add
    determ = cov_xx * cov_yy - cov_xy * cov_xy
    opacity = 1.0 / (1.0 + jnp.exp(-raw[10]))
    camera_eye = [
        -(
            camera_turn[0][column] * shift_vec[0]
            + camera_turn[1][column] * shift_vec[1]
            + camera_turn[2][column] * shift_vec[2]
        )
        for column in range(3)
    ]
    offset = [position[column] - camera_eye[column] for column in range(3)]
    length = lax.rsqrt(offset[0] * offset[0] + offset[1] * offset[1] + offset[2] * offset[2])
    harmonic_terms = harmonics(offset[0] * length, offset[1] * length, offset[2] * length)
    colours = []
    for channel in range(3):
        total = 0.5 + jnp.zeros_like(opacity)
        for harmonic in range(16):
            total = total + raw[11 + 16 * channel + harmonic] * harmonic_terms[harmonic]
        colours.append(total)
    return [mean_x, mean_y, cov_yy / determ, -cov_xy / determ, cov_xx / determ, opacity] + colours


def three_pieces(value):
    high = value.astype(jnp.bfloat16)
    rest = value - high.astype(jnp.float32)
    middle = rest.astype(jnp.bfloat16)
    low = (rest - middle.astype(jnp.float32)).astype(jnp.bfloat16)
    return high, middle, low


def two_pieces(value):
    high = value.astype(jnp.bfloat16)
    return high, (value - high.astype(jnp.float32)).astype(jnp.bfloat16)


def matmul(left, right):
    return jnp.dot(left, right, preferred_element_type=jnp.float32)


def matmul_nt(left, right):
    return lax.dot_general(
        left, right, (((1,), (1,)), ((), ())), preferred_element_type=jnp.float32
    )


def column_hot(visible_ref, columns):
    views = visible_ref.shape[0]
    ids = jnp.concatenate([visible_ref[view : view + 1, :] for view in range(views)], axis=1)
    place = lax.broadcasted_iota(jnp.int32, (columns, ids.shape[1]), 0)
    return jnp.where(place == ids, 1.0, 0.0).astype(jnp.bfloat16)


def camera_rows(cameras_ref, own_rows):
    views = cameras_ref.shape[0]
    lane = lax.broadcasted_iota(jnp.int32, (1, views * own_rows), 1)
    rows = []
    for entry in range(11):
        row = jnp.full(lane.shape, cameras_ref[0, entry], jnp.float32)
        for view in range(1, views):
            row = jnp.where(lane >= view * own_rows, cameras_ref[view, entry], row)
        rows.append(row)
    return rows


def send_kernel(
    views, tiles, params_ref, visible_ref, cameras_ref, all_ref, picked_ref, outgoing,
    view_send, view_recv, tile_send, tile_recv
):
    my_view, my_tile = lax.axis_index("view"), lax.axis_index("tile")
    barrier = pltpu.get_barrier_semaphore()
    for step in range(1, views):
        pl.semaphore_signal(
            barrier, inc=1, device_id=(lax.rem(my_view + step, views), my_tile), device_id_type=MESH
        )
    for step in range(1, tiles):
        pl.semaphore_signal(
            barrier, inc=1, device_id=(my_view, lax.rem(my_tile + step, tiles)), device_id_type=MESH
        )
    width, columns = params_ref.shape
    own_rows = visible_ref.shape[1]
    hot = column_hot(visible_ref, columns)
    padded = jnp.concatenate(
        [params_ref[...], jnp.zeros((64 - width, columns), jnp.float32)], axis=0
    )
    parts = matmul(jnp.concatenate(three_pieces(padded), axis=0), hot)
    picked_ref[...] = parts[0:64] + parts[64:128] + parts[128:192]
    cameras = camera_rows(cameras_ref, own_rows)
    raw = [picked_ref[row : row + 1, :] for row in range(width)]
    out = project(raw, cameras)
    zero = jnp.zeros_like(out[0])
    lower = jnp.concatenate(out[0:4] + [out[8], zero, zero, zero], axis=0)
    upper = jnp.concatenate(out[4:8] + [zero, zero, zero, zero], axis=0)
    for view in range(views):
        span = slice(view * own_rows, (view + 1) * own_rows)
        outgoing[view] = jnp.concatenate([lower[:, span], upper[:, span]], axis=1)
    pl.semaphore_wait(barrier, views + tiles - 2)
    for step in range(1, views):
        other = lax.rem(my_view + step, views)
        pltpu.make_async_remote_copy(
            src_ref=outgoing.at[other], dst_ref=all_ref.at[my_tile, my_view],
            send_sem=view_send.at[other], recv_sem=view_recv.at[my_view],
            device_id=(other, my_tile), device_id_type=MESH,
        ).start()
    all_ref[my_tile, my_view] = outgoing[my_view]
    for step in range(1, views):
        other = lax.rem(my_view + step, views)
        pltpu.make_async_remote_copy(
            src_ref=outgoing.at[other], dst_ref=all_ref.at[my_tile, other],
            send_sem=view_send.at[other], recv_sem=view_recv.at[other],
            device_id=(other, my_tile), device_id_type=MESH,
        ).wait_recv()
    for step in range(1, tiles):
        other = lax.rem(my_tile + step, tiles)
        pltpu.make_async_remote_copy(
            src_ref=all_ref.at[my_tile], dst_ref=all_ref.at[my_tile],
            send_sem=tile_send.at[other], recv_sem=tile_recv.at[my_tile],
            device_id=(my_view, other), device_id_type=MESH,
        ).start()
    for step in range(1, views):
        other = lax.rem(my_view + step, views)
        pltpu.make_async_remote_copy(
            src_ref=outgoing.at[other], dst_ref=all_ref.at[my_tile, my_view],
            send_sem=view_send.at[other], recv_sem=view_recv.at[my_view],
            device_id=(other, my_tile), device_id_type=MESH,
        ).wait_send()
    for step in range(1, tiles):
        other = lax.rem(my_tile + step, tiles)
        copy = pltpu.make_async_remote_copy(
            src_ref=all_ref.at[my_tile], dst_ref=all_ref.at[other],
            send_sem=tile_send.at[other], recv_sem=tile_recv.at[other],
            device_id=(my_view, other), device_id_type=MESH,
        )
        copy.wait_send()
        copy.wait_recv()


def return_kernel(
    views, tiles, given_ref, out_ref, landed, summed, view_send, view_recv, tile_send, tile_recv
):
    my_view, my_tile = lax.axis_index("view"), lax.axis_index("tile")
    barrier = pltpu.get_barrier_semaphore()
    for step in range(1, views):
        pl.semaphore_signal(
            barrier, inc=1, device_id=(lax.rem(my_view + step, views), my_tile), device_id_type=MESH
        )
    for step in range(1, tiles):
        pl.semaphore_signal(
            barrier, inc=1, device_id=(my_view, lax.rem(my_tile + step, tiles)), device_id_type=MESH
        )
    pl.semaphore_wait(barrier, views + tiles - 2)
    for step in range(1, tiles):
        other = lax.rem(my_tile + step, tiles)
        pltpu.make_async_remote_copy(
            src_ref=given_ref.at[other], dst_ref=landed.at[my_tile],
            send_sem=tile_send.at[other], recv_sem=tile_recv.at[my_tile],
            device_id=(my_view, other), device_id_type=MESH,
        ).start()
    total = given_ref[my_tile]
    for step in range(1, tiles):
        other = lax.rem(my_tile + step, tiles)
        pltpu.make_async_remote_copy(
            src_ref=given_ref.at[other], dst_ref=landed.at[other],
            send_sem=tile_send.at[other], recv_sem=tile_recv.at[other],
            device_id=(my_view, other), device_id_type=MESH,
        ).wait_recv()
        total = total + landed[other]
    summed[...] = total
    for step in range(1, views):
        other = lax.rem(my_view + step, views)
        pltpu.make_async_remote_copy(
            src_ref=summed.at[other], dst_ref=out_ref.at[my_view],
            send_sem=view_send.at[other], recv_sem=view_recv.at[my_view],
            device_id=(other, my_tile), device_id_type=MESH,
        ).start()
    out_ref[my_view] = summed[my_view]
    for step in range(1, tiles):
        other = lax.rem(my_tile + step, tiles)
        pltpu.make_async_remote_copy(
            src_ref=given_ref.at[other], dst_ref=landed.at[my_tile],
            send_sem=tile_send.at[other], recv_sem=tile_recv.at[my_tile],
            device_id=(my_view, other), device_id_type=MESH,
        ).wait_send()
    for step in range(1, views):
        other = lax.rem(my_view + step, views)
        copy = pltpu.make_async_remote_copy(
            src_ref=summed.at[other], dst_ref=out_ref.at[other],
            send_sem=view_send.at[other], recv_sem=view_recv.at[other],
            device_id=(other, my_tile), device_id_type=MESH,
        )
        copy.wait_send()
        copy.wait_recv()


def list_hot(lists_ref, tile, own_rows):
    ids = lists_ref[tile : tile + 1, :]
    place = lax.broadcasted_iota(jnp.int32, (2 * own_rows, ids.shape[1]), 0)
    low_ids = lax.rem(ids, own_rows)
    lower = jnp.where(place == low_ids, 1.0, 0.0).astype(jnp.bfloat16)
    upper = jnp.where(place == low_ids + own_rows, 1.0, 0.0).astype(jnp.bfloat16)
    return lax.div(ids, own_rows), lower, upper


def composite_kernel(
    owners, chunk, all_ref, lists_ref, counts_ref, targets_ref, given_ref, image_ref,
    rows, grads, weights, weight_parts, ratios, carried, held
):
    tiles = lists_ref.shape[0]
    entries = lists_ref.shape[1]
    own_rows = all_ref.shape[1] // 2
    chunk_rows = chunk * SUBS
    most = counts_ref[0, 0]
    for tile in range(1, tiles):
        most = jnp.maximum(most, counts_ref[0, tile])

    for tile in range(tiles):
        owner_ids, lower, upper = list_hot(lists_ref, tile, own_rows)
        lower3 = jnp.concatenate([lower] * 3, axis=0)
        upper3 = jnp.concatenate([upper] * 3, axis=0)

        def gather(index, held_rows):
            start = pl.multiple_of(index * chunk_rows, chunk_rows)
            source = jnp.concatenate(three_pieces(all_ref[pl.ds(start, chunk_rows), :]), axis=1)
            found_low = matmul(source, lower3)
            found_up = matmul(source, upper3)
            low, up = held_rows
            for owner in range(chunk):
                mine = (owner_ids == index * chunk + owner).astype(jnp.float32)
                span = slice(owner * SUBS, (owner + 1) * SUBS)
                low = low + found_low[span] * mine
                up = up + found_up[span] * mine
            return low, up

        empty = jnp.zeros((SUBS, entries), jnp.float32)
        low, up = lax.fori_loop(0, owners // chunk, gather, (empty, empty))
        rows[tile, 0:SUBS, :] = low
        rows[tile, SUBS : 2 * SUBS, :] = up

    first_tile = lax.axis_index("tile") * tiles
    half = SIDE // 2
    middles = []
    for tile in range(tiles):
        number = first_tile + tile
        middles.append(
            (
                (lax.rem(number, WIN_COLS) * SIDE + half).astype(jnp.float32),
                (lax.div(number, WIN_COLS) * SIDE + half).astype(jnp.float32),
            )
        )
    side_x = lax.broadcasted_iota(jnp.int32, (SIDE, BLOCK), 0).astype(jnp.float32) + (0.5 - half)
    spot = lax.broadcasted_iota(jnp.int32, (2 * BLOCK, 2 * BLOCK), 0) % BLOCK
    lane = lax.broadcasted_iota(jnp.int32, (2 * BLOCK, 2 * BLOCK), 1)
    ahead = jnp.where((spot < lane) | (lane >= BLOCK), 1.0, 0.0).astype(jnp.bfloat16)
    behind = jnp.where((spot > lane) | (lane >= BLOCK), 1.0, 0.0).astype(jnp.bfloat16)

    carried[...] = jnp.zeros_like(carried)
    held[...] = jnp.zeros_like(held)
    grads[...] = jnp.zeros_like(grads)

    def forward(block, _):
        start = pl.multiple_of(block * BLOCK, BLOCK)
        for tile in range(tiles):
            live = (block < counts_ref[0, tile]).astype(jnp.float32)
            low = rows[tile, 0:SUBS, pl.ds(start, BLOCK)]
            up = rows[tile, SUBS : 2 * SUBS, pl.ds(start, BLOCK)]
            mean_x = low[0:1] - middles[tile][0]
            mean_y = low[1:2] - middles[tile][1]
            form_a = -0.5 * low[2:3]
            form_b = -low[3:4]
            form_c = -0.5 * up[0:1]
            opacity = up[1:2] * live
            delta_x = side_x - mean_x
            square = form_a * delta_x * delta_x
            cross = form_b * delta_x
            pieces = []
            for line in range(SIDE):
                delta_y = (line + 0.5 - half) - mean_y
                pieces.append((cross + form_c * delta_y) * delta_y + square)
            alpha = opacity * jnp.exp(jnp.concatenate(pieces, axis=0))
            decay = jnp.log(1.0 - alpha)
            before = matmul(jnp.concatenate(two_pieces(decay), axis=1), ahead)
            past = carried[tile]
            weight = alpha * jnp.exp(before[:, 0:BLOCK] + past)
            carried[tile] = past + before[:, BLOCK:]
            ratios[tile, block] = alpha * jnp.exp(-decay)
            weights[tile, block] = weight
            parts = jnp.concatenate(two_pieces(weight), axis=1)
            weight_parts[tile, block] = parts
            colour = jnp.concatenate([up[2:4], low[4:5], jnp.zeros((5, BLOCK), jnp.float32)], axis=0)
            high = colour.astype(jnp.bfloat16).astype(jnp.float32)
            both = jnp.concatenate([high, colour - high], axis=0).astype(jnp.bfloat16)
            held[tile] += matmul_nt(parts, jnp.concatenate([both, both], axis=1))
        return 0

    lax.fori_loop(0, most, forward, 0)

    slopes, slopes_wide = [], []
    for tile in range(tiles):
        drawn = jnp.transpose(
            jnp.concatenate(
                [held[tile], jnp.zeros((PIX, BLOCK - 2 * SUBS), jnp.float32)], axis=1
            )
        )
        drawn = drawn[0:3] + drawn[SUBS : SUBS + 3]
        image_ref[:, tile * PIX : (tile + 1) * PIX] = drawn
        slope = 2.0 * (drawn - targets_ref[:, tile * PIX : (tile + 1) * PIX])
        high = slope.astype(jnp.bfloat16).astype(jnp.float32)
        stack = jnp.concatenate(
            [high, slope - high, high, jnp.zeros((BLOCK - 9, PIX), jnp.float32)], axis=0
        )
        slopes.append(stack[0 : 2 * SUBS].astype(jnp.bfloat16))
        slopes_wide.append(jnp.transpose(stack).astype(jnp.bfloat16)[:, 0 : 2 * SUBS])

    pixel = lax.broadcasted_iota(jnp.int32, (2 * SUBS, PIX), 1)
    kind = lax.broadcasted_iota(jnp.int32, (2 * SUBS, PIX), 0)
    at_x = (pixel % SIDE).astype(jnp.float32) + (0.5 - half)
    at_y = (pixel // SIDE).astype(jnp.float32) + (0.5 - half)
    power_x = jnp.where((kind == 1) | (kind == 4), at_x, jnp.where(kind == 3, at_x * at_x, 1.0))
    power_y = jnp.where((kind == 2) | (kind == 4), at_y, jnp.where(kind == 5, at_y * at_y, 1.0))
    basis = jnp.where(kind < 6, power_x * power_y, 0.0).astype(jnp.bfloat16)

    carried[...] = jnp.zeros_like(carried)

    def backward(index, _):
        block = most - 1 - index
        start = pl.multiple_of(block * BLOCK, BLOCK)
        for tile in range(tiles):
            low = rows[tile, 0:SUBS, pl.ds(start, BLOCK)]
            up = rows[tile, SUBS : 2 * SUBS, pl.ds(start, BLOCK)]
            colour = jnp.concatenate([up[2:4], low[4:5]], axis=0)
            high = colour.astype(jnp.bfloat16).astype(jnp.float32)
            both = jnp.concatenate(
                [high, high, colour - high, jnp.zeros((7, BLOCK), jnp.float32)], axis=0
            ).astype(jnp.bfloat16)
            pulled = matmul(slopes_wide[tile], both) * weights[tile, block]
            after = matmul(jnp.concatenate(two_pieces(pulled), axis=1), behind)
            past = carried[tile]
            inner = pulled - (after[:, 0:BLOCK] + past) * ratios[tile, block]
            carried[tile] = past + after[:, BLOCK:]
            inner_high, inner_low = two_pieces(inner)
            sums = matmul(basis, inner_high) + matmul(basis, inner_low)
            parts = weight_parts[tile, block]
            tint = matmul(slopes[tile], parts[:, 0:BLOCK])
            tint_low = matmul(slopes[tile], parts[:, BLOCK:])
            tint = tint[0:3] + tint[3:6] + tint_low[0:3]
            mean_x = low[0:1] - middles[tile][0]
            mean_y = low[1:2] - middles[tile][1]
            form_a, form_b, form_c = low[2:3], low[3:4], up[0:1]
            whole, by_x, by_y = sums[0:1], sums[1:2], sums[2:3]
            sum_x = by_x - mean_x * whole
            sum_y = by_y - mean_y * whole
            sum_xx = sums[3:4] - 2.0 * mean_x * by_x + mean_x * mean_x * whole
            sum_xy = sums[4:5] - mean_x * by_y - mean_y * by_x + mean_x * mean_y * whole
            sum_yy = sums[5:6] - 2.0 * mean_y * by_y + mean_y * mean_y * whole
            zeros = jnp.zeros((4, BLOCK), jnp.float32)
            grads[tile, 0:SUBS, pl.ds(start, BLOCK)] = jnp.concatenate(
                [
                    form_a * sum_x + form_b * sum_y,
                    form_b * sum_x + form_c * sum_y,
                    -0.5 * sum_xx,
                    -sum_xy,
                    tint[2:3],
                    zeros[0:3],
                ],
                axis=0,
            )
            grads[tile, SUBS : 2 * SUBS, pl.ds(start, BLOCK)] = jnp.concatenate(
                [-0.5 * sum_yy, whole / up[1:2], tint[0:2], zeros], axis=0
            )
        return 0

    lax.fori_loop(0, most, backward, 0)

    def scatter(index, _):
        begin = pl.multiple_of(index * chunk_rows, chunk_rows)
        total = jnp.zeros((chunk_rows, 2 * own_rows), jnp.float32)
        owner = lax.broadcasted_iota(jnp.int32, (chunk_rows, entries), 0) // SUBS + index * chunk
        for tile in range(tiles):
            owner_ids, lower, upper = list_hot(lists_ref, tile, own_rows)
            mine = owner == owner_ids
            for part, hot in ((0, lower), (1, upper)):
                values = grads[tile, part * SUBS : (part + 1) * SUBS, :]
                high = values.astype(jnp.bfloat16).astype(jnp.float32)
                for piece in (high, values - high):
                    spread = jnp.concatenate([piece] * chunk, axis=0)
                    total = total + matmul_nt(
                        jnp.where(mine, spread, 0.0).astype(jnp.bfloat16), hot
                    )
        given_ref[pl.ds(begin, chunk_rows), :] = total
        return 0

    lax.fori_loop(0, owners // chunk, scatter, 0)


def update_kernel(
    params_ref, first_ref, second_ref, visible_ref, cameras_ref, picked_ref, arrived_ref,
    new_params_ref, new_first_ref, new_second_ref, slopes
):
    width, columns = params_ref.shape
    views, own_rows = visible_ref.shape
    lower = jnp.concatenate([arrived_ref[view][:, 0:own_rows] for view in range(views)], axis=1)
    upper = jnp.concatenate([arrived_ref[view][:, own_rows:] for view in range(views)], axis=1)
    cotangent = [lower[row : row + 1] for row in range(4)]
    cotangent += [upper[row : row + 1] for row in range(4)]
    cotangent += [lower[4:5]]
    cameras = camera_rows(cameras_ref, own_rows)
    raw = [picked_ref[row : row + 1, :] for row in range(width)]
    _, pullback = jax.vjp(lambda source: project(source, cameras), raw)
    (returned,) = pullback(cotangent)
    slopes[...] = jnp.ones_like(slopes)
    for row in range(width):
        slopes[row : row + 1, :] = returned[row]
    hot = column_hot(visible_ref, columns)
    parts = matmul_nt(jnp.concatenate(three_pieces(slopes[...]), axis=0), hot)
    grad = parts[0:64] + parts[64:128] + parts[128:192]
    seen = grad[width : width + 1] > 0.5
    grad = grad[0:width]
    first, second, params = first_ref[...], second_ref[...], params_ref[...]
    moved_first = beta_first * first + (1.0 - beta_first) * grad
    moved_second = beta_second * second + (1.0 - beta_second) * grad * grad
    moved_params = params - learn_rate * moved_first / (jnp.sqrt(moved_second) + adam_eps)
    new_first_ref[...] = jnp.where(seen, moved_first, first)
    new_second_ref[...] = jnp.where(seen, moved_second, second)
    new_params_ref[...] = jnp.where(seen, moved_params, params)


def shards(views, tiles, params, first, second, visible, cameras, tile_lists, tile_blocks, targets):
    own_rows = visible.shape[1]
    owners = views * tiles
    per_device, entries = tile_lists.shape[1:]
    blocks = entries // BLOCK
    block_shape = (SUBS, 2 * own_rows)
    f32 = jnp.float32
    dma = pltpu.SemaphoreType.DMA
    everyone, picked = pl.pallas_call(
        functools.partial(send_kernel, views, tiles),
        out_shape=[
            jax.ShapeDtypeStruct((tiles, views) + block_shape, f32),
            jax.ShapeDtypeStruct((64, views * own_rows), f32),
        ],
        in_specs=[VMEM, VMEM, SMEM],
        out_specs=[VMEM, VMEM],
        scratch_shapes=[
            pltpu.VMEM((views,) + block_shape, f32),
            dma((views,)), dma((views,)), dma((tiles,)), dma((tiles,)),
        ],
        compiler_params=pltpu.CompilerParams(
            collective_id=0, has_side_effects=True, vmem_limit_bytes=LIMIT
        ),
        name="project_send",
    )(params, visible, cameras)
    chunk = min(owners, 32)
    given, rendered = pl.pallas_call(
        functools.partial(composite_kernel, owners, chunk),
        out_shape=[
            jax.ShapeDtypeStruct((owners * SUBS, 2 * own_rows), f32),
            jax.ShapeDtypeStruct((3, per_device * PIX), f32),
        ],
        in_specs=[VMEM, VMEM, SMEM, VMEM],
        out_specs=[VMEM, VMEM],
        scratch_shapes=[
            pltpu.VMEM((per_device, 2 * SUBS, entries), f32),
            pltpu.VMEM((per_device, 2 * SUBS, entries), f32),
            pltpu.VMEM((per_device, blocks, PIX, BLOCK), f32),
            pltpu.VMEM((per_device, blocks, PIX, 2 * BLOCK), jnp.bfloat16),
            pltpu.VMEM((per_device, blocks, PIX, BLOCK), f32),
            pltpu.VMEM((per_device, PIX, BLOCK), f32),
            pltpu.VMEM((per_device, PIX, 2 * SUBS), f32),
        ],
        compiler_params=pltpu.CompilerParams(vmem_limit_bytes=LIMIT),
        name="composite",
    )(everyone.reshape(owners * SUBS, 2 * own_rows), tile_lists[0], tile_blocks, targets[0])
    arrived = pl.pallas_call(
        functools.partial(return_kernel, views, tiles),
        out_shape=jax.ShapeDtypeStruct((views,) + block_shape, f32),
        in_specs=[VMEM],
        out_specs=VMEM,
        scratch_shapes=[
            pltpu.VMEM((tiles, views) + block_shape, f32),
            pltpu.VMEM((views,) + block_shape, f32),
            dma((views,)), dma((views,)), dma((tiles,)), dma((tiles,)),
        ],
        compiler_params=pltpu.CompilerParams(
            collective_id=1, has_side_effects=True, vmem_limit_bytes=LIMIT
        ),
        name="gradient_return",
    )(given.reshape((tiles, views) + block_shape))
    like = jax.ShapeDtypeStruct(params.shape, f32)
    new_params, new_first, new_second = pl.pallas_call(
        update_kernel,
        out_shape=[like, like, like],
        in_specs=[VMEM, VMEM, VMEM, VMEM, SMEM, VMEM, VMEM],
        out_specs=[VMEM, VMEM, VMEM],
        scratch_shapes=[pltpu.VMEM((64, views * own_rows), f32)],
        compiler_params=pltpu.CompilerParams(vmem_limit_bytes=LIMIT),
        name="update",
    )(params, first, second, visible, cameras, picked, arrived)
    return (new_params, new_first, new_second, rendered[None])


def solution(mesh):
    in_specs = (
        P(None, ("view", "tile")),
        P(None, ("view", "tile")),
        P(None, ("view", "tile")),
        P(None, ("view", "tile")),
        P(),
        P("view", "tile", None),
        P("view", "tile"),
        P("view", None, "tile"),
    )
    out_specs = (
        P(None, ("view", "tile")),
        P(None, ("view", "tile")),
        P(None, ("view", "tile")),
        P("view", None, "tile"),
    )
    body = functools.partial(shards, mesh.shape["view"], mesh.shape["tile"])
    return jax.shard_map(body, mesh=mesh, in_specs=in_specs, out_specs=out_specs, check_vma=False)
```

```python
import functools

import jax
import jax.numpy as jnp
from jax import lax
from jax.experimental import pallas as pl
from jax.experimental.pallas import tpu as pltpu
from jax.sharding import PartitionSpec as P

SIDE = 16
PIX = 256
BLOCK = 128
WIN_COLS = 8
SUBS = 8
MESH = pl.DeviceIdType.MESH
VMEM = pl.BlockSpec(memory_space=pltpu.VMEM)
ANY = pl.BlockSpec(memory_space=pl.ANY)
SMEM = pl.BlockSpec(memory_space=pltpu.SMEM)
LIMIT = 48 * 1024 * 1024


harm_zero = 0.28209479177387814
harm_one = 0.4886025119029199
harm_two = (
    1.0925484305920792,
    -1.0925484305920792,
    0.31539156525252005,
    -1.0925484305920792,
    0.5462742152960396,
)
harm_three = (
    -0.5900435899266435,
    2.890611442640554,
    -0.4570457994644658,
    0.3731763325901154,
    -0.4570457994644658,
    1.445305721320277,
    -0.5900435899266435,
)
learn_rate = 0.05
beta_first = 0.9
beta_second = 0.999
adam_eps = 1e-08
blur_add = 0.3


def rotation(real_part, axis_one, axis_two, axis_three):
    inverse = lax.rsqrt(
        real_part * real_part + axis_one * axis_one + axis_two * axis_two + axis_three * axis_three
    )
    real_unit = real_part * inverse
    unit_one = axis_one * inverse
    unit_two = axis_two * inverse
    unit_three = axis_three * inverse
    return (
        (
            1.0 - 2.0 * (unit_two * unit_two + unit_three * unit_three),
            2.0 * (unit_one * unit_two - real_unit * unit_three),
            2.0 * (unit_one * unit_three + real_unit * unit_two),
        ),
        (
            2.0 * (unit_one * unit_two + real_unit * unit_three),
            1.0 - 2.0 * (unit_one * unit_one + unit_three * unit_three),
            2.0 * (unit_two * unit_three - real_unit * unit_one),
        ),
        (
            2.0 * (unit_one * unit_three - real_unit * unit_two),
            2.0 * (unit_two * unit_three + real_unit * unit_one),
            1.0 - 2.0 * (unit_one * unit_one + unit_two * unit_two),
        ),
    )


def harmonics(first_dir, second_dir, third_dir):
    sq_first = first_dir * first_dir
    sq_second = second_dir * second_dir
    sq_third = third_dir * third_dir
    return [
        harm_zero,
        -harm_one * second_dir,
        harm_one * third_dir,
        -harm_one * first_dir,
        harm_two[0] * first_dir * second_dir,
        harm_two[1] * second_dir * third_dir,
        harm_two[2] * (2.0 * sq_third - sq_first - sq_second),
        harm_two[3] * first_dir * third_dir,
        harm_two[4] * (sq_first - sq_second),
        harm_three[0] * second_dir * (3.0 * sq_first - sq_second),
        harm_three[1] * first_dir * second_dir * third_dir,
        harm_three[2] * second_dir * (4.0 * sq_third - sq_first - sq_second),
        harm_three[3] * third_dir * (2.0 * sq_third - 3.0 * sq_first - 3.0 * sq_second),
        harm_three[4] * first_dir * (4.0 * sq_third - sq_first - sq_second),
        harm_three[5] * third_dir * (sq_first - sq_second),
        harm_three[6] * first_dir * (sq_first - 3.0 * sq_second),
    ]


def project(raw, camera):
    camera_turn = rotation(camera[0], camera[1], camera[2], camera[3])
    shift_vec = (camera[4], camera[5], camera[6])
    focal_x = camera[7]
    focal_y = camera[8]
    position = (raw[0], raw[1], raw[2])
    viewed = [
        camera_turn[across][0] * position[0]
        + camera_turn[across][1] * position[1]
        + camera_turn[across][2] * position[2]
        + shift_vec[across]
        for across in range(3)
    ]
    inverse = 1.0 / viewed[2]
    mean_x = focal_x * viewed[0] * inverse + camera[9]
    mean_y = focal_y * viewed[1] * inverse + camera[10]
    gauss_turn = rotation(raw[6], raw[7], raw[8], raw[9])
    stretch = [jnp.exp(raw[3 + column]) for column in range(3)]
    jac_xx = focal_x * inverse
    jac_xz = -focal_x * viewed[0] * inverse * inverse
    jac_yy = focal_y * inverse
    jac_yz = -focal_y * viewed[1] * inverse * inverse
    leading_x = [
        jac_xx * camera_turn[0][column] + jac_xz * camera_turn[2][column] for column in range(3)
    ]
    leading_y = [
        jac_yy * camera_turn[1][column] + jac_yz * camera_turn[2][column] for column in range(3)
    ]
    axes_x = [
        (
            leading_x[0] * gauss_turn[0][column]
            + leading_x[1] * gauss_turn[1][column]
            + leading_x[2] * gauss_turn[2][column]
        )
        * stretch[column]
        for column in range(3)
    ]
    axes_y = [
        (
            leading_y[0] * gauss_turn[0][column]
            + leading_y[1] * gauss_turn[1][column]
            + leading_y[2] * gauss_turn[2][column]
        )
        * stretch[column]
        for column in range(3)
    ]
    cov_xx = axes_x[0] * axes_x[0] + axes_x[1] * axes_x[1] + axes_x[2] * axes_x[2] + blur_add
    cov_xy = axes_x[0] * axes_y[0] + axes_x[1] * axes_y[1] + axes_x[2] * axes_y[2]
    cov_yy = axes_y[0] * axes_y[0] + axes_y[1] * axes_y[1] + axes_y[2] * axes_y[2] + blur_add
    determ = cov_xx * cov_yy - cov_xy * cov_xy
    opacity = 1.0 / (1.0 + jnp.exp(-raw[10]))
    camera_eye = [
        -(
            camera_turn[0][column] * shift_vec[0]
            + camera_turn[1][column] * shift_vec[1]
            + camera_turn[2][column] * shift_vec[2]
        )
        for column in range(3)
    ]
    offset = [position[column] - camera_eye[column] for column in range(3)]
    length = lax.rsqrt(offset[0] * offset[0] + offset[1] * offset[1] + offset[2] * offset[2])
    harmonic_terms = harmonics(offset[0] * length, offset[1] * length, offset[2] * length)
    colours = []
    for channel in range(3):
        total = 0.5 + jnp.zeros_like(opacity)
        for harmonic in range(16):
            total = total + raw[11 + 16 * channel + harmonic] * harmonic_terms[harmonic]
        colours.append(total)
    return [mean_x, mean_y, cov_yy / determ, -cov_xy / determ, cov_xx / determ, opacity] + colours


def three_pieces(value):
    high = value.astype(jnp.bfloat16)
    rest = value - high.astype(jnp.float32)
    middle = rest.astype(jnp.bfloat16)
    low = (rest - middle.astype(jnp.float32)).astype(jnp.bfloat16)
    return high, middle, low


def two_pieces(value):
    high = value.astype(jnp.bfloat16)
    return high, (value - high.astype(jnp.float32)).astype(jnp.bfloat16)


def matmul(left, right):
    return jnp.dot(left, right, preferred_element_type=jnp.float32)


def matmul_nt(left, right):
    return lax.dot_general(
        left, right, (((1,), (1,)), ((), ())), preferred_element_type=jnp.float32
    )


def column_hot(visible_ref, columns):
    views = visible_ref.shape[0]
    ids = jnp.concatenate([visible_ref[view : view + 1, :] for view in range(views)], axis=1)
    place = lax.broadcasted_iota(jnp.int32, (columns, ids.shape[1]), 0)
    return jnp.where(place == ids, 1.0, 0.0).astype(jnp.bfloat16)


def camera_rows(cameras_ref, own_rows):
    views = cameras_ref.shape[0]
    lane = lax.broadcasted_iota(jnp.int32, (1, views * own_rows), 1)
    rows = []
    for entry in range(11):
        row = jnp.full(lane.shape, cameras_ref[0, entry], jnp.float32)
        for view in range(1, views):
            row = jnp.where(lane >= view * own_rows, cameras_ref[view, entry], row)
        rows.append(row)
    return rows


def list_hot(lists, lanes):
    place = lax.broadcasted_iota(jnp.int32, (lanes, lists.shape[1]), 0)
    hot = jnp.where(place == lax.bitwise_and(lists, lanes - 1), 1.0, 0.0).astype(jnp.bfloat16)
    return hot, lax.shift_right_logical(lists, lanes.bit_length() - 1)


def step_kernel(
    views, tiles, params_hbm, visible_ref, cameras_ref, lists_hbm, counts_ref, targets_ref,
    picked_ref, arrived_ref, image_ref,
    params_ref, lists_ref, outgoing, everyone, hots, hots_wide, rows, grads, weights,
    weight_parts, ratios, carried, held, given, landed, summed,
    load_sem, out_sem, out_recv, spread_sem, spread_recv, view_send, view_recv, tile_send, tile_recv
):
    my_view, my_tile = lax.axis_index("view"), lax.axis_index("tile")
    others_view = [lax.rem(my_view + step, views) for step in range(1, views)]
    others_tile = [lax.rem(my_tile + step, tiles) for step in range(1, tiles)]
    barrier = pltpu.get_barrier_semaphore()
    for other in others_view:
        pl.semaphore_signal(barrier, inc=1, device_id=(other, my_tile), device_id_type=MESH)
    for other in others_tile:
        pl.semaphore_signal(barrier, inc=1, device_id=(my_view, other), device_id_type=MESH)
    load_params = pltpu.make_async_copy(params_hbm, params_ref, load_sem.at[0])
    load_lists = pltpu.make_async_copy(lists_hbm, lists_ref, load_sem.at[1])
    load_params.start()
    load_lists.start()

    width, columns = params_ref.shape
    own_rows = visible_ref.shape[1]
    wide = 2 * own_rows
    hot = column_hot(visible_ref, columns)
    cameras = camera_rows(cameras_ref, own_rows)
    load_params.wait()
    padded = jnp.concatenate(
        [params_ref[...], jnp.zeros((64 - width, columns), jnp.float32)], axis=0
    )
    found = matmul(jnp.concatenate(three_pieces(padded), axis=0), hot)
    picked_ref[...] = found[0:64] + found[64:128] + found[128:192]
    raw = [picked_ref[row : row + 1, :] for row in range(width)]
    out = project(raw, cameras)
    lower = jnp.concatenate(out[0:8], axis=0)
    upper = jnp.concatenate([out[8], jnp.zeros((7, out[8].shape[1]), jnp.float32)], axis=0)
    for view in range(views):
        span = slice(view * own_rows, (view + 1) * own_rows)
        outgoing[view] = jnp.concatenate([lower[:, span], upper[:, span]], axis=1)

    def to_view(source, other, landing, sends, receives, slot):
        return pltpu.make_async_remote_copy(
            src_ref=source.at[other], dst_ref=landing, send_sem=sends.at[other],
            recv_sem=receives.at[slot], device_id=(other, my_tile), device_id_type=MESH,
        )

    def spread(place, view, other, slot):
        return pltpu.make_async_remote_copy(
            src_ref=everyone.at[my_tile, view], dst_ref=everyone.at[place, view],
            send_sem=spread_sem.at[other, view], recv_sem=spread_recv.at[slot, view],
            device_id=(my_view, other), device_id_type=MESH,
        )

    everyone[my_tile, my_view] = outgoing[my_view]
    pl.semaphore_wait(barrier, views + tiles - 2)
    for other in others_view:
        to_view(outgoing, other, everyone.at[my_tile, my_view], out_sem, out_recv, my_view).start()
    for other in others_tile:
        spread(my_tile, my_view, other, my_tile).start()

    load_lists.wait()
    per_device, entries = lists_ref.shape
    groups, groups_wide = [], []
    for tile in range(per_device):
        ids = lists_ref[tile : tile + 1, :]
        narrow, group = list_hot(ids, own_rows)
        hots[tile] = jnp.concatenate([narrow] * 4, axis=0)
        groups.append(jnp.broadcast_to(group, (SUBS, entries)))
        hots_wide[tile], group = list_hot(ids, wide)
        groups_wide.append(jnp.broadcast_to(group, (SUBS, entries)))

    for other in others_view:
        to_view(outgoing, other, everyone.at[my_tile, other], out_sem, out_recv, other).wait_recv()
        for peer in others_tile:
            spread(my_tile, other, peer, my_tile).start()
    for other in others_view:
        to_view(outgoing, other, everyone.at[my_tile, my_view], out_sem, out_recv, my_view).wait_send()
    for peer in others_tile:
        for view in range(views):
            copy = spread(peer, view, peer, peer)
            copy.wait_send()
            copy.wait_recv()

    batch = max(1, min(tiles, 32 // views))
    chunk = batch * views
    lane = lax.broadcasted_iota(jnp.int32, (chunk * (SUBS + 1), wide), 1)

    def gather(index, held_rows):
        source = everyone[pl.ds(index * batch, batch)].reshape(chunk, SUBS, wide)
        last = pltpu.roll(source[:, 0, :], own_rows, 1)
        source = jnp.concatenate([source.reshape(chunk * SUBS, wide), last], axis=0)
        high, middle, low = [piece.astype(jnp.float32) for piece in three_pieces(source)]
        source = jnp.concatenate(
            [
                jnp.where(lane < own_rows, high, pltpu.roll(middle, own_rows, 1)),
                jnp.where(lane < own_rows, low, 0.0),
            ],
            axis=1,
        ).astype(jnp.bfloat16)
        new_rows = []
        for tile in range(per_device):
            located = matmul(source, hots[tile])
            first, second = held_rows[tile]
            for owner in range(chunk):
                mine = groups[tile] == index * chunk + owner
                first = first + jnp.where(mine, located[owner * SUBS : (owner + 1) * SUBS], 0.0)
            for start in range(0, chunk, SUBS):
                begin = chunk * SUBS + start
                number = lax.broadcasted_iota(jnp.int32, (SUBS, entries), 0) + (
                    index * chunk + start
                )
                second = second + jnp.where(
                    groups[tile] == number, located[begin : begin + SUBS], 0.0
                )
            new_rows.append((first, second))
        return tuple(new_rows)

    empty = jnp.zeros((SUBS, entries), jnp.float32)
    collected = lax.fori_loop(0, tiles // batch, gather, ((empty, empty),) * per_device)
    for tile in range(per_device):
        rows[tile, 0:SUBS, :] = collected[tile][0]
        rows[tile, SUBS : 2 * SUBS, :] = jnp.broadcast_to(
            jnp.sum(collected[tile][1], axis=0, keepdims=True), (SUBS, entries)
        )

    first_tile = my_tile * per_device
    half = SIDE // 2
    middles = []
    for tile in range(per_device):
        number = first_tile + tile
        middles.append(
            (
                (lax.rem(number, WIN_COLS) * SIDE + half).astype(jnp.float32),
                (lax.div(number, WIN_COLS) * SIDE + half).astype(jnp.float32),
            )
        )
    side_x = lax.broadcasted_iota(jnp.int32, (SIDE, BLOCK), 0).astype(jnp.float32) + (0.5 - half)
    spot = lax.bitwise_and(
        lax.broadcasted_iota(jnp.int32, (2 * BLOCK, 2 * BLOCK), 0), BLOCK - 1
    )
    lane_two = lax.broadcasted_iota(jnp.int32, (2 * BLOCK, 2 * BLOCK), 1)
    ahead = jnp.where((spot < lane_two) | (lane_two >= BLOCK), 1.0, 0.0).astype(jnp.bfloat16)
    behind = jnp.where((spot > lane_two) | (lane_two >= BLOCK), 1.0, 0.0).astype(jnp.bfloat16)
    blocks = entries // BLOCK

    carried[...] = jnp.zeros_like(carried)
    held[...] = jnp.zeros_like(held)

    def forward(block, _):
        start = pl.multiple_of(block * BLOCK, BLOCK)
        for tile in range(per_device):
            live = (block < counts_ref[0, tile]).astype(jnp.float32)
            low = rows[tile, 0:SUBS, pl.ds(start, BLOCK)]
            up = rows[tile, SUBS : 2 * SUBS, pl.ds(start, BLOCK)]
            mean_x = low[0:1] - middles[tile][0]
            mean_y = low[1:2] - middles[tile][1]
            form_a = -0.5 * low[2:3]
            form_b = -low[3:4]
            form_c = -0.5 * low[4:5]
            opacity = low[5:6] * live
            delta_x = side_x - mean_x
            square = form_a * delta_x * delta_x
            cross = form_b * delta_x
            pieces = []
            for line in range(SIDE):
                delta_y = (line + 0.5 - half) - mean_y
                pieces.append((cross + form_c * delta_y) * delta_y + square)
            alpha = opacity * jnp.exp(jnp.concatenate(pieces, axis=0))
            decay = jnp.log(1.0 - alpha)
            before = matmul(jnp.concatenate(two_pieces(decay), axis=1), ahead)
            past = carried[tile]
            weight = alpha * jnp.exp(before[:, 0:BLOCK] + past)
            carried[tile] = past + before[:, BLOCK:]
            ratios[tile, block] = alpha * jnp.exp(-decay)
            weights[tile, block] = weight
            parts = jnp.concatenate(two_pieces(weight), axis=1)
            weight_parts[tile, block] = parts
            colour = jnp.concatenate([low[6:8], up[0:1], jnp.zeros((5, BLOCK), jnp.float32)], axis=0)
            high = colour.astype(jnp.bfloat16).astype(jnp.float32)
            both = jnp.concatenate([high, colour - high], axis=0).astype(jnp.bfloat16)
            held[tile] += matmul_nt(parts, jnp.concatenate([both, both], axis=1))
        return 0

    lax.fori_loop(0, blocks, forward, 0)

    slopes, slopes_wide = [], []
    for tile in range(per_device):
        drawn = jnp.transpose(
            jnp.concatenate(
                [held[tile], jnp.zeros((PIX, BLOCK - 2 * SUBS), jnp.float32)], axis=1
            )
        )
        drawn = drawn[0:3] + drawn[SUBS : SUBS + 3]
        image_ref[:, 0, tile * PIX : (tile + 1) * PIX] = drawn
        slope = 2.0 * (drawn - targets_ref[:, 0, tile * PIX : (tile + 1) * PIX])
        high = slope.astype(jnp.bfloat16).astype(jnp.float32)
        stack = jnp.concatenate(
            [high, slope - high, high, jnp.zeros((BLOCK - 9, PIX), jnp.float32)], axis=0
        )
        slopes.append(stack[0 : 2 * SUBS].astype(jnp.bfloat16))
        slopes_wide.append(jnp.transpose(stack).astype(jnp.bfloat16)[:, 0 : 2 * SUBS])

    pixel = lax.broadcasted_iota(jnp.int32, (2 * SUBS, PIX), 1)
    kind = lax.broadcasted_iota(jnp.int32, (2 * SUBS, PIX), 0)
    at_x = lax.bitwise_and(pixel, SIDE - 1).astype(jnp.float32) + (0.5 - half)
    at_y = lax.shift_right_logical(pixel, SIDE.bit_length() - 1).astype(jnp.float32) + (0.5 - half)
    power_x = jnp.where((kind == 1) | (kind == 4), at_x, jnp.where(kind == 3, at_x * at_x, 1.0))
    power_y = jnp.where((kind == 2) | (kind == 4), at_y, jnp.where(kind == 5, at_y * at_y, 1.0))
    basis = jnp.where(kind < 6, power_x * power_y, 0.0).astype(jnp.bfloat16)

    carried[...] = jnp.zeros_like(carried)

    def backward(index, _):
        block = blocks - 1 - index
        start = pl.multiple_of(block * BLOCK, BLOCK)
        for tile in range(per_device):
            low = rows[tile, 0:SUBS, pl.ds(start, BLOCK)]
            up = rows[tile, SUBS : 2 * SUBS, pl.ds(start, BLOCK)]
            colour = jnp.concatenate([low[6:8], up[0:1]], axis=0)
            high = colour.astype(jnp.bfloat16).astype(jnp.float32)
            both = jnp.concatenate(
                [high, high, colour - high, jnp.zeros((7, BLOCK), jnp.float32)], axis=0
            ).astype(jnp.bfloat16)
            pulled = matmul(slopes_wide[tile], both) * weights[tile, block]
            after = matmul(jnp.concatenate(two_pieces(pulled), axis=1), behind)
            past = carried[tile]
            inner = pulled - (after[:, 0:BLOCK] + past) * ratios[tile, block]
            carried[tile] = past + after[:, BLOCK:]
            inner_high, inner_low = two_pieces(inner)
            sums = matmul(basis, inner_high) + matmul(basis, inner_low)
            parts = weight_parts[tile, block]
            tint = matmul(slopes[tile], parts[:, 0:BLOCK])
            tint_low = matmul(slopes[tile], parts[:, BLOCK:])
            tint = tint[0:3] + tint[3:6] + tint_low[0:3]
            mean_x = low[0:1] - middles[tile][0]
            mean_y = low[1:2] - middles[tile][1]
            form_a, form_b, form_c = low[2:3], low[3:4], low[4:5]
            whole, by_x, by_y = sums[0:1], sums[1:2], sums[2:3]
            sum_x = by_x - mean_x * whole
            sum_y = by_y - mean_y * whole
            sum_xx = sums[3:4] - 2.0 * mean_x * by_x + mean_x * mean_x * whole
            sum_xy = sums[4:5] - mean_x * by_y - mean_y * by_x + mean_x * mean_y * whole
            sum_yy = sums[5:6] - 2.0 * mean_y * by_y + mean_y * mean_y * whole
            grads[tile, 0:SUBS, pl.ds(start, BLOCK)] = jnp.concatenate(
                [
                    form_a * sum_x + form_b * sum_y,
                    form_b * sum_x + form_c * sum_y,
                    -0.5 * sum_xx,
                    -sum_xy,
                    -0.5 * sum_yy,
                    whole / low[5:6],
                    tint[0:2],
                ],
                axis=0,
            )
            grads[tile, SUBS : 2 * SUBS, pl.ds(start, BLOCK)] = jnp.broadcast_to(
                tint[2:3], (SUBS, BLOCK)
            )
        return 0

    lax.fori_loop(0, blocks, backward, 0)

    pairs = chunk // 2
    lane_pair = lax.broadcasted_iota(jnp.int32, (pairs, SUBS, wide), 2)

    def scatter(index, _):
        total = jnp.zeros((2 * pairs * (SUBS + 1), wide), jnp.float32)
        for tile in range(per_device):
            main = grads[tile, 0:SUBS, :]
            last = grads[tile, SUBS : 2 * SUBS, :]
            parts = [[], [], [], []]
            main_high = main.astype(jnp.bfloat16).astype(jnp.float32)
            last_high = last.astype(jnp.bfloat16).astype(jnp.float32)
            for pair in range(pairs):
                mine = groups_wide[tile] == index * pairs + pair
                parts[0].append(jnp.where(mine, main_high, 0.0))
                parts[1].append(jnp.where(mine, main - main_high, 0.0))
            for start in range(0, pairs, SUBS):
                number = lax.broadcasted_iota(jnp.int32, (SUBS, entries), 0) + (
                    index * pairs + start
                )
                mine = groups_wide[tile] == number
                parts[2].append(jnp.where(mine, last_high, 0.0))
                parts[3].append(jnp.where(mine, last - last_high, 0.0))
            left = jnp.concatenate(parts[0] + parts[1] + parts[2] + parts[3], axis=0)
            total = total + matmul_nt(left.astype(jnp.bfloat16), hots_wide[tile])
        size = pairs * SUBS
        main = (total[0:size] + total[size : 2 * size]).reshape(pairs, SUBS, wide)
        last = total[2 * size : 2 * size + pairs] + total[2 * size + pairs :]
        turned = pltpu.roll(last, own_rows, 1)
        even = jnp.where(
            lane_pair < own_rows, main, jnp.broadcast_to(turned[:, None, :], main.shape)
        )
        odd = jnp.where(
            lane_pair < own_rows,
            pltpu.roll(main, own_rows, 2),
            jnp.broadcast_to(last[:, None, :], main.shape),
        )
        for pair in range(pairs):
            place = index * batch + 2 * pair // views
            given[place, 2 * pair % views] = even[pair]
            given[place, 2 * pair % views + 1] = odd[pair]
        return 0

    lax.fori_loop(0, tiles // batch, scatter, 0)

    def to_tile(other, place, slot):
        return pltpu.make_async_remote_copy(
            src_ref=given.at[other], dst_ref=landed.at[place], send_sem=tile_send.at[other],
            recv_sem=tile_recv.at[slot], device_id=(my_view, other), device_id_type=MESH,
        )

    for other in others_tile:
        to_tile(other, my_tile, my_tile).start()
    total = given[my_tile]
    for other in others_tile:
        to_tile(other, other, other).wait_recv()
        total = total + landed[other]
    summed[...] = total
    for other in others_view:
        to_view(summed, other, arrived_ref.at[my_view], view_send, view_recv, my_view).start()
    arrived_ref[my_view] = summed[my_view]
    for other in others_tile:
        to_tile(other, my_tile, my_tile).wait_send()
    for other in others_view:
        copy = to_view(summed, other, arrived_ref.at[other], view_send, view_recv, other)
        copy.wait_send()
        copy.wait_recv()


def update_kernel(
    params_hbm, first_hbm, second_hbm, visible_ref, cameras_ref, picked_ref, arrived_ref, drawn_ref,
    new_params_hbm, new_first_hbm, new_second_hbm, image_ref,
    params_ref, first_ref, second_ref, new_params, new_first, new_second, slopes, load_sem, store_sem
):
    loads = [
        pltpu.make_async_copy(params_hbm, params_ref, load_sem.at[0]),
        pltpu.make_async_copy(first_hbm, first_ref, load_sem.at[1]),
        pltpu.make_async_copy(second_hbm, second_ref, load_sem.at[2]),
    ]
    for load in loads:
        load.start()
    image_ref[...] = drawn_ref[...]
    width, columns = params_ref.shape
    views, own_rows = visible_ref.shape
    lower = jnp.concatenate([arrived_ref[view][:, 0:own_rows] for view in range(views)], axis=1)
    upper = jnp.concatenate([arrived_ref[view][:, own_rows:] for view in range(views)], axis=1)
    cotangent = [lower[row : row + 1] for row in range(8)] + [upper[0:1]]
    cameras = camera_rows(cameras_ref, own_rows)
    raw = [picked_ref[row : row + 1, :] for row in range(width)]
    _, pullback = jax.vjp(lambda source: project(source, cameras), raw)
    (returned,) = pullback(cotangent)
    slopes[...] = jnp.ones_like(slopes)
    for row in range(width):
        slopes[row : row + 1, :] = returned[row]
    hot = column_hot(visible_ref, columns)
    parts = matmul_nt(jnp.concatenate(three_pieces(slopes[...]), axis=0), hot)
    grad = parts[0:64] + parts[64:128] + parts[128:192]
    seen = grad[width : width + 1] > 0.5
    grad = grad[0:width]
    for load in loads:
        load.wait()
    first, second, params = first_ref[...], second_ref[...], params_ref[...]
    moved_first = beta_first * first + (1.0 - beta_first) * grad
    moved_second = beta_second * second + (1.0 - beta_second) * grad * grad
    new_first[...] = jnp.where(seen, moved_first, first)
    store_first = pltpu.make_async_copy(new_first, new_first_hbm, store_sem.at[1])
    store_first.start()
    new_second[...] = jnp.where(seen, moved_second, second)
    store_second = pltpu.make_async_copy(new_second, new_second_hbm, store_sem.at[2])
    store_second.start()
    moved_params = params - learn_rate * moved_first / (jnp.sqrt(moved_second) + adam_eps)
    new_params[...] = jnp.where(seen, moved_params, params)
    store_params = pltpu.make_async_copy(new_params, new_params_hbm, store_sem.at[0])
    store_params.start()
    store_first.wait()
    store_second.wait()
    store_params.wait()


def shards(views, tiles, params, first, second, visible, cameras, tile_lists, tile_blocks, targets):
    own_rows = visible.shape[1]
    per_device, entries = tile_lists.shape[1:]
    blocks = entries // BLOCK
    packet = (SUBS, 2 * own_rows)
    f32 = jnp.float32
    dma = pltpu.SemaphoreType.DMA
    image_shape = jax.ShapeDtypeStruct((3, 1, per_device * PIX), f32)
    picked, arrived, drawn = pl.pallas_call(
        functools.partial(step_kernel, views, tiles),
        out_shape=[
            jax.ShapeDtypeStruct((64, views * own_rows), f32),
            jax.ShapeDtypeStruct((views,) + packet, f32),
            image_shape,
        ],
        in_specs=[ANY, VMEM, SMEM, ANY, SMEM, VMEM],
        out_specs=[VMEM, VMEM, VMEM],
        scratch_shapes=[
            pltpu.VMEM(params.shape, f32),
            pltpu.VMEM((per_device, entries), jnp.int32),
            pltpu.VMEM((views,) + packet, f32),
            pltpu.VMEM((tiles, views) + packet, f32),
            pltpu.VMEM((per_device, 4 * own_rows, entries), jnp.bfloat16),
            pltpu.VMEM((per_device, 2 * own_rows, entries), jnp.bfloat16),
            pltpu.VMEM((per_device, 2 * SUBS, entries), f32),
            pltpu.VMEM((per_device, 2 * SUBS, entries), f32),
            pltpu.VMEM((per_device, blocks, PIX, BLOCK), f32),
            pltpu.VMEM((per_device, blocks, PIX, 2 * BLOCK), jnp.bfloat16),
            pltpu.VMEM((per_device, blocks, PIX, BLOCK), f32),
            pltpu.VMEM((per_device, PIX, BLOCK), f32),
            pltpu.VMEM((per_device, PIX, 2 * SUBS), f32),
            pltpu.VMEM((tiles, views) + packet, f32),
            pltpu.VMEM((tiles, views) + packet, f32),
            pltpu.VMEM((views,) + packet, f32),
            dma((2,)),
            dma((views,)), dma((views,)), dma((tiles, views)), dma((tiles, views)),
            dma((views,)), dma((views,)), dma((tiles,)), dma((tiles,)),
        ],
        compiler_params=pltpu.CompilerParams(
            collective_id=0, has_side_effects=True, vmem_limit_bytes=LIMIT
        ),
        name="render_step",
    )(params, visible, cameras, tile_lists[0], tile_blocks, jnp.transpose(targets, (1, 0, 2)))
    like = jax.ShapeDtypeStruct(params.shape, f32)
    new_params, new_first, new_second, rendered = pl.pallas_call(
        update_kernel,
        out_shape=[like, like, like, image_shape],
        in_specs=[ANY, ANY, ANY, VMEM, SMEM, VMEM, VMEM, VMEM],
        out_specs=[ANY, ANY, ANY, VMEM],
        scratch_shapes=[pltpu.VMEM(params.shape, f32)] * 6
        + [pltpu.VMEM((64, views * own_rows), f32), dma((3,)), dma((3,))],
        compiler_params=pltpu.CompilerParams(vmem_limit_bytes=LIMIT),
        name="update",
    )(params, first, second, visible, cameras, picked, arrived, drawn)
    return (new_params, new_first, new_second, jnp.transpose(rendered, (1, 0, 2)))


def solution(mesh):
    in_specs = (
        P(None, ("view", "tile")),
        P(None, ("view", "tile")),
        P(None, ("view", "tile")),
        P(None, ("view", "tile")),
        P(),
        P("view", "tile", None),
        P("view", "tile"),
        P("view", None, "tile"),
    )
    out_specs = (
        P(None, ("view", "tile")),
        P(None, ("view", "tile")),
        P(None, ("view", "tile")),
        P("view", None, "tile"),
    )
    body = functools.partial(shards, mesh.shape["view"], mesh.shape["tile"])
    return jax.shard_map(body, mesh=mesh, in_specs=in_specs, out_specs=out_specs, check_vma=False)
```

```python
import functools

import jax
import jax.numpy as jnp
from jax import lax
from jax.experimental import pallas as pl
from jax.experimental.pallas import tpu as pltpu
from jax.sharding import PartitionSpec as P

SIDE = 16
PIX = 256
BLOCK = 128
WIN_COLS = 8
SUBS = 8
MESH = pl.DeviceIdType.MESH
VMEM = pl.BlockSpec(memory_space=pltpu.VMEM)
ANY = pl.BlockSpec(memory_space=pl.ANY)
SMEM = pl.BlockSpec(memory_space=pltpu.SMEM)
LIMIT = 62 * 1024 * 1024


harm_zero = 0.28209479177387814
harm_one = 0.4886025119029199
harm_two = (
    1.0925484305920792,
    -1.0925484305920792,
    0.31539156525252005,
    -1.0925484305920792,
    0.5462742152960396,
)
harm_three = (
    -0.5900435899266435,
    2.890611442640554,
    -0.4570457994644658,
    0.3731763325901154,
    -0.4570457994644658,
    1.445305721320277,
    -0.5900435899266435,
)
learn_rate = 0.05
beta_first = 0.9
beta_second = 0.999
adam_eps = 1e-08
blur_add = 0.3


def rotation(real_part, axis_one, axis_two, axis_three):
    inverse = lax.rsqrt(
        real_part * real_part + axis_one * axis_one + axis_two * axis_two + axis_three * axis_three
    )
    real_unit = real_part * inverse
    unit_one = axis_one * inverse
    unit_two = axis_two * inverse
    unit_three = axis_three * inverse
    return (
        (
            1.0 - 2.0 * (unit_two * unit_two + unit_three * unit_three),
            2.0 * (unit_one * unit_two - real_unit * unit_three),
            2.0 * (unit_one * unit_three + real_unit * unit_two),
        ),
        (
            2.0 * (unit_one * unit_two + real_unit * unit_three),
            1.0 - 2.0 * (unit_one * unit_one + unit_three * unit_three),
            2.0 * (unit_two * unit_three - real_unit * unit_one),
        ),
        (
            2.0 * (unit_one * unit_three - real_unit * unit_two),
            2.0 * (unit_two * unit_three + real_unit * unit_one),
            1.0 - 2.0 * (unit_one * unit_one + unit_two * unit_two),
        ),
    )


def harmonics(first_dir, second_dir, third_dir):
    sq_first = first_dir * first_dir
    sq_second = second_dir * second_dir
    sq_third = third_dir * third_dir
    return [
        harm_zero,
        -harm_one * second_dir,
        harm_one * third_dir,
        -harm_one * first_dir,
        harm_two[0] * first_dir * second_dir,
        harm_two[1] * second_dir * third_dir,
        harm_two[2] * (2.0 * sq_third - sq_first - sq_second),
        harm_two[3] * first_dir * third_dir,
        harm_two[4] * (sq_first - sq_second),
        harm_three[0] * second_dir * (3.0 * sq_first - sq_second),
        harm_three[1] * first_dir * second_dir * third_dir,
        harm_three[2] * second_dir * (4.0 * sq_third - sq_first - sq_second),
        harm_three[3] * third_dir * (2.0 * sq_third - 3.0 * sq_first - 3.0 * sq_second),
        harm_three[4] * first_dir * (4.0 * sq_third - sq_first - sq_second),
        harm_three[5] * third_dir * (sq_first - sq_second),
        harm_three[6] * first_dir * (sq_first - 3.0 * sq_second),
    ]


def project(raw, camera):
    camera_turn = rotation(camera[0], camera[1], camera[2], camera[3])
    shift_vec = (camera[4], camera[5], camera[6])
    focal_x = camera[7]
    focal_y = camera[8]
    position = (raw[0], raw[1], raw[2])
    viewed = [
        camera_turn[across][0] * position[0]
        + camera_turn[across][1] * position[1]
        + camera_turn[across][2] * position[2]
        + shift_vec[across]
        for across in range(3)
    ]
    inverse = 1.0 / viewed[2]
    mean_x = focal_x * viewed[0] * inverse + camera[9]
    mean_y = focal_y * viewed[1] * inverse + camera[10]
    gauss_turn = rotation(raw[6], raw[7], raw[8], raw[9])
    stretch = [jnp.exp(raw[3 + column]) for column in range(3)]
    jac_xx = focal_x * inverse
    jac_xz = -focal_x * viewed[0] * inverse * inverse
    jac_yy = focal_y * inverse
    jac_yz = -focal_y * viewed[1] * inverse * inverse
    leading_x = [
        jac_xx * camera_turn[0][column] + jac_xz * camera_turn[2][column] for column in range(3)
    ]
    leading_y = [
        jac_yy * camera_turn[1][column] + jac_yz * camera_turn[2][column] for column in range(3)
    ]
    axes_x = [
        (
            leading_x[0] * gauss_turn[0][column]
            + leading_x[1] * gauss_turn[1][column]
            + leading_x[2] * gauss_turn[2][column]
        )
        * stretch[column]
        for column in range(3)
    ]
    axes_y = [
        (
            leading_y[0] * gauss_turn[0][column]
            + leading_y[1] * gauss_turn[1][column]
            + leading_y[2] * gauss_turn[2][column]
        )
        * stretch[column]
        for column in range(3)
    ]
    cov_xx = axes_x[0] * axes_x[0] + axes_x[1] * axes_x[1] + axes_x[2] * axes_x[2] + blur_add
    cov_xy = axes_x[0] * axes_y[0] + axes_x[1] * axes_y[1] + axes_x[2] * axes_y[2]
    cov_yy = axes_y[0] * axes_y[0] + axes_y[1] * axes_y[1] + axes_y[2] * axes_y[2] + blur_add
    determ = cov_xx * cov_yy - cov_xy * cov_xy
    opacity = 1.0 / (1.0 + jnp.exp(-raw[10]))
    camera_eye = [
        -(
            camera_turn[0][column] * shift_vec[0]
            + camera_turn[1][column] * shift_vec[1]
            + camera_turn[2][column] * shift_vec[2]
        )
        for column in range(3)
    ]
    offset = [position[column] - camera_eye[column] for column in range(3)]
    length = lax.rsqrt(offset[0] * offset[0] + offset[1] * offset[1] + offset[2] * offset[2])
    harmonic_terms = harmonics(offset[0] * length, offset[1] * length, offset[2] * length)
    colours = []
    for channel in range(3):
        total = 0.5 + jnp.zeros_like(opacity)
        for harmonic in range(16):
            total = total + raw[11 + 16 * channel + harmonic] * harmonic_terms[harmonic]
        colours.append(total)
    return [mean_x, mean_y, cov_yy / determ, -cov_xy / determ, cov_xx / determ, opacity] + colours


def three_pieces(value):
    high = value.astype(jnp.bfloat16)
    rest = value - high.astype(jnp.float32)
    middle = rest.astype(jnp.bfloat16)
    low = (rest - middle.astype(jnp.float32)).astype(jnp.bfloat16)
    return high, middle, low


def two_pieces(value):
    high = value.astype(jnp.bfloat16)
    return high, (value - high.astype(jnp.float32)).astype(jnp.bfloat16)


def matmul(left, right):
    return jnp.dot(left, right, preferred_element_type=jnp.float32)


def matmul_nt(left, right):
    return lax.dot_general(
        left, right, (((1,), (1,)), ((), ())), preferred_element_type=jnp.float32
    )


def visible_row(visible_ref):
    views = visible_ref.shape[0]
    return jnp.concatenate([visible_ref[view : view + 1, :] for view in range(views)], axis=1)


def column_hot(visible_ref, columns):
    ids = visible_row(visible_ref)
    place = lax.broadcasted_iota(jnp.int32, (columns, ids.shape[1]), 0)
    return jnp.where(place == ids, 1.0, 0.0).astype(jnp.bfloat16)


def camera_rows(cameras_ref, own_rows):
    views = cameras_ref.shape[0]
    lane = lax.broadcasted_iota(jnp.int32, (1, views * own_rows), 1)
    rows = []
    for entry in range(11):
        row = jnp.full(lane.shape, cameras_ref[0, entry], jnp.float32)
        for view in range(1, views):
            row = jnp.where(lane >= view * own_rows, cameras_ref[view, entry], row)
        rows.append(row)
    return rows


def down(row, lanes):
    spread_row = jnp.broadcast_to(row.astype(jnp.float32), (lanes, row.shape[1]))
    return jnp.transpose(spread_row)


def list_hot_down(lists, lanes):
    ids = down(lax.bitwise_and(lists, lanes - 1), lanes)
    lane = lax.broadcasted_iota(jnp.int32, ids.shape, 1).astype(jnp.float32)
    return jnp.where(ids == lane, 1.0, 0.0).astype(jnp.bfloat16)


def list_hot(lists, lanes):
    place = lax.broadcasted_iota(jnp.int32, (lanes, lists.shape[1]), 0)
    hot = jnp.where(place == lax.bitwise_and(lists, lanes - 1), 1.0, 0.0).astype(jnp.bfloat16)
    return hot, lax.shift_right_logical(lists, lanes.bit_length() - 1)


def step_kernel(
    views, tiles, params_hbm, visible_ref, cameras_ref, lists_hbm, counts_ref, targets_ref,
    grad_ref, seen_ref, image_ref,
    params_ref, lists_ref, picked_ref, outgoing, everyone, hot_back, hots, hots_wide, rows, grads,
    weights, weight_parts, ratios, carried, held, given, landed, summed, arrived_ref, slopes_ref,
    load_sem, out_sem, out_recv, spread_sem, spread_recv, view_send, view_recv, tile_send, tile_recv
):
    my_view, my_tile = lax.axis_index("view"), lax.axis_index("tile")
    others_view = [lax.rem(my_view + step, views) for step in range(1, views)]
    others_tile = [lax.rem(my_tile + step, tiles) for step in range(1, tiles)]
    barrier = pltpu.get_barrier_semaphore()
    for other in others_view:
        pl.semaphore_signal(barrier, inc=1, device_id=(other, my_tile), device_id_type=MESH)
    for other in others_tile:
        pl.semaphore_signal(barrier, inc=1, device_id=(my_view, other), device_id_type=MESH)
    load_params = pltpu.make_async_copy(params_hbm, params_ref, load_sem.at[0])
    load_lists = pltpu.make_async_copy(lists_hbm, lists_ref, load_sem.at[1])
    load_params.start()
    load_lists.start()

    width, columns = params_ref.shape
    own_rows = visible_ref.shape[1]
    wide = 2 * own_rows
    hot = column_hot(visible_ref, columns)
    cameras = camera_rows(cameras_ref, own_rows)
    load_params.wait()
    padded = jnp.concatenate(
        [params_ref[...], jnp.zeros((64 - width, columns), jnp.float32)], axis=0
    )
    found = matmul(jnp.concatenate(three_pieces(padded), axis=0), hot)
    picked_ref[...] = found[0:64] + found[64:128] + found[128:192]
    raw = [picked_ref[row : row + 1, :] for row in range(width)]
    out = project(raw, cameras)
    lower = jnp.concatenate(out[0:8], axis=0)
    upper = jnp.concatenate([out[8], jnp.zeros((7, out[8].shape[1]), jnp.float32)], axis=0)
    for view in range(views):
        span = slice(view * own_rows, (view + 1) * own_rows)
        outgoing[view] = jnp.concatenate([lower[:, span], upper[:, span]], axis=1)

    def to_view(source, other, landing, sends, receives):
        return pltpu.make_async_remote_copy(
            src_ref=source, dst_ref=landing, send_sem=sends, recv_sem=receives,
            device_id=(other, my_tile), device_id_type=MESH,
        )

    def spread(source, other, slot):
        return pltpu.make_async_remote_copy(
            src_ref=source, dst_ref=source, send_sem=spread_sem.at[other],
            recv_sem=spread_recv.at[slot], device_id=(my_view, other), device_id_type=MESH,
        )

    everyone[my_tile, my_view] = outgoing[my_view]
    pl.semaphore_wait(barrier, views + tiles - 2)
    for other in others_view:
        to_view(
            outgoing.at[other], other, everyone.at[my_tile, my_view], out_sem.at[0],
            out_recv.at[my_view],
        ).start()
    for other in others_tile:
        spread(everyone.at[my_tile, my_view], other, my_tile).start()

    load_lists.wait()
    per_device, entries = lists_ref.shape
    groups, groups_wide = [], []
    for tile in range(per_device):
        ids = lists_ref[tile : tile + 1, :]
        narrow, group = list_hot(ids, own_rows)
        hots[tile] = jnp.concatenate([narrow] * 4, axis=0)
        groups.append(jnp.broadcast_to(group, (SUBS, entries)))
        hots_wide[tile] = list_hot_down(ids, wide)
        group = lax.shift_right_logical(ids, wide.bit_length() - 1)
        groups_wide.append(jnp.broadcast_to(group, (SUBS, entries)))

    for other in others_view:
        to_view(
            outgoing.at[other], other, everyone.at[my_tile, other], out_sem.at[0],
            out_recv.at[other],
        ).wait_recv()
        for peer in others_tile:
            spread(everyone.at[my_tile, other], peer, my_tile).start()
    ids_down = down(visible_row(visible_ref), BLOCK)
    for start in range(0, columns, BLOCK):
        lane_at = lax.broadcasted_iota(jnp.int32, ids_down.shape, 1).astype(jnp.float32) + start
        hot_back[:, start : start + BLOCK] = jnp.where(ids_down == lane_at, 1.0, 0.0).astype(
            jnp.bfloat16
        )
    for peer in others_tile:
        spread(everyone.at[peer], peer, peer).wait_recv()

    batch = max(1, min(tiles, 32 // views))
    chunk = batch * views
    lane = lax.broadcasted_iota(jnp.int32, (chunk * (SUBS + 1), wide), 1)

    def gather(index, held_rows):
        source = everyone[pl.ds(index * batch, batch)].reshape(chunk, SUBS, wide)
        last = pltpu.roll(source[:, 0, :], own_rows, 1)
        source = jnp.concatenate([source.reshape(chunk * SUBS, wide), last], axis=0)
        high, middle, low = [piece.astype(jnp.float32) for piece in three_pieces(source)]
        source = jnp.concatenate(
            [
                jnp.where(lane < own_rows, high, pltpu.roll(middle, own_rows, 1)),
                jnp.where(lane < own_rows, low, 0.0),
            ],
            axis=1,
        ).astype(jnp.bfloat16)
        new_rows = []
        for tile in range(per_device):
            located = matmul(source, hots[tile])
            first, second = held_rows[tile]
            for owner in range(chunk):
                mine = groups[tile] == index * chunk + owner
                first = first + jnp.where(mine, located[owner * SUBS : (owner + 1) * SUBS], 0.0)
            for start in range(0, chunk, SUBS):
                begin = chunk * SUBS + start
                number = lax.broadcasted_iota(jnp.int32, (SUBS, entries), 0) + (
                    index * chunk + start
                )
                second = second + jnp.where(
                    groups[tile] == number, located[begin : begin + SUBS], 0.0
                )
            new_rows.append((first, second))
        return tuple(new_rows)

    empty = jnp.zeros((SUBS, entries), jnp.float32)
    collected = lax.fori_loop(0, tiles // batch, gather, ((empty, empty),) * per_device)
    for tile in range(per_device):
        rows[tile, 0:SUBS, :] = collected[tile][0]
        rows[tile, SUBS : 2 * SUBS, :] = jnp.broadcast_to(
            jnp.sum(collected[tile][1], axis=0, keepdims=True), (SUBS, entries)
        )

    first_tile = my_tile * per_device
    half = SIDE // 2
    middles = []
    for tile in range(per_device):
        number = first_tile + tile
        middles.append(
            (
                (lax.rem(number, WIN_COLS) * SIDE + half).astype(jnp.float32),
                (lax.div(number, WIN_COLS) * SIDE + half).astype(jnp.float32),
            )
        )
    side_x = lax.broadcasted_iota(jnp.int32, (SIDE, BLOCK), 0).astype(jnp.float32) + (0.5 - half)
    spot = lax.bitwise_and(
        lax.broadcasted_iota(jnp.int32, (2 * BLOCK, 2 * BLOCK), 0), BLOCK - 1
    )
    lane_two = lax.broadcasted_iota(jnp.int32, (2 * BLOCK, 2 * BLOCK), 1)
    ahead = jnp.where((spot < lane_two) | (lane_two >= BLOCK), 1.0, 0.0).astype(jnp.bfloat16)
    behind = jnp.where((spot > lane_two) | (lane_two >= BLOCK), 1.0, 0.0).astype(jnp.bfloat16)
    blocks = entries // BLOCK

    carried[...] = jnp.zeros_like(carried)
    held[...] = jnp.zeros_like(held)

    def forward(block, _):
        start = pl.multiple_of(block * BLOCK, BLOCK)
        for tile in range(per_device):
            live = (block < counts_ref[0, tile]).astype(jnp.float32)
            low = rows[tile, 0:SUBS, pl.ds(start, BLOCK)]
            up = rows[tile, SUBS : 2 * SUBS, pl.ds(start, BLOCK)]
            mean_x = low[0:1] - middles[tile][0]
            mean_y = low[1:2] - middles[tile][1]
            form_a = -0.5 * low[2:3]
            form_b = -low[3:4]
            form_c = -0.5 * low[4:5]
            opacity = low[5:6] * live
            delta_x = side_x - mean_x
            square = form_a * delta_x * delta_x
            cross = form_b * delta_x
            pieces = []
            for line in range(SIDE):
                delta_y = (line + 0.5 - half) - mean_y
                pieces.append((cross + form_c * delta_y) * delta_y + square)
            alpha = opacity * jnp.exp(jnp.concatenate(pieces, axis=0))
            decay = jnp.log(1.0 - alpha)
            before = matmul(jnp.concatenate(two_pieces(decay), axis=1), ahead)
            past = carried[tile]
            weight = alpha * jnp.exp(before[:, 0:BLOCK] + past)
            carried[tile] = past + before[:, BLOCK:]
            ratios[tile, block] = alpha * jnp.exp(-decay)
            weights[tile, block] = weight
            parts = jnp.concatenate(two_pieces(weight), axis=1)
            weight_parts[tile, block] = parts
            colour = jnp.concatenate([low[6:8], up[0:1], jnp.zeros((5, BLOCK), jnp.float32)], axis=0)
            high = colour.astype(jnp.bfloat16).astype(jnp.float32)
            both = jnp.concatenate([high, colour - high], axis=0).astype(jnp.bfloat16)
            held[tile] += matmul_nt(parts, jnp.concatenate([both, both], axis=1))
        return 0

    lax.fori_loop(0, blocks, forward, 0)

    slopes, slopes_wide = [], []
    for tile in range(per_device):
        drawn = jnp.transpose(
            jnp.concatenate(
                [held[tile], jnp.zeros((PIX, BLOCK - 2 * SUBS), jnp.float32)], axis=1
            )
        )
        image_ref[0:3, 0, tile * PIX : (tile + 1) * PIX] = drawn[0:3]
        image_ref[3:6, 0, tile * PIX : (tile + 1) * PIX] = drawn[SUBS : SUBS + 3]
        drawn = drawn[0:3] + drawn[SUBS : SUBS + 3]
        slope = 2.0 * (drawn - targets_ref[:, 0, tile * PIX : (tile + 1) * PIX])
        high = slope.astype(jnp.bfloat16).astype(jnp.float32)
        stack = jnp.concatenate(
            [high, slope - high, high, jnp.zeros((BLOCK - 9, PIX), jnp.float32)], axis=0
        )
        slopes.append(stack[0 : 2 * SUBS].astype(jnp.bfloat16))
        slopes_wide.append(jnp.transpose(stack).astype(jnp.bfloat16)[:, 0 : 2 * SUBS])

    pixel = lax.broadcasted_iota(jnp.int32, (2 * SUBS, PIX), 1)
    kind = lax.broadcasted_iota(jnp.int32, (2 * SUBS, PIX), 0)
    at_x = lax.bitwise_and(pixel, SIDE - 1).astype(jnp.float32) + (0.5 - half)
    at_y = lax.shift_right_logical(pixel, SIDE.bit_length() - 1).astype(jnp.float32) + (0.5 - half)
    power_x = jnp.where((kind == 1) | (kind == 4), at_x, jnp.where(kind == 3, at_x * at_x, 1.0))
    power_y = jnp.where((kind == 2) | (kind == 4), at_y, jnp.where(kind == 5, at_y * at_y, 1.0))
    basis = jnp.where(kind < 6, power_x * power_y, 0.0).astype(jnp.bfloat16)

    carried[...] = jnp.zeros_like(carried)

    def backward(index, _):
        block = blocks - 1 - index
        start = pl.multiple_of(block * BLOCK, BLOCK)
        for tile in range(per_device):
            low = rows[tile, 0:SUBS, pl.ds(start, BLOCK)]
            up = rows[tile, SUBS : 2 * SUBS, pl.ds(start, BLOCK)]
            colour = jnp.concatenate([low[6:8], up[0:1]], axis=0)
            high = colour.astype(jnp.bfloat16).astype(jnp.float32)
            both = jnp.concatenate(
                [high, high, colour - high, jnp.zeros((7, BLOCK), jnp.float32)], axis=0
            ).astype(jnp.bfloat16)
            pulled = matmul(slopes_wide[tile], both) * weights[tile, block]
            after = matmul(jnp.concatenate(two_pieces(pulled), axis=1), behind)
            past = carried[tile]
            inner = pulled - (after[:, 0:BLOCK] + past) * ratios[tile, block]
            carried[tile] = past + after[:, BLOCK:]
            inner_high, inner_low = two_pieces(inner)
            sums = matmul(basis, inner_high) + matmul(basis, inner_low)
            parts = weight_parts[tile, block]
            tint = matmul(slopes[tile], parts[:, 0:BLOCK])
            tint_low = matmul(slopes[tile], parts[:, BLOCK:])
            tint = tint[0:3] + tint[3:6] + tint_low[0:3]
            mean_x = low[0:1] - middles[tile][0]
            mean_y = low[1:2] - middles[tile][1]
            form_a, form_b, form_c = low[2:3], low[3:4], low[4:5]
            whole, by_x, by_y = sums[0:1], sums[1:2], sums[2:3]
            sum_x = by_x - mean_x * whole
            sum_y = by_y - mean_y * whole
            sum_xx = sums[3:4] - 2.0 * mean_x * by_x + mean_x * mean_x * whole
            sum_xy = sums[4:5] - mean_x * by_y - mean_y * by_x + mean_x * mean_y * whole
            sum_yy = sums[5:6] - 2.0 * mean_y * by_y + mean_y * mean_y * whole
            grads[tile, 0:SUBS, pl.ds(start, BLOCK)] = jnp.concatenate(
                [
                    form_a * sum_x + form_b * sum_y,
                    form_b * sum_x + form_c * sum_y,
                    -0.5 * sum_xx,
                    -sum_xy,
                    -0.5 * sum_yy,
                    whole / low[5:6],
                    tint[0:2],
                ],
                axis=0,
            )
            grads[tile, SUBS : 2 * SUBS, pl.ds(start, BLOCK)] = jnp.broadcast_to(
                tint[2:3], (SUBS, BLOCK)
            )
        return 0

    lax.fori_loop(0, blocks, backward, 0)

    pairs = chunk // 2
    lane_pair = lax.broadcasted_iota(jnp.int32, (pairs, SUBS, wide), 2)

    def scatter(index, _):
        total = jnp.zeros((2 * pairs * (SUBS + 1), wide), jnp.float32)
        for tile in range(per_device):
            main = grads[tile, 0:SUBS, :]
            last = grads[tile, SUBS : 2 * SUBS, :]
            parts = [[], [], [], []]
            main_high = main.astype(jnp.bfloat16).astype(jnp.float32)
            last_high = last.astype(jnp.bfloat16).astype(jnp.float32)
            for pair in range(pairs):
                mine = groups_wide[tile] == index * pairs + pair
                parts[0].append(jnp.where(mine, main_high, 0.0))
                parts[1].append(jnp.where(mine, main - main_high, 0.0))
            for start in range(0, pairs, SUBS):
                number = lax.broadcasted_iota(jnp.int32, (SUBS, entries), 0) + (
                    index * pairs + start
                )
                mine = groups_wide[tile] == number
                parts[2].append(jnp.where(mine, last_high, 0.0))
                parts[3].append(jnp.where(mine, last - last_high, 0.0))
            left = jnp.concatenate(parts[0] + parts[1] + parts[2] + parts[3], axis=0)
            total = total + matmul(left.astype(jnp.bfloat16), hots_wide[tile])
        size = pairs * SUBS
        main = (total[0:size] + total[size : 2 * size]).reshape(pairs, SUBS, wide)
        last = total[2 * size : 2 * size + pairs] + total[2 * size + pairs :]
        turned = pltpu.roll(last, own_rows, 1)
        even = jnp.where(
            lane_pair < own_rows, main, jnp.broadcast_to(turned[:, None, :], main.shape)
        )
        odd = jnp.where(
            lane_pair < own_rows,
            pltpu.roll(main, own_rows, 2),
            jnp.broadcast_to(last[:, None, :], main.shape),
        )
        for pair in range(pairs):
            place = index * batch + 2 * pair // views
            given[place, 2 * pair % views] = even[pair]
            given[place, 2 * pair % views + 1] = odd[pair]
        return 0

    lax.fori_loop(0, tiles // batch, scatter, 0)

    def to_tile(source, other, slot, view):
        return pltpu.make_async_remote_copy(
            src_ref=source, dst_ref=landed.at[view, slot], send_sem=tile_send.at[other],
            recv_sem=tile_recv.at[view], device_id=(my_view, other), device_id_type=MESH,
        )

    for view in others_view + [my_view]:
        for step, other in enumerate(others_tile):
            to_tile(given.at[other, view], other, tiles - 2 - step, view).start()
    _, pullback = jax.vjp(lambda source: project(source, cameras), raw)
    for view in others_view + [my_view]:
        pltpu.make_async_remote_copy(
            src_ref=landed.at[view], dst_ref=landed.at[view], send_sem=tile_send.at[0],
            recv_sem=tile_recv.at[view], device_id=(my_view, others_tile[0]), device_id_type=MESH,
        ).wait_recv()
        total = given[my_tile, view]
        for slot in range(tiles - 1):
            total = total + landed[view, slot]
        summed[view] = total
        if view is not my_view:
            to_view(
                summed.at[view], view, arrived_ref.at[my_view], view_send.at[0],
                view_recv.at[my_view],
            ).start()
    arrived_ref[my_view] = summed[my_view]
    for other in others_view:
        to_view(
            summed.at[other], other, arrived_ref.at[other], view_send.at[0], view_recv.at[other]
        ).wait_recv()
    lower = jnp.concatenate([arrived_ref[view][:, 0:own_rows] for view in range(views)], axis=1)
    upper = jnp.concatenate([arrived_ref[view][:, own_rows:] for view in range(views)], axis=1)
    (returned,) = pullback([lower[row : row + 1] for row in range(8)] + [upper[0:1]])
    slopes_ref[...] = jnp.ones_like(slopes_ref)
    for row in range(width):
        slopes_ref[row : row + 1, :] = returned[row]
    found = matmul(jnp.concatenate(three_pieces(slopes_ref[...]), axis=0), hot_back[...])
    found = found[0:64] + found[64:128] + found[128:192]
    grad_ref[...] = found[0:width]
    seen_ref[...] = found[width : width + 1]

    rest = pl.ds(0, views - 1)
    to_view(
        outgoing.at[rest], others_view[0], everyone.at[my_tile, rest], out_sem.at[0],
        out_recv.at[my_view],
    ).wait_send()
    to_view(
        summed.at[rest], others_view[0], arrived_ref.at[rest], view_send.at[0],
        view_recv.at[my_view],
    ).wait_send()
    for other in others_tile:
        spread(everyone.at[my_tile], other, my_tile).wait_send()
        pltpu.make_async_remote_copy(
            src_ref=given.at[other], dst_ref=given.at[other], send_sem=tile_send.at[other],
            recv_sem=tile_recv.at[my_view], device_id=(my_view, other), device_id_type=MESH,
        ).wait_send()


def shards(views, tiles, params, first, second, visible, cameras, tile_lists, tile_blocks, targets):
    own_rows = visible.shape[1]
    per_device, entries = tile_lists.shape[1:]
    blocks = entries // BLOCK
    packet = (SUBS, 2 * own_rows)
    f32 = jnp.float32
    dma = pltpu.SemaphoreType.DMA
    grad, seen, drawn = pl.pallas_call(
        functools.partial(step_kernel, views, tiles),
        out_shape=[
            jax.ShapeDtypeStruct(params.shape, f32),
            jax.ShapeDtypeStruct((1, params.shape[1]), f32),
            jax.ShapeDtypeStruct((6, 1, per_device * PIX), f32),
        ],
        in_specs=[ANY, VMEM, SMEM, ANY, SMEM, VMEM],
        out_specs=[VMEM, VMEM, VMEM],
        scratch_shapes=[
            pltpu.VMEM(params.shape, f32),
            pltpu.VMEM((per_device, entries), jnp.int32),
            pltpu.VMEM((64, views * own_rows), f32),
            pltpu.VMEM((views,) + packet, f32),
            pltpu.VMEM((tiles, views) + packet, f32),
            pltpu.VMEM((views * own_rows, params.shape[1]), jnp.bfloat16),
            pltpu.VMEM((per_device, 4 * own_rows, entries), jnp.bfloat16),
            pltpu.VMEM((per_device, entries, 2 * own_rows), jnp.bfloat16),
            pltpu.VMEM((per_device, 2 * SUBS, entries), f32),
            pltpu.VMEM((per_device, 2 * SUBS, entries), f32),
            pltpu.VMEM((per_device, blocks, PIX, BLOCK), f32),
            pltpu.VMEM((per_device, blocks, PIX, 2 * BLOCK), jnp.bfloat16),
            pltpu.VMEM((per_device, blocks, PIX, BLOCK), f32),
            pltpu.VMEM((per_device, PIX, BLOCK), f32),
            pltpu.VMEM((per_device, PIX, 2 * SUBS), f32),
            pltpu.VMEM((tiles, views) + packet, f32),
            pltpu.VMEM((views, tiles - 1) + packet, f32),
            pltpu.VMEM((views,) + packet, f32),
            pltpu.VMEM((views,) + packet, f32),
            pltpu.VMEM((64, views * own_rows), f32),
            dma((2,)),
            dma((1,)), dma((views,)), dma((tiles,)), dma((tiles,)),
            dma((1,)), dma((views,)), dma((tiles,)), dma((views,)),
        ],
        compiler_params=pltpu.CompilerParams(
            collective_id=0, has_side_effects=True, vmem_limit_bytes=LIMIT
        ),
        name="render_step",
    )(params, visible, cameras, tile_lists[0], tile_blocks, jnp.transpose(targets, (1, 0, 2)))
    seen = seen > 0.5
    moved_first = beta_first * first + (1.0 - beta_first) * grad
    moved_second = beta_second * second + (1.0 - beta_second) * grad * grad
    moved_params = params - learn_rate * moved_first / (jnp.sqrt(moved_second) + adam_eps)
    new_first = jnp.where(seen, moved_first, first)
    new_second = jnp.where(seen, moved_second, second)
    new_params = jnp.where(seen, moved_params, params)
    return (new_params, new_first, new_second, jnp.transpose(drawn[0:3] + drawn[3:6], (1, 0, 2)))


def solution(mesh):
    in_specs = (
        P(None, ("view", "tile")),
        P(None, ("view", "tile")),
        P(None, ("view", "tile")),
        P(None, ("view", "tile")),
        P(),
        P("view", "tile", None),
        P("view", "tile"),
        P("view", None, "tile"),
    )
    out_specs = (
        P(None, ("view", "tile")),
        P(None, ("view", "tile")),
        P(None, ("view", "tile")),
        P("view", None, "tile"),
    )
    body = functools.partial(shards, mesh.shape["view"], mesh.shape["tile"])
    return jax.shard_map(body, mesh=mesh, in_specs=in_specs, out_specs=out_specs, check_vma=False)
```

```python
import functools

import jax
import jax.numpy as jnp
from jax import lax
from jax.experimental import pallas as pl
from jax.experimental.pallas import tpu as pltpu
from jax.sharding import PartitionSpec as P

SIDE = 16
PIX = 256
BLOCK = 128
WIN_COLS = 8
SUBS = 8
MESH = pl.DeviceIdType.MESH
VMEM = pl.BlockSpec(memory_space=pltpu.VMEM)
ANY = pl.BlockSpec(memory_space=pl.ANY)
SMEM = pl.BlockSpec(memory_space=pltpu.SMEM)
LIMIT = 62 * 1024 * 1024


harm_zero = 0.28209479177387814
harm_one = 0.4886025119029199
harm_two = (
    1.0925484305920792,
    -1.0925484305920792,
    0.31539156525252005,
    -1.0925484305920792,
    0.5462742152960396,
)
harm_three = (
    -0.5900435899266435,
    2.890611442640554,
    -0.4570457994644658,
    0.3731763325901154,
    -0.4570457994644658,
    1.445305721320277,
    -0.5900435899266435,
)
learn_rate = 0.05
beta_first = 0.9
beta_second = 0.999
adam_eps = 1e-08
blur_add = 0.3


def rotation(real_part, axis_one, axis_two, axis_three):
    inverse = lax.rsqrt(
        real_part * real_part + axis_one * axis_one + axis_two * axis_two + axis_three * axis_three
    )
    real_unit = real_part * inverse
    unit_one = axis_one * inverse
    unit_two = axis_two * inverse
    unit_three = axis_three * inverse
    return (
        (
            1.0 - 2.0 * (unit_two * unit_two + unit_three * unit_three),
            2.0 * (unit_one * unit_two - real_unit * unit_three),
            2.0 * (unit_one * unit_three + real_unit * unit_two),
        ),
        (
            2.0 * (unit_one * unit_two + real_unit * unit_three),
            1.0 - 2.0 * (unit_one * unit_one + unit_three * unit_three),
            2.0 * (unit_two * unit_three - real_unit * unit_one),
        ),
        (
            2.0 * (unit_one * unit_three - real_unit * unit_two),
            2.0 * (unit_two * unit_three + real_unit * unit_one),
            1.0 - 2.0 * (unit_one * unit_one + unit_two * unit_two),
        ),
    )


def harmonics(first_dir, second_dir, third_dir):
    sq_first = first_dir * first_dir
    sq_second = second_dir * second_dir
    sq_third = third_dir * third_dir
    return [
        harm_zero,
        -harm_one * second_dir,
        harm_one * third_dir,
        -harm_one * first_dir,
        harm_two[0] * first_dir * second_dir,
        harm_two[1] * second_dir * third_dir,
        harm_two[2] * (2.0 * sq_third - sq_first - sq_second),
        harm_two[3] * first_dir * third_dir,
        harm_two[4] * (sq_first - sq_second),
        harm_three[0] * second_dir * (3.0 * sq_first - sq_second),
        harm_three[1] * first_dir * second_dir * third_dir,
        harm_three[2] * second_dir * (4.0 * sq_third - sq_first - sq_second),
        harm_three[3] * third_dir * (2.0 * sq_third - 3.0 * sq_first - 3.0 * sq_second),
        harm_three[4] * first_dir * (4.0 * sq_third - sq_first - sq_second),
        harm_three[5] * third_dir * (sq_first - sq_second),
        harm_three[6] * first_dir * (sq_first - 3.0 * sq_second),
    ]


def project(raw, camera):
    camera_turn = rotation(camera[0], camera[1], camera[2], camera[3])
    shift_vec = (camera[4], camera[5], camera[6])
    focal_x = camera[7]
    focal_y = camera[8]
    position = (raw[0], raw[1], raw[2])
    viewed = [
        camera_turn[across][0] * position[0]
        + camera_turn[across][1] * position[1]
        + camera_turn[across][2] * position[2]
        + shift_vec[across]
        for across in range(3)
    ]
    inverse = 1.0 / viewed[2]
    mean_x = focal_x * viewed[0] * inverse + camera[9]
    mean_y = focal_y * viewed[1] * inverse + camera[10]
    gauss_turn = rotation(raw[6], raw[7], raw[8], raw[9])
    stretch = [jnp.exp(raw[3 + column]) for column in range(3)]
    jac_xx = focal_x * inverse
    jac_xz = -focal_x * viewed[0] * inverse * inverse
    jac_yy = focal_y * inverse
    jac_yz = -focal_y * viewed[1] * inverse * inverse
    leading_x = [
        jac_xx * camera_turn[0][column] + jac_xz * camera_turn[2][column] for column in range(3)
    ]
    leading_y = [
        jac_yy * camera_turn[1][column] + jac_yz * camera_turn[2][column] for column in range(3)
    ]
    axes_x = [
        (
            leading_x[0] * gauss_turn[0][column]
            + leading_x[1] * gauss_turn[1][column]
            + leading_x[2] * gauss_turn[2][column]
        )
        * stretch[column]
        for column in range(3)
    ]
    axes_y = [
        (
            leading_y[0] * gauss_turn[0][column]
            + leading_y[1] * gauss_turn[1][column]
            + leading_y[2] * gauss_turn[2][column]
        )
        * stretch[column]
        for column in range(3)
    ]
    cov_xx = axes_x[0] * axes_x[0] + axes_x[1] * axes_x[1] + axes_x[2] * axes_x[2] + blur_add
    cov_xy = axes_x[0] * axes_y[0] + axes_x[1] * axes_y[1] + axes_x[2] * axes_y[2]
    cov_yy = axes_y[0] * axes_y[0] + axes_y[1] * axes_y[1] + axes_y[2] * axes_y[2] + blur_add
    determ = cov_xx * cov_yy - cov_xy * cov_xy
    opacity = 1.0 / (1.0 + jnp.exp(-raw[10]))
    camera_eye = [
        -(
            camera_turn[0][column] * shift_vec[0]
            + camera_turn[1][column] * shift_vec[1]
            + camera_turn[2][column] * shift_vec[2]
        )
        for column in range(3)
    ]
    offset = [position[column] - camera_eye[column] for column in range(3)]
    length = lax.rsqrt(offset[0] * offset[0] + offset[1] * offset[1] + offset[2] * offset[2])
    harmonic_terms = harmonics(offset[0] * length, offset[1] * length, offset[2] * length)
    colours = []
    for channel in range(3):
        total = 0.5 + jnp.zeros_like(opacity)
        for harmonic in range(16):
            total = total + raw[11 + 16 * channel + harmonic] * harmonic_terms[harmonic]
        colours.append(total)
    return [mean_x, mean_y, cov_yy / determ, -cov_xy / determ, cov_xx / determ, opacity] + colours


def three_pieces(value):
    high = value.astype(jnp.bfloat16)
    rest = value - high.astype(jnp.float32)
    middle = rest.astype(jnp.bfloat16)
    low = (rest - middle.astype(jnp.float32)).astype(jnp.bfloat16)
    return high, middle, low


def two_pieces(value):
    high = value.astype(jnp.bfloat16)
    return high, (value - high.astype(jnp.float32)).astype(jnp.bfloat16)


def matmul(left, right):
    return jnp.dot(left, right, preferred_element_type=jnp.float32)


def matmul_nt(left, right):
    return lax.dot_general(
        left, right, (((1,), (1,)), ((), ())), preferred_element_type=jnp.float32
    )


def visible_row(visible_ref):
    views = visible_ref.shape[0]
    return jnp.concatenate([visible_ref[view : view + 1, :] for view in range(views)], axis=1)


def column_hot(visible_ref, columns):
    ids = visible_row(visible_ref)
    place = lax.broadcasted_iota(jnp.int32, (columns, ids.shape[1]), 0)
    return jnp.where(place == ids, 1.0, 0.0).astype(jnp.bfloat16)


def camera_rows(cameras_ref, own_rows):
    views = cameras_ref.shape[0]
    lane = lax.broadcasted_iota(jnp.int32, (1, views * own_rows), 1)
    rows = []
    for entry in range(11):
        row = jnp.full(lane.shape, cameras_ref[0, entry], jnp.float32)
        for view in range(1, views):
            row = jnp.where(lane >= view * own_rows, cameras_ref[view, entry], row)
        rows.append(row)
    return rows


def down(row, lanes):
    spread_row = jnp.broadcast_to(row.astype(jnp.float32), (lanes, row.shape[1]))
    return jnp.transpose(spread_row)


def list_hot_down(lists, lanes):
    ids = down(lax.bitwise_and(lists, lanes - 1), lanes)
    lane = lax.broadcasted_iota(jnp.int32, ids.shape, 1).astype(jnp.float32)
    return jnp.where(ids == lane, 1.0, 0.0).astype(jnp.bfloat16)


def list_hot(lists, lanes):
    place = lax.broadcasted_iota(jnp.int32, (lanes, lists.shape[1]), 0)
    hot = jnp.where(place == lax.bitwise_and(lists, lanes - 1), 1.0, 0.0).astype(jnp.bfloat16)
    return hot, lax.shift_right_logical(lists, lanes.bit_length() - 1)


def step_kernel(
    views, tiles, params_hbm, visible_ref, cameras_ref, lists_hbm, counts_ref, targets_ref,
    grad_ref, seen_ref, image_ref,
    params_ref, lists_ref, picked_ref, outgoing, everyone, hot_back, hots, hots_wide, rows, grads,
    weights, weight_parts, ratios, carried, held, given, landed, slopes_ref,
    load_sem, out_sem, out_recv, back_sem, back_recv
):
    my_view, my_tile = lax.axis_index("view"), lax.axis_index("tile")
    owners = views * tiles
    me = my_tile * views + my_view

    def owner_at(step):
        other = lax.rem(me + step, owners)
        return other, lax.rem(other, views), lax.div(other, views)

    load_params = pltpu.make_async_copy(params_hbm, params_ref, load_sem.at[0])
    load_lists = pltpu.make_async_copy(lists_hbm, lists_ref, load_sem.at[1])
    load_params.start()
    load_lists.start()
    barrier = pltpu.get_barrier_semaphore()

    def greet(step, _):
        _, view, tile = owner_at(step)
        pl.semaphore_signal(barrier, inc=1, device_id=(view, tile), device_id_type=MESH)
        return 0

    lax.fori_loop(1, owners, greet, 0)

    width, columns = params_ref.shape
    own_rows = visible_ref.shape[1]
    wide = 2 * own_rows
    hot = column_hot(visible_ref, columns)
    cameras = camera_rows(cameras_ref, own_rows)
    load_params.wait()
    padded = jnp.concatenate(
        [params_ref[...], jnp.zeros((64 - width, columns), jnp.float32)], axis=0
    )
    found = matmul(jnp.concatenate(three_pieces(padded), axis=0), hot)
    picked_ref[...] = found[0:64] + found[64:128] + found[128:192]
    raw = [picked_ref[row : row + 1, :] for row in range(width)]
    out = project(raw, cameras)
    lower = jnp.concatenate(out[0:8], axis=0)
    upper = jnp.concatenate([out[8], jnp.zeros((7, out[8].shape[1]), jnp.float32)], axis=0)
    for view in range(views):
        span = slice(view * own_rows, (view + 1) * own_rows)
        outgoing[view] = jnp.concatenate([lower[:, span], upper[:, span]], axis=1)

    def to_owner(source, landing, sends, receives, view, tile):
        return pltpu.make_async_remote_copy(
            src_ref=source, dst_ref=landing, send_sem=sends.at[0], recv_sem=receives.at[0],
            device_id=(view, tile), device_id_type=MESH,
        )

    def send_rows(step, _):
        _, view, tile = owner_at(step)
        to_owner(outgoing.at[view], everyone.at[me], out_sem, out_recv, view, tile).start()
        return 0

    everyone[me] = outgoing[my_view]
    pl.semaphore_wait(barrier, owners - 1)
    lax.fori_loop(1, owners, send_rows, 0)

    load_lists.wait()
    per_device, entries = lists_ref.shape
    groups, groups_wide = [], []
    for tile in range(per_device):
        ids = lists_ref[tile : tile + 1, :]
        narrow, group = list_hot(ids, own_rows)
        hots[tile] = jnp.concatenate([narrow] * 4, axis=0)
        groups.append(jnp.broadcast_to(group, (SUBS, entries)))
        hots_wide[tile] = list_hot_down(ids, wide)
        group = lax.shift_right_logical(ids, wide.bit_length() - 1)
        groups_wide.append(jnp.broadcast_to(group, (SUBS, entries)))

    ids_down = down(visible_row(visible_ref), BLOCK)
    for start in range(0, columns, BLOCK):
        lane_at = lax.broadcasted_iota(jnp.int32, ids_down.shape, 1).astype(jnp.float32) + start
        hot_back[:, start : start + BLOCK] = jnp.where(ids_down == lane_at, 1.0, 0.0).astype(
            jnp.bfloat16
        )
    rest = pl.ds(0, owners - 1)
    _, next_view, next_tile = owner_at(1)
    all_rows = to_owner(
        everyone.at[rest], everyone.at[rest], out_sem, out_recv, next_view, next_tile
    )
    all_rows.wait_recv()

    batch = max(1, min(tiles, 32 // views))
    chunk = batch * views
    lane = lax.broadcasted_iota(jnp.int32, (chunk * (SUBS + 1), wide), 1)

    def gather(index, held_rows):
        source = everyone[pl.ds(index * chunk, chunk)]
        last = pltpu.roll(source[:, 0, :], own_rows, 1)
        source = jnp.concatenate([source.reshape(chunk * SUBS, wide), last], axis=0)
        high, middle, low = [piece.astype(jnp.float32) for piece in three_pieces(source)]
        source = jnp.concatenate(
            [
                jnp.where(lane < own_rows, high, pltpu.roll(middle, own_rows, 1)),
                jnp.where(lane < own_rows, low, 0.0),
            ],
            axis=1,
        ).astype(jnp.bfloat16)
        new_rows = []
        for tile in range(per_device):
            located = matmul(source, hots[tile])
            first, second = held_rows[tile]
            for owner in range(chunk):
                mine = groups[tile] == index * chunk + owner
                first = first + jnp.where(mine, located[owner * SUBS : (owner + 1) * SUBS], 0.0)
            for start in range(0, chunk, SUBS):
                begin = chunk * SUBS + start
                number = lax.broadcasted_iota(jnp.int32, (SUBS, entries), 0) + (
                    index * chunk + start
                )
                second = second + jnp.where(
                    groups[tile] == number, located[begin : begin + SUBS], 0.0
                )
            new_rows.append((first, second))
        return tuple(new_rows)

    empty = jnp.zeros((SUBS, entries), jnp.float32)
    collected = lax.fori_loop(0, tiles // batch, gather, ((empty, empty),) * per_device)
    for tile in range(per_device):
        rows[tile, 0:SUBS, :] = collected[tile][0]
        rows[tile, SUBS : 2 * SUBS, :] = jnp.broadcast_to(
            jnp.sum(collected[tile][1], axis=0, keepdims=True), (SUBS, entries)
        )

    first_tile = my_tile * per_device
    half = SIDE // 2
    middles = []
    for tile in range(per_device):
        number = first_tile + tile
        middles.append(
            (
                (lax.rem(number, WIN_COLS) * SIDE + half).astype(jnp.float32),
                (lax.div(number, WIN_COLS) * SIDE + half).astype(jnp.float32),
            )
        )
    side_x = lax.broadcasted_iota(jnp.int32, (SIDE, BLOCK), 0).astype(jnp.float32) + (0.5 - half)
    spot = lax.bitwise_and(
        lax.broadcasted_iota(jnp.int32, (2 * BLOCK, 2 * BLOCK), 0), BLOCK - 1
    )
    lane_two = lax.broadcasted_iota(jnp.int32, (2 * BLOCK, 2 * BLOCK), 1)
    ahead = jnp.where((spot < lane_two) | (lane_two >= BLOCK), 1.0, 0.0).astype(jnp.bfloat16)
    behind = jnp.where((spot > lane_two) | (lane_two >= BLOCK), 1.0, 0.0).astype(jnp.bfloat16)
    blocks = entries // BLOCK

    carried[...] = jnp.zeros_like(carried)
    held[...] = jnp.zeros_like(held)

    def forward(block, _):
        start = pl.multiple_of(block * BLOCK, BLOCK)
        for tile in range(per_device):
            live = (block < counts_ref[0, tile]).astype(jnp.float32)
            low = rows[tile, 0:SUBS, pl.ds(start, BLOCK)]
            up = rows[tile, SUBS : 2 * SUBS, pl.ds(start, BLOCK)]
            mean_x = low[0:1] - middles[tile][0]
            mean_y = low[1:2] - middles[tile][1]
            form_a = -0.5 * low[2:3]
            form_b = -low[3:4]
            form_c = -0.5 * low[4:5]
            opacity = low[5:6] * live
            delta_x = side_x - mean_x
            square = form_a * delta_x * delta_x
            cross = form_b * delta_x
            pieces = []
            for line in range(SIDE):
                delta_y = (line + 0.5 - half) - mean_y
                pieces.append((cross + form_c * delta_y) * delta_y + square)
            alpha = opacity * jnp.exp(jnp.concatenate(pieces, axis=0))
            decay = jnp.log(1.0 - alpha)
            before = matmul(jnp.concatenate(two_pieces(decay), axis=1), ahead)
            past = carried[tile]
            weight = alpha * jnp.exp(before[:, 0:BLOCK] + past)
            carried[tile] = past + before[:, BLOCK:]
            ratios[tile, block] = alpha * jnp.exp(-decay)
            weights[tile, block] = weight
            parts = jnp.concatenate(two_pieces(weight), axis=1)
            weight_parts[tile, block] = parts
            colour = jnp.concatenate([low[6:8], up[0:1], jnp.zeros((5, BLOCK), jnp.float32)], axis=0)
            high = colour.astype(jnp.bfloat16).astype(jnp.float32)
            both = jnp.concatenate([high, colour - high], axis=0).astype(jnp.bfloat16)
            held[tile] += matmul_nt(parts, jnp.concatenate([both, both], axis=1))
        return 0

    lax.fori_loop(0, blocks, forward, 0)

    slopes, slopes_wide = [], []
    for tile in range(per_device):
        drawn = jnp.transpose(
            jnp.concatenate(
                [held[tile], jnp.zeros((PIX, BLOCK - 2 * SUBS), jnp.float32)], axis=1
            )
        )
        drawn = drawn[0:3] + drawn[SUBS : SUBS + 3]
        image_ref[:, 0, tile * PIX : (tile + 1) * PIX] = drawn
        slope = 2.0 * (drawn - targets_ref[:, 0, tile * PIX : (tile + 1) * PIX])
        high = slope.astype(jnp.bfloat16).astype(jnp.float32)
        stack = jnp.concatenate(
            [high, slope - high, high, jnp.zeros((BLOCK - 9, PIX), jnp.float32)], axis=0
        )
        slopes.append(stack[0 : 2 * SUBS].astype(jnp.bfloat16))
        slopes_wide.append(jnp.transpose(stack).astype(jnp.bfloat16)[:, 0 : 2 * SUBS])

    pixel = lax.broadcasted_iota(jnp.int32, (2 * SUBS, PIX), 1)
    kind = lax.broadcasted_iota(jnp.int32, (2 * SUBS, PIX), 0)
    at_x = lax.bitwise_and(pixel, SIDE - 1).astype(jnp.float32) + (0.5 - half)
    at_y = lax.shift_right_logical(pixel, SIDE.bit_length() - 1).astype(jnp.float32) + (0.5 - half)
    power_x = jnp.where((kind == 1) | (kind == 4), at_x, jnp.where(kind == 3, at_x * at_x, 1.0))
    power_y = jnp.where((kind == 2) | (kind == 4), at_y, jnp.where(kind == 5, at_y * at_y, 1.0))
    basis = jnp.where(kind < 6, power_x * power_y, 0.0).astype(jnp.bfloat16)

    carried[...] = jnp.zeros_like(carried)

    def backward(index, _):
        block = blocks - 1 - index
        start = pl.multiple_of(block * BLOCK, BLOCK)
        for tile in range(per_device):
            low = rows[tile, 0:SUBS, pl.ds(start, BLOCK)]
            up = rows[tile, SUBS : 2 * SUBS, pl.ds(start, BLOCK)]
            colour = jnp.concatenate([low[6:8], up[0:1]], axis=0)
            high = colour.astype(jnp.bfloat16).astype(jnp.float32)
            both = jnp.concatenate(
                [high, high, colour - high, jnp.zeros((7, BLOCK), jnp.float32)], axis=0
            ).astype(jnp.bfloat16)
            pulled = matmul(slopes_wide[tile], both) * weights[tile, block]
            after = matmul(jnp.concatenate(two_pieces(pulled), axis=1), behind)
            past = carried[tile]
            inner = pulled - (after[:, 0:BLOCK] + past) * ratios[tile, block]
            carried[tile] = past + after[:, BLOCK:]
            inner_high, inner_low = two_pieces(inner)
            sums = matmul(basis, inner_high) + matmul(basis, inner_low)
            parts = weight_parts[tile, block]
            tint = matmul(slopes[tile], parts[:, 0:BLOCK])
            tint_low = matmul(slopes[tile], parts[:, BLOCK:])
            tint = tint[0:3] + tint[3:6] + tint_low[0:3]
            mean_x = low[0:1] - middles[tile][0]
            mean_y = low[1:2] - middles[tile][1]
            form_a, form_b, form_c = low[2:3], low[3:4], low[4:5]
            whole, by_x, by_y = sums[0:1], sums[1:2], sums[2:3]
            sum_x = by_x - mean_x * whole
            sum_y = by_y - mean_y * whole
            sum_xx = sums[3:4] - 2.0 * mean_x * by_x + mean_x * mean_x * whole
            sum_xy = sums[4:5] - mean_x * by_y - mean_y * by_x + mean_x * mean_y * whole
            sum_yy = sums[5:6] - 2.0 * mean_y * by_y + mean_y * mean_y * whole
            grads[tile, 0:SUBS, pl.ds(start, BLOCK)] = jnp.concatenate(
                [
                    form_a * sum_x + form_b * sum_y,
                    form_b * sum_x + form_c * sum_y,
                    -0.5 * sum_xx,
                    -sum_xy,
                    -0.5 * sum_yy,
                    whole / low[5:6],
                    tint[0:2],
                ],
                axis=0,
            )
            grads[tile, SUBS : 2 * SUBS, pl.ds(start, BLOCK)] = jnp.broadcast_to(
                tint[2:3], (SUBS, BLOCK)
            )
        return 0

    lax.fori_loop(0, blocks, backward, 0)

    pairs = chunk // 2
    lane_pair = lax.broadcasted_iota(jnp.int32, (pairs, SUBS, wide), 2)

    def scatter(index, _):
        total = jnp.zeros((2 * pairs * (SUBS + 1), wide), jnp.float32)
        for tile in range(per_device):
            main = grads[tile, 0:SUBS, :]
            last = grads[tile, SUBS : 2 * SUBS, :]
            parts = [[], [], [], []]
            main_high = main.astype(jnp.bfloat16).astype(jnp.float32)
            last_high = last.astype(jnp.bfloat16).astype(jnp.float32)
            for pair in range(pairs):
                mine = groups_wide[tile] == index * pairs + pair
                parts[0].append(jnp.where(mine, main_high, 0.0))
                parts[1].append(jnp.where(mine, main - main_high, 0.0))
            for start in range(0, pairs, SUBS):
                number = lax.broadcasted_iota(jnp.int32, (SUBS, entries), 0) + (
                    index * pairs + start
                )
                mine = groups_wide[tile] == number
                parts[2].append(jnp.where(mine, last_high, 0.0))
                parts[3].append(jnp.where(mine, last - last_high, 0.0))
            left = jnp.concatenate(parts[0] + parts[1] + parts[2] + parts[3], axis=0)
            total = total + matmul(left.astype(jnp.bfloat16), hots_wide[tile])
        size = pairs * SUBS
        main = (total[0:size] + total[size : 2 * size]).reshape(pairs, SUBS, wide)
        last = total[2 * size : 2 * size + pairs] + total[2 * size + pairs :]
        turned = pltpu.roll(last, own_rows, 1)
        even = jnp.where(
            lane_pair < own_rows, main, jnp.broadcast_to(turned[:, None, :], main.shape)
        )
        odd = jnp.where(
            lane_pair < own_rows,
            pltpu.roll(main, own_rows, 2),
            jnp.broadcast_to(last[:, None, :], main.shape),
        )
        for pair in range(pairs):
            given[index * chunk + 2 * pair] = even[pair]
            given[index * chunk + 2 * pair + 1] = odd[pair]
        return 0

    lax.fori_loop(0, tiles // batch, scatter, 0)

    def send_back(step, _):
        other, view, tile = owner_at(step)
        to_owner(given.at[other], landed.at[me], back_sem, back_recv, view, tile).start()
        return 0

    lax.fori_loop(1, owners, send_back, 0)
    landed[me] = given[me]
    _, pullback = jax.vjp(lambda source: project(source, cameras), raw)
    all_back = to_owner(
        given.at[rest], landed.at[rest], back_sem, back_recv, next_view, next_tile
    )
    all_back.wait_recv()
    arrived = landed[pl.ds(0, views)]
    for tile in range(1, tiles):
        arrived = arrived + landed[pl.ds(tile * views, views)]
    lower = jnp.concatenate([arrived[view][:, 0:own_rows] for view in range(views)], axis=1)
    upper = jnp.concatenate([arrived[view][:, own_rows:] for view in range(views)], axis=1)
    (returned,) = pullback([lower[row : row + 1] for row in range(8)] + [upper[0:1]])
    slopes_ref[...] = jnp.ones_like(slopes_ref)
    for row in range(width):
        slopes_ref[row : row + 1, :] = returned[row]
    found = matmul(jnp.concatenate(three_pieces(slopes_ref[...]), axis=0), hot_back[...])
    found = found[0:64] + found[64:128] + found[128:192]
    grad_ref[...] = found[0:width]
    seen_ref[...] = found[width : width + 1]

    all_rows.wait_send()
    all_back.wait_send()


def update_kernel(
    params_ref, first_ref, second_ref, grad_ref, seen_ref, drawn_ref,
    new_params_ref, new_first_ref, new_second_ref, image_ref
):
    grad = grad_ref[...]
    seen = seen_ref[...] > 0.5
    first, second, params = first_ref[...], second_ref[...], params_ref[...]
    moved_first = beta_first * first + (1.0 - beta_first) * grad
    moved_second = beta_second * second + (1.0 - beta_second) * grad * grad
    moved_params = params - learn_rate * moved_first / (jnp.sqrt(moved_second) + adam_eps)
    new_first_ref[...] = jnp.where(seen, moved_first, first)
    new_second_ref[...] = jnp.where(seen, moved_second, second)
    new_params_ref[...] = jnp.where(seen, moved_params, params)
    image_ref[...] = drawn_ref[...]


def shards(views, tiles, params, first, second, visible, cameras, tile_lists, tile_blocks, targets):
    own_rows = visible.shape[1]
    per_device, entries = tile_lists.shape[1:]
    blocks = entries // BLOCK
    packet = (SUBS, 2 * own_rows)
    f32 = jnp.float32
    dma = pltpu.SemaphoreType.DMA
    owners = views * tiles
    image_shape = jax.ShapeDtypeStruct((3, 1, per_device * PIX), f32)
    grad, seen, drawn = pl.pallas_call(
        functools.partial(step_kernel, views, tiles),
        out_shape=[
            jax.ShapeDtypeStruct(params.shape, f32),
            jax.ShapeDtypeStruct((1, params.shape[1]), f32),
            image_shape,
        ],
        in_specs=[ANY, VMEM, SMEM, ANY, SMEM, VMEM],
        out_specs=[VMEM, VMEM, VMEM],
        scratch_shapes=[
            pltpu.VMEM(params.shape, f32),
            pltpu.VMEM((per_device, entries), jnp.int32),
            pltpu.VMEM((64, views * own_rows), f32),
            pltpu.VMEM((views,) + packet, f32),
            pltpu.VMEM((owners,) + packet, f32),
            pltpu.VMEM((views * own_rows, params.shape[1]), jnp.bfloat16),
            pltpu.VMEM((per_device, 4 * own_rows, entries), jnp.bfloat16),
            pltpu.VMEM((per_device, entries, 2 * own_rows), jnp.bfloat16),
            pltpu.VMEM((per_device, 2 * SUBS, entries), f32),
            pltpu.VMEM((per_device, 2 * SUBS, entries), f32),
            pltpu.VMEM((per_device, blocks, PIX, BLOCK), f32),
            pltpu.VMEM((per_device, blocks, PIX, 2 * BLOCK), jnp.bfloat16),
            pltpu.VMEM((per_device, blocks, PIX, BLOCK), f32),
            pltpu.VMEM((per_device, PIX, BLOCK), f32),
            pltpu.VMEM((per_device, PIX, 2 * SUBS), f32),
            pltpu.VMEM((owners,) + packet, f32),
            pltpu.VMEM((owners,) + packet, f32),
            pltpu.VMEM((64, views * own_rows), f32),
            dma((2,)),
            dma((1,)), dma((1,)), dma((1,)), dma((1,)),
        ],
        compiler_params=pltpu.CompilerParams(
            collective_id=0, has_side_effects=True, vmem_limit_bytes=LIMIT
        ),
        name="render_step",
    )(params, visible, cameras, tile_lists[0], tile_blocks, jnp.transpose(targets, (1, 0, 2)))
    like = jax.ShapeDtypeStruct(params.shape, f32)
    new_params, new_first, new_second, rendered = pl.pallas_call(
        update_kernel,
        out_shape=[like, like, like, image_shape],
        in_specs=[VMEM] * 6,
        out_specs=[VMEM] * 4,
        compiler_params=pltpu.CompilerParams(vmem_limit_bytes=LIMIT),
        name="update",
    )(params, first, second, grad, seen, drawn)
    return (new_params, new_first, new_second, jnp.transpose(rendered, (1, 0, 2)))


def solution(mesh):
    in_specs = (
        P(None, ("view", "tile")),
        P(None, ("view", "tile")),
        P(None, ("view", "tile")),
        P(None, ("view", "tile")),
        P(),
        P("view", "tile", None),
        P("view", "tile"),
        P("view", None, "tile"),
    )
    out_specs = (
        P(None, ("view", "tile")),
        P(None, ("view", "tile")),
        P(None, ("view", "tile")),
        P("view", None, "tile"),
    )
    body = functools.partial(shards, mesh.shape["view"], mesh.shape["tile"])
    return jax.shard_map(body, mesh=mesh, in_specs=in_specs, out_specs=out_specs, check_vma=False)
```

```python
import functools

import jax
import jax.numpy as jnp
from jax import lax
from jax.experimental import pallas as pl
from jax.experimental.pallas import tpu as pltpu
from jax.sharding import PartitionSpec as P

SIDE = 16
PIX = 256
BLOCK = 128
WIN_COLS = 8
SUBS = 8
PACK = 5
MESH = pl.DeviceIdType.MESH
VMEM = pl.BlockSpec(memory_space=pltpu.VMEM)
ANY = pl.BlockSpec(memory_space=pl.ANY)
SMEM = pl.BlockSpec(memory_space=pltpu.SMEM)
LIMIT = 62 * 1024 * 1024


harm_zero = 0.28209479177387814
harm_one = 0.4886025119029199
harm_two = (
    1.0925484305920792,
    -1.0925484305920792,
    0.31539156525252005,
    -1.0925484305920792,
    0.5462742152960396,
)
harm_three = (
    -0.5900435899266435,
    2.890611442640554,
    -0.4570457994644658,
    0.3731763325901154,
    -0.4570457994644658,
    1.445305721320277,
    -0.5900435899266435,
)
learn_rate = 0.05
beta_first = 0.9
beta_second = 0.999
adam_eps = 1e-08
blur_add = 0.3


def rotation(real_part, axis_one, axis_two, axis_three):
    inverse = lax.rsqrt(
        real_part * real_part + axis_one * axis_one + axis_two * axis_two + axis_three * axis_three
    )
    real_unit = real_part * inverse
    unit_one = axis_one * inverse
    unit_two = axis_two * inverse
    unit_three = axis_three * inverse
    return (
        (
            1.0 - 2.0 * (unit_two * unit_two + unit_three * unit_three),
            2.0 * (unit_one * unit_two - real_unit * unit_three),
            2.0 * (unit_one * unit_three + real_unit * unit_two),
        ),
        (
            2.0 * (unit_one * unit_two + real_unit * unit_three),
            1.0 - 2.0 * (unit_one * unit_one + unit_three * unit_three),
            2.0 * (unit_two * unit_three - real_unit * unit_one),
        ),
        (
            2.0 * (unit_one * unit_three - real_unit * unit_two),
            2.0 * (unit_two * unit_three + real_unit * unit_one),
            1.0 - 2.0 * (unit_one * unit_one + unit_two * unit_two),
        ),
    )


def harmonics(first_dir, second_dir, third_dir):
    sq_first = first_dir * first_dir
    sq_second = second_dir * second_dir
    sq_third = third_dir * third_dir
    return [
        harm_zero,
        -harm_one * second_dir,
        harm_one * third_dir,
        -harm_one * first_dir,
        harm_two[0] * first_dir * second_dir,
        harm_two[1] * second_dir * third_dir,
        harm_two[2] * (2.0 * sq_third - sq_first - sq_second),
        harm_two[3] * first_dir * third_dir,
        harm_two[4] * (sq_first - sq_second),
        harm_three[0] * second_dir * (3.0 * sq_first - sq_second),
        harm_three[1] * first_dir * second_dir * third_dir,
        harm_three[2] * second_dir * (4.0 * sq_third - sq_first - sq_second),
        harm_three[3] * third_dir * (2.0 * sq_third - 3.0 * sq_first - 3.0 * sq_second),
        harm_three[4] * first_dir * (4.0 * sq_third - sq_first - sq_second),
        harm_three[5] * third_dir * (sq_first - sq_second),
        harm_three[6] * first_dir * (sq_first - 3.0 * sq_second),
    ]


def project(raw, camera):
    camera_turn = rotation(camera[0], camera[1], camera[2], camera[3])
    shift_vec = (camera[4], camera[5], camera[6])
    focal_x = camera[7]
    focal_y = camera[8]
    position = (raw[0], raw[1], raw[2])
    viewed = [
        camera_turn[across][0] * position[0]
        + camera_turn[across][1] * position[1]
        + camera_turn[across][2] * position[2]
        + shift_vec[across]
        for across in range(3)
    ]
    inverse = 1.0 / viewed[2]
    mean_x = focal_x * viewed[0] * inverse + camera[9]
    mean_y = focal_y * viewed[1] * inverse + camera[10]
    gauss_turn = rotation(raw[6], raw[7], raw[8], raw[9])
    stretch = [jnp.exp(raw[3 + column]) for column in range(3)]
    jac_xx = focal_x * inverse
    jac_xz = -focal_x * viewed[0] * inverse * inverse
    jac_yy = focal_y * inverse
    jac_yz = -focal_y * viewed[1] * inverse * inverse
    leading_x = [
        jac_xx * camera_turn[0][column] + jac_xz * camera_turn[2][column] for column in range(3)
    ]
    leading_y = [
        jac_yy * camera_turn[1][column] + jac_yz * camera_turn[2][column] for column in range(3)
    ]
    axes_x = [
        (
            leading_x[0] * gauss_turn[0][column]
            + leading_x[1] * gauss_turn[1][column]
            + leading_x[2] * gauss_turn[2][column]
        )
        * stretch[column]
        for column in range(3)
    ]
    axes_y = [
        (
            leading_y[0] * gauss_turn[0][column]
            + leading_y[1] * gauss_turn[1][column]
            + leading_y[2] * gauss_turn[2][column]
        )
        * stretch[column]
        for column in range(3)
    ]
    cov_xx = axes_x[0] * axes_x[0] + axes_x[1] * axes_x[1] + axes_x[2] * axes_x[2] + blur_add
    cov_xy = axes_x[0] * axes_y[0] + axes_x[1] * axes_y[1] + axes_x[2] * axes_y[2]
    cov_yy = axes_y[0] * axes_y[0] + axes_y[1] * axes_y[1] + axes_y[2] * axes_y[2] + blur_add
    determ = cov_xx * cov_yy - cov_xy * cov_xy
    opacity = 1.0 / (1.0 + jnp.exp(-raw[10]))
    camera_eye = [
        -(
            camera_turn[0][column] * shift_vec[0]
            + camera_turn[1][column] * shift_vec[1]
            + camera_turn[2][column] * shift_vec[2]
        )
        for column in range(3)
    ]
    offset = [position[column] - camera_eye[column] for column in range(3)]
    length = lax.rsqrt(offset[0] * offset[0] + offset[1] * offset[1] + offset[2] * offset[2])
    harmonic_terms = harmonics(offset[0] * length, offset[1] * length, offset[2] * length)
    colours = []
    for channel in range(3):
        total = 0.5 + jnp.zeros_like(opacity)
        for harmonic in range(16):
            total = total + raw[11 + 16 * channel + harmonic] * harmonic_terms[harmonic]
        colours.append(total)
    return [mean_x, mean_y, cov_yy / determ, -cov_xy / determ, cov_xx / determ, opacity] + colours


def three_pieces(value):
    high = value.astype(jnp.bfloat16)
    rest = value - high.astype(jnp.float32)
    middle = rest.astype(jnp.bfloat16)
    low = (rest - middle.astype(jnp.float32)).astype(jnp.bfloat16)
    return high, middle, low


def two_pieces(value):
    high = value.astype(jnp.bfloat16)
    return high, (value - high.astype(jnp.float32)).astype(jnp.bfloat16)


def matmul(left, right):
    return jnp.dot(left, right, preferred_element_type=jnp.float32)


def matmul_nt(left, right):
    return lax.dot_general(
        left, right, (((1,), (1,)), ((), ())), preferred_element_type=jnp.float32
    )


def visible_row(visible_ref):
    views = visible_ref.shape[0]
    return jnp.concatenate([visible_ref[view : view + 1, :] for view in range(views)], axis=1)


def column_hot(visible_ref, columns):
    ids = visible_row(visible_ref)
    place = lax.broadcasted_iota(jnp.int32, (columns, ids.shape[1]), 0)
    return jnp.where(place == ids, 1.0, 0.0).astype(jnp.bfloat16)


def camera_rows(cameras_ref, own_rows):
    views = cameras_ref.shape[0]
    lane = lax.broadcasted_iota(jnp.int32, (1, views * own_rows), 1)
    rows = []
    for entry in range(11):
        row = jnp.full(lane.shape, cameras_ref[0, entry], jnp.float32)
        for view in range(1, views):
            row = jnp.where(lane >= view * own_rows, cameras_ref[view, entry], row)
        rows.append(row)
    return rows


def down(row, lanes):
    spread_row = jnp.broadcast_to(row.astype(jnp.float32), (lanes, row.shape[1]))
    return jnp.transpose(spread_row)


def list_hot_down(lists, lanes):
    ids = down(lax.bitwise_and(lists, lanes - 1), lanes)
    lane = lax.broadcasted_iota(jnp.int32, ids.shape, 1).astype(jnp.float32)
    return jnp.where(ids == lane, 1.0, 0.0).astype(jnp.bfloat16)


def list_hot(lists, lanes):
    place = lax.broadcasted_iota(jnp.int32, (lanes, lists.shape[1]), 0)
    hot = jnp.where(place == lax.bitwise_and(lists, lanes - 1), 1.0, 0.0).astype(jnp.bfloat16)
    return hot, lax.shift_right_logical(lists, lanes.bit_length() - 1)


def step_kernel(
    views, tiles, params_hbm, visible_ref, cameras_ref, lists_hbm, counts_ref, targets_ref,
    grad_ref, seen_ref, image_ref,
    params_ref, lists_ref, picked_ref, outgoing, everyone, hot_back, hots, hots_wide, rows, grads,
    weights, weight_parts, ratios, carried, held, given, landed, slopes_ref,
    load_sem, out_sem, out_recv, back_sem, back_recv
):
    my_view, my_tile = lax.axis_index("view"), lax.axis_index("tile")
    owners = views * tiles
    me = my_tile * views + my_view

    partners = []
    for step_view in range(views):
        view = lax.rem(my_view + step_view, views)
        for step_tile in range(tiles):
            if step_view or step_tile:
                tile = lax.rem(my_tile + step_tile, tiles)
                partners.append((tile * views + view, view, tile))
    load_params = pltpu.make_async_copy(params_hbm, params_ref, load_sem.at[0])
    load_lists = pltpu.make_async_copy(lists_hbm, lists_ref, load_sem.at[1])
    load_params.start()
    load_lists.start()
    barrier = pltpu.get_barrier_semaphore()

    for _, view, tile in partners:
        pl.semaphore_signal(barrier, inc=1, device_id=(view, tile), device_id_type=MESH)

    width, columns = params_ref.shape
    own_rows = visible_ref.shape[1]
    wide = 2 * own_rows
    hot = column_hot(visible_ref, columns)
    cameras = camera_rows(cameras_ref, own_rows)
    load_params.wait()
    padded = jnp.concatenate(
        [params_ref[...], jnp.zeros((64 - width, columns), jnp.float32)], axis=0
    )
    found = matmul(jnp.concatenate(three_pieces(padded), axis=0), hot)
    picked_ref[...] = found[0:64] + found[64:128] + found[128:192]
    raw = [picked_ref[row : row + 1, :] for row in range(width)]
    out = project(raw, cameras)
    lower = jnp.concatenate(out[0:4] + [out[8]], axis=0)
    upper = jnp.concatenate(out[4:8] + [jnp.zeros_like(out[8])], axis=0)
    for view in range(views):
        span = slice(view * own_rows, (view + 1) * own_rows)
        outgoing[view] = jnp.concatenate([lower[:, span], upper[:, span]], axis=1)

    def to_owner(source, landing, sends, receives, view, tile):
        return pltpu.make_async_remote_copy(
            src_ref=source, dst_ref=landing, send_sem=sends.at[0], recv_sem=receives.at[0],
            device_id=(view, tile), device_id_type=MESH,
        )

    everyone[me] = outgoing[my_view]
    pl.semaphore_wait(barrier, owners - 1)
    for _, view, tile in partners:
        to_owner(outgoing.at[view], everyone.at[me], out_sem, out_recv, view, tile).start()

    load_lists.wait()
    per_device, entries = lists_ref.shape
    groups, groups_wide = [], []
    for tile in range(per_device):
        ids = lists_ref[tile : tile + 1, :]
        narrow, group = list_hot(ids, own_rows)
        hots[tile] = jnp.concatenate([narrow] * 4, axis=0)
        groups.append(jnp.broadcast_to(group, (SUBS, entries)))
        hots_wide[tile] = list_hot_down(ids, wide)
        group = lax.shift_right_logical(ids, wide.bit_length() - 1)
        groups_wide.append(jnp.broadcast_to(group, (SUBS, entries)))

    ids_down = down(visible_row(visible_ref), BLOCK)
    for start in range(0, columns, BLOCK):
        lane_at = lax.broadcasted_iota(jnp.int32, ids_down.shape, 1).astype(jnp.float32) + start
        hot_back[:, start : start + BLOCK] = jnp.where(ids_down == lane_at, 1.0, 0.0).astype(
            jnp.bfloat16
        )
    rest = pl.ds(0, owners - 1)
    _, next_view, next_tile = partners[0]
    all_rows = to_owner(
        everyone.at[rest], everyone.at[rest], out_sem, out_recv, next_view, next_tile
    )
    all_rows.wait_recv()

    batch = max(1, min(tiles, 32 // views))
    chunk = batch * views
    lane = lax.broadcasted_iota(jnp.int32, (chunk * (SUBS + 1), wide), 1)

    def gather(index, held_rows):
        source = everyone[pl.ds(index * chunk, chunk)]
        last = source[:, 4, :]
        source = jnp.concatenate([source, jnp.zeros((chunk, SUBS - PACK, wide), jnp.float32)], axis=1)
        turned = pltpu.roll(pltpu.roll(source, own_rows, 2), 4, 1)
        source = jnp.where(lax.broadcasted_iota(jnp.int32, source.shape, 1) < 4, source, turned)
        source = jnp.concatenate([source.reshape(chunk * SUBS, wide), last], axis=0)
        high, middle, low = [piece.astype(jnp.float32) for piece in three_pieces(source)]
        source = jnp.concatenate(
            [
                jnp.where(lane < own_rows, high, pltpu.roll(middle, own_rows, 1)),
                jnp.where(lane < own_rows, low, 0.0),
            ],
            axis=1,
        ).astype(jnp.bfloat16)
        new_rows = []
        for tile in range(per_device):
            located = matmul(source, hots[tile])
            first, second = held_rows[tile]
            for owner in range(chunk):
                mine = groups[tile] == index * chunk + owner
                first = first + jnp.where(mine, located[owner * SUBS : (owner + 1) * SUBS], 0.0)
            for start in range(0, chunk, SUBS):
                begin = chunk * SUBS + start
                number = lax.broadcasted_iota(jnp.int32, (SUBS, entries), 0) + (
                    index * chunk + start
                )
                second = second + jnp.where(
                    groups[tile] == number, located[begin : begin + SUBS], 0.0
                )
            new_rows.append((first, second))
        return tuple(new_rows)

    empty = jnp.zeros((SUBS, entries), jnp.float32)
    collected = lax.fori_loop(0, tiles // batch, gather, ((empty, empty),) * per_device)
    for tile in range(per_device):
        rows[tile, 0:SUBS, :] = collected[tile][0]
        rows[tile, SUBS : 2 * SUBS, :] = jnp.broadcast_to(
            jnp.sum(collected[tile][1], axis=0, keepdims=True), (SUBS, entries)
        )

    first_tile = my_tile * per_device
    half = SIDE // 2
    middles = []
    for tile in range(per_device):
        number = first_tile + tile
        middles.append(
            (
                (lax.rem(number, WIN_COLS) * SIDE + half).astype(jnp.float32),
                (lax.div(number, WIN_COLS) * SIDE + half).astype(jnp.float32),
            )
        )
    side_x = lax.broadcasted_iota(jnp.int32, (SIDE, BLOCK), 0).astype(jnp.float32) + (0.5 - half)
    spot = lax.bitwise_and(
        lax.broadcasted_iota(jnp.int32, (2 * BLOCK, 2 * BLOCK), 0), BLOCK - 1
    )
    lane_two = lax.broadcasted_iota(jnp.int32, (2 * BLOCK, 2 * BLOCK), 1)
    ahead = jnp.where((spot < lane_two) | (lane_two >= BLOCK), 1.0, 0.0).astype(jnp.bfloat16)
    behind = jnp.where((spot > lane_two) | (lane_two >= BLOCK), 1.0, 0.0).astype(jnp.bfloat16)
    blocks = entries // BLOCK
    stride = 2 if blocks % 2 == 0 else 1

    carried[...] = jnp.zeros_like(carried)
    held[...] = jnp.zeros_like(held)

    def forward(block, _):
        start = pl.multiple_of(block * BLOCK, BLOCK)
        for tile in range(per_device):
            live = (block < counts_ref[0, tile]).astype(jnp.float32)
            low = rows[tile, 0:SUBS, pl.ds(start, BLOCK)]
            up = rows[tile, SUBS : 2 * SUBS, pl.ds(start, BLOCK)]
            mean_x = low[0:1] - middles[tile][0]
            mean_y = low[1:2] - middles[tile][1]
            form_a = -0.5 * low[2:3]
            form_b = -low[3:4]
            form_c = -0.5 * low[4:5]
            opacity = low[5:6] * live
            delta_x = side_x - mean_x
            square = form_a * delta_x * delta_x
            cross = form_b * delta_x
            pieces = []
            for line in range(SIDE):
                delta_y = (line + 0.5 - half) - mean_y
                pieces.append((cross + form_c * delta_y) * delta_y + square)
            alpha = opacity * jnp.exp(jnp.concatenate(pieces, axis=0))
            decay = jnp.log(1.0 - alpha)
            before = matmul(jnp.concatenate(two_pieces(decay), axis=1), ahead)
            past = carried[tile]
            weight = alpha * jnp.exp(before[:, 0:BLOCK] + past)
            carried[tile] = past + before[:, BLOCK:]
            ratios[tile, block] = alpha * jnp.exp(-decay)
            weights[tile, block] = weight
            parts = jnp.concatenate(two_pieces(weight), axis=1)
            weight_parts[tile, block] = parts
            colour = jnp.concatenate([low[6:8], up[0:1], jnp.zeros((5, BLOCK), jnp.float32)], axis=0)
            high = colour.astype(jnp.bfloat16).astype(jnp.float32)
            both = jnp.concatenate([high, colour - high], axis=0).astype(jnp.bfloat16)
            held[tile] += matmul_nt(parts, jnp.concatenate([both, both], axis=1))
        return 0

    def forward_pair(index, _):
        for part in range(stride):
            forward(index * stride + part, 0)
        return 0

    lax.fori_loop(0, blocks // stride, forward_pair, 0)

    slopes, slopes_wide = [], []
    for tile in range(per_device):
        drawn = jnp.transpose(
            jnp.concatenate(
                [held[tile], jnp.zeros((PIX, BLOCK - 2 * SUBS), jnp.float32)], axis=1
            )
        )
        drawn = drawn[0:3] + drawn[SUBS : SUBS + 3]
        image_ref[:, 0, tile * PIX : (tile + 1) * PIX] = drawn
        slope = 2.0 * (drawn - targets_ref[:, 0, tile * PIX : (tile + 1) * PIX])
        high = slope.astype(jnp.bfloat16).astype(jnp.float32)
        stack = jnp.concatenate(
            [high, slope - high, high, jnp.zeros((BLOCK - 9, PIX), jnp.float32)], axis=0
        )
        slopes.append(stack[0 : 2 * SUBS].astype(jnp.bfloat16))
        slopes_wide.append(jnp.transpose(stack).astype(jnp.bfloat16)[:, 0 : 2 * SUBS])

    pixel = lax.broadcasted_iota(jnp.int32, (2 * SUBS, PIX), 1)
    kind = lax.broadcasted_iota(jnp.int32, (2 * SUBS, PIX), 0)
    at_x = lax.bitwise_and(pixel, SIDE - 1).astype(jnp.float32) + (0.5 - half)
    at_y = lax.shift_right_logical(pixel, SIDE.bit_length() - 1).astype(jnp.float32) + (0.5 - half)
    power_x = jnp.where((kind == 1) | (kind == 4), at_x, jnp.where(kind == 3, at_x * at_x, 1.0))
    power_y = jnp.where((kind == 2) | (kind == 4), at_y, jnp.where(kind == 5, at_y * at_y, 1.0))
    basis = jnp.where(kind < 6, power_x * power_y, 0.0).astype(jnp.bfloat16)

    carried[...] = jnp.zeros_like(carried)

    def backward(index, _):
        block = blocks - 1 - index
        start = pl.multiple_of(block * BLOCK, BLOCK)
        for tile in range(per_device):
            low = rows[tile, 0:SUBS, pl.ds(start, BLOCK)]
            up = rows[tile, SUBS : 2 * SUBS, pl.ds(start, BLOCK)]
            colour = jnp.concatenate([low[6:8], up[0:1]], axis=0)
            high = colour.astype(jnp.bfloat16).astype(jnp.float32)
            both = jnp.concatenate(
                [high, high, colour - high, jnp.zeros((7, BLOCK), jnp.float32)], axis=0
            ).astype(jnp.bfloat16)
            pulled = matmul(slopes_wide[tile], both) * weights[tile, block]
            after = matmul(jnp.concatenate(two_pieces(pulled), axis=1), behind)
            past = carried[tile]
            inner = pulled - (after[:, 0:BLOCK] + past) * ratios[tile, block]
            carried[tile] = past + after[:, BLOCK:]
            sums = matmul(basis, jnp.concatenate(two_pieces(inner), axis=1))
            sums = sums[:, 0:BLOCK] + sums[:, BLOCK:]
            tint = matmul(slopes[tile], weight_parts[tile, block])
            tint = tint[0:3, 0:BLOCK] + tint[3:6, 0:BLOCK] + tint[0:3, BLOCK:]
            mean_x = low[0:1] - middles[tile][0]
            mean_y = low[1:2] - middles[tile][1]
            form_a, form_b, form_c = low[2:3], low[3:4], low[4:5]
            whole, by_x, by_y = sums[0:1], sums[1:2], sums[2:3]
            sum_x = by_x - mean_x * whole
            sum_y = by_y - mean_y * whole
            sum_xx = sums[3:4] - 2.0 * mean_x * by_x + mean_x * mean_x * whole
            sum_xy = sums[4:5] - mean_x * by_y - mean_y * by_x + mean_x * mean_y * whole
            sum_yy = sums[5:6] - 2.0 * mean_y * by_y + mean_y * mean_y * whole
            grads[tile, 0:SUBS, pl.ds(start, BLOCK)] = jnp.concatenate(
                [
                    form_a * sum_x + form_b * sum_y,
                    form_b * sum_x + form_c * sum_y,
                    -0.5 * sum_xx,
                    -sum_xy,
                    -0.5 * sum_yy,
                    whole / low[5:6],
                    tint[0:2],
                ],
                axis=0,
            )
            grads[tile, SUBS : 2 * SUBS, pl.ds(start, BLOCK)] = jnp.broadcast_to(
                tint[2:3], (SUBS, BLOCK)
            )
        return 0

    def backward_pair(index, _):
        for part in range(stride):
            backward(index * stride + part, 0)
        return 0

    lax.fori_loop(0, blocks // stride, backward_pair, 0)

    pairs = chunk // 2
    lane_pair = lax.broadcasted_iota(jnp.int32, (pairs, SUBS, wide), 2)

    def scatter(index, _):
        total = jnp.zeros((2 * pairs * (SUBS + 1), wide), jnp.float32)
        for tile in range(per_device):
            main = grads[tile, 0:SUBS, :]
            last = grads[tile, SUBS : 2 * SUBS, :]
            parts = [[], [], [], []]
            main_high = main.astype(jnp.bfloat16).astype(jnp.float32)
            last_high = last.astype(jnp.bfloat16).astype(jnp.float32)
            for pair in range(pairs):
                mine = groups_wide[tile] == index * pairs + pair
                parts[0].append(jnp.where(mine, main_high, 0.0))
                parts[1].append(jnp.where(mine, main - main_high, 0.0))
            for start in range(0, pairs, SUBS):
                number = lax.broadcasted_iota(jnp.int32, (SUBS, entries), 0) + (
                    index * pairs + start
                )
                mine = groups_wide[tile] == number
                parts[2].append(jnp.where(mine, last_high, 0.0))
                parts[3].append(jnp.where(mine, last - last_high, 0.0))
            left = jnp.concatenate(parts[0] + parts[1] + parts[2] + parts[3], axis=0)
            total = total + matmul(left.astype(jnp.bfloat16), hots_wide[tile])
        size = pairs * SUBS
        main = (total[0:size] + total[size : 2 * size]).reshape(pairs, SUBS, wide)
        last = total[2 * size : 2 * size + pairs] + total[2 * size + pairs :]
        raised = pltpu.roll(main, 4, 1)
        row_pair = lax.broadcasted_iota(jnp.int32, main.shape, 1)
        last_turned = pltpu.roll(last, own_rows, 1)
        low_lane = lane_pair < own_rows
        even = jnp.where(
            row_pair < 4,
            jnp.where(low_lane, main, pltpu.roll(raised, own_rows, 2)),
            jnp.broadcast_to(last[:, None, :], main.shape),
        )
        odd = jnp.where(
            row_pair < 4,
            jnp.where(low_lane, pltpu.roll(main, own_rows, 2), raised),
            jnp.broadcast_to(last_turned[:, None, :], main.shape),
        )
        for pair in range(pairs):
            given[index * chunk + 2 * pair] = even[pair, 0:PACK]
            given[index * chunk + 2 * pair + 1] = odd[pair, 0:PACK]
        return 0

    lax.fori_loop(0, tiles // batch, scatter, 0)

    for other, view, tile in partners:
        to_owner(given.at[other], landed.at[me], back_sem, back_recv, view, tile).start()
    landed[me] = given[me]
    _, pullback = jax.vjp(lambda source: project(source, cameras), raw)
    all_back = to_owner(
        given.at[rest], landed.at[rest], back_sem, back_recv, next_view, next_tile
    )
    all_back.wait_recv()
    arrived = landed[pl.ds(0, views)]
    for tile in range(1, tiles):
        arrived = arrived + landed[pl.ds(tile * views, views)]
    lower = jnp.concatenate([arrived[view][:, 0:own_rows] for view in range(views)], axis=1)
    upper = jnp.concatenate([arrived[view][:, own_rows:] for view in range(views)], axis=1)
    (returned,) = pullback(
        [lower[row : row + 1] for row in range(4)]
        + [upper[row : row + 1] for row in range(4)]
        + [lower[4:5]]
    )
    slopes_ref[...] = jnp.ones_like(slopes_ref)
    for row in range(width):
        slopes_ref[row : row + 1, :] = returned[row]
    found = matmul(jnp.concatenate(three_pieces(slopes_ref[...]), axis=0), hot_back[...])
    found = found[0:64] + found[64:128] + found[128:192]
    grad_ref[...] = found[0:width]
    seen_ref[...] = found[width : width + 1]

    all_rows.wait_send()
    all_back.wait_send()


def update_kernel(
    params_ref, first_ref, second_ref, grad_ref, seen_ref, drawn_ref,
    new_params_ref, new_first_ref, new_second_ref, image_ref
):
    grad = grad_ref[...]
    seen = seen_ref[...] > 0.5
    first, second, params = first_ref[...], second_ref[...], params_ref[...]
    moved_first = beta_first * first + (1.0 - beta_first) * grad
    moved_second = beta_second * second + (1.0 - beta_second) * grad * grad
    moved_params = params - learn_rate * moved_first / (jnp.sqrt(moved_second) + adam_eps)
    new_first_ref[...] = jnp.where(seen, moved_first, first)
    new_second_ref[...] = jnp.where(seen, moved_second, second)
    new_params_ref[...] = jnp.where(seen, moved_params, params)
    image_ref[...] = drawn_ref[...]


def shards(views, tiles, params, first, second, visible, cameras, tile_lists, tile_blocks, targets):
    own_rows = visible.shape[1]
    per_device, entries = tile_lists.shape[1:]
    blocks = entries // BLOCK
    packet = (PACK, 2 * own_rows)
    f32 = jnp.float32
    dma = pltpu.SemaphoreType.DMA
    owners = views * tiles
    image_shape = jax.ShapeDtypeStruct((3, 1, per_device * PIX), f32)
    grad, seen, drawn = pl.pallas_call(
        functools.partial(step_kernel, views, tiles),
        out_shape=[
            jax.ShapeDtypeStruct(params.shape, f32),
            jax.ShapeDtypeStruct((1, params.shape[1]), f32),
            image_shape,
        ],
        in_specs=[ANY, VMEM, SMEM, ANY, SMEM, VMEM],
        out_specs=[VMEM, VMEM, VMEM],
        scratch_shapes=[
            pltpu.VMEM(params.shape, f32),
            pltpu.VMEM((per_device, entries), jnp.int32),
            pltpu.VMEM((64, views * own_rows), f32),
            pltpu.VMEM((views,) + packet, f32),
            pltpu.VMEM((owners,) + packet, f32),
            pltpu.VMEM((views * own_rows, params.shape[1]), jnp.bfloat16),
            pltpu.VMEM((per_device, 4 * own_rows, entries), jnp.bfloat16),
            pltpu.VMEM((per_device, entries, 2 * own_rows), jnp.bfloat16),
            pltpu.VMEM((per_device, 2 * SUBS, entries), f32),
            pltpu.VMEM((per_device, 2 * SUBS, entries), f32),
            pltpu.VMEM((per_device, blocks, PIX, BLOCK), f32),
            pltpu.VMEM((per_device, blocks, PIX, 2 * BLOCK), jnp.bfloat16),
            pltpu.VMEM((per_device, blocks, PIX, BLOCK), f32),
            pltpu.VMEM((per_device, PIX, BLOCK), f32),
            pltpu.VMEM((per_device, PIX, 2 * SUBS), f32),
            pltpu.VMEM((owners,) + packet, f32),
            pltpu.VMEM((owners,) + packet, f32),
            pltpu.VMEM((64, views * own_rows), f32),
            dma((2,)),
            dma((1,)), dma((1,)), dma((1,)), dma((1,)),
        ],
        compiler_params=pltpu.CompilerParams(
            collective_id=0, has_side_effects=True, vmem_limit_bytes=LIMIT
        ),
        name="render_step",
    )(params, visible, cameras, tile_lists[0], tile_blocks, jnp.transpose(targets, (1, 0, 2)))
    like = jax.ShapeDtypeStruct(params.shape, f32)
    new_params, new_first, new_second, rendered = pl.pallas_call(
        update_kernel,
        out_shape=[like, like, like, image_shape],
        in_specs=[VMEM] * 6,
        out_specs=[VMEM] * 4,
        compiler_params=pltpu.CompilerParams(vmem_limit_bytes=LIMIT),
        name="update",
    )(params, first, second, grad, seen, drawn)
    return (new_params, new_first, new_second, jnp.transpose(rendered, (1, 0, 2)))


def solution(mesh):
    in_specs = (
        P(None, ("view", "tile")),
        P(None, ("view", "tile")),
        P(None, ("view", "tile")),
        P(None, ("view", "tile")),
        P(),
        P("view", "tile", None),
        P("view", "tile"),
        P("view", None, "tile"),
    )
    out_specs = (
        P(None, ("view", "tile")),
        P(None, ("view", "tile")),
        P(None, ("view", "tile")),
        P("view", None, "tile"),
    )
    body = functools.partial(shards, mesh.shape["view"], mesh.shape["tile"])
    return jax.shard_map(body, mesh=mesh, in_specs=in_specs, out_specs=out_specs, check_vma=False)
```

```python
import functools

import jax
import jax.numpy as jnp
from jax import lax
from jax.experimental import pallas as pl
from jax.experimental.pallas import tpu as pltpu
from jax.sharding import PartitionSpec as P

SIDE = 16
PIX = 256
BLOCK = 128
WIN_COLS = 8
SUBS = 8
PACK = 5
MESH = pl.DeviceIdType.MESH
VMEM = pl.BlockSpec(memory_space=pltpu.VMEM)
ANY = pl.BlockSpec(memory_space=pl.ANY)
SMEM = pl.BlockSpec(memory_space=pltpu.SMEM)
LIMIT = 62 * 1024 * 1024


harm_zero = 0.28209479177387814
harm_one = 0.4886025119029199
harm_two = (
    1.0925484305920792,
    -1.0925484305920792,
    0.31539156525252005,
    -1.0925484305920792,
    0.5462742152960396,
)
harm_three = (
    -0.5900435899266435,
    2.890611442640554,
    -0.4570457994644658,
    0.3731763325901154,
    -0.4570457994644658,
    1.445305721320277,
    -0.5900435899266435,
)
learn_rate = 0.05
beta_first = 0.9
beta_second = 0.999
adam_eps = 1e-08
blur_add = 0.3


def rotation(real_part, axis_one, axis_two, axis_three):
    inverse = lax.rsqrt(
        real_part * real_part + axis_one * axis_one + axis_two * axis_two + axis_three * axis_three
    )
    real_unit = real_part * inverse
    unit_one = axis_one * inverse
    unit_two = axis_two * inverse
    unit_three = axis_three * inverse
    return (
        (
            1.0 - 2.0 * (unit_two * unit_two + unit_three * unit_three),
            2.0 * (unit_one * unit_two - real_unit * unit_three),
            2.0 * (unit_one * unit_three + real_unit * unit_two),
        ),
        (
            2.0 * (unit_one * unit_two + real_unit * unit_three),
            1.0 - 2.0 * (unit_one * unit_one + unit_three * unit_three),
            2.0 * (unit_two * unit_three - real_unit * unit_one),
        ),
        (
            2.0 * (unit_one * unit_three - real_unit * unit_two),
            2.0 * (unit_two * unit_three + real_unit * unit_one),
            1.0 - 2.0 * (unit_one * unit_one + unit_two * unit_two),
        ),
    )


def harmonics(first_dir, second_dir, third_dir):
    sq_first = first_dir * first_dir
    sq_second = second_dir * second_dir
    sq_third = third_dir * third_dir
    return [
        harm_zero,
        -harm_one * second_dir,
        harm_one * third_dir,
        -harm_one * first_dir,
        harm_two[0] * first_dir * second_dir,
        harm_two[1] * second_dir * third_dir,
        harm_two[2] * (2.0 * sq_third - sq_first - sq_second),
        harm_two[3] * first_dir * third_dir,
        harm_two[4] * (sq_first - sq_second),
        harm_three[0] * second_dir * (3.0 * sq_first - sq_second),
        harm_three[1] * first_dir * second_dir * third_dir,
        harm_three[2] * second_dir * (4.0 * sq_third - sq_first - sq_second),
        harm_three[3] * third_dir * (2.0 * sq_third - 3.0 * sq_first - 3.0 * sq_second),
        harm_three[4] * first_dir * (4.0 * sq_third - sq_first - sq_second),
        harm_three[5] * third_dir * (sq_first - sq_second),
        harm_three[6] * first_dir * (sq_first - 3.0 * sq_second),
    ]


def project(raw, camera):
    camera_turn = rotation(camera[0], camera[1], camera[2], camera[3])
    shift_vec = (camera[4], camera[5], camera[6])
    focal_x = camera[7]
    focal_y = camera[8]
    position = (raw[0], raw[1], raw[2])
    viewed = [
        camera_turn[across][0] * position[0]
        + camera_turn[across][1] * position[1]
        + camera_turn[across][2] * position[2]
        + shift_vec[across]
        for across in range(3)
    ]
    inverse = 1.0 / viewed[2]
    mean_x = focal_x * viewed[0] * inverse + camera[9]
    mean_y = focal_y * viewed[1] * inverse + camera[10]
    gauss_turn = rotation(raw[6], raw[7], raw[8], raw[9])
    stretch = [jnp.exp(raw[3 + column]) for column in range(3)]
    jac_xx = focal_x * inverse
    jac_xz = -focal_x * viewed[0] * inverse * inverse
    jac_yy = focal_y * inverse
    jac_yz = -focal_y * viewed[1] * inverse * inverse
    leading_x = [
        jac_xx * camera_turn[0][column] + jac_xz * camera_turn[2][column] for column in range(3)
    ]
    leading_y = [
        jac_yy * camera_turn[1][column] + jac_yz * camera_turn[2][column] for column in range(3)
    ]
    axes_x = [
        (
            leading_x[0] * gauss_turn[0][column]
            + leading_x[1] * gauss_turn[1][column]
            + leading_x[2] * gauss_turn[2][column]
        )
        * stretch[column]
        for column in range(3)
    ]
    axes_y = [
        (
            leading_y[0] * gauss_turn[0][column]
            + leading_y[1] * gauss_turn[1][column]
            + leading_y[2] * gauss_turn[2][column]
        )
        * stretch[column]
        for column in range(3)
    ]
    cov_xx = axes_x[0] * axes_x[0] + axes_x[1] * axes_x[1] + axes_x[2] * axes_x[2] + blur_add
    cov_xy = axes_x[0] * axes_y[0] + axes_x[1] * axes_y[1] + axes_x[2] * axes_y[2]
    cov_yy = axes_y[0] * axes_y[0] + axes_y[1] * axes_y[1] + axes_y[2] * axes_y[2] + blur_add
    determ = cov_xx * cov_yy - cov_xy * cov_xy
    opacity = 1.0 / (1.0 + jnp.exp(-raw[10]))
    camera_eye = [
        -(
            camera_turn[0][column] * shift_vec[0]
            + camera_turn[1][column] * shift_vec[1]
            + camera_turn[2][column] * shift_vec[2]
        )
        for column in range(3)
    ]
    offset = [position[column] - camera_eye[column] for column in range(3)]
    length = lax.rsqrt(offset[0] * offset[0] + offset[1] * offset[1] + offset[2] * offset[2])
    harmonic_terms = harmonics(offset[0] * length, offset[1] * length, offset[2] * length)
    colours = []
    for channel in range(3):
        total = 0.5 + jnp.zeros_like(opacity)
        for harmonic in range(16):
            total = total + raw[11 + 16 * channel + harmonic] * harmonic_terms[harmonic]
        colours.append(total)
    return [mean_x, mean_y, cov_yy / determ, -cov_xy / determ, cov_xx / determ, opacity] + colours


def three_pieces(value):
    high = value.astype(jnp.bfloat16)
    rest = value - high.astype(jnp.float32)
    middle = rest.astype(jnp.bfloat16)
    low = (rest - middle.astype(jnp.float32)).astype(jnp.bfloat16)
    return high, middle, low


def two_pieces(value):
    high = value.astype(jnp.bfloat16)
    return high, (value - high.astype(jnp.float32)).astype(jnp.bfloat16)


def matmul(left, right):
    return jnp.dot(left, right, preferred_element_type=jnp.float32)


def matmul_nt(left, right):
    return lax.dot_general(
        left, right, (((1,), (1,)), ((), ())), preferred_element_type=jnp.float32
    )


def visible_row(visible_ref):
    views = visible_ref.shape[0]
    return jnp.concatenate([visible_ref[view : view + 1, :] for view in range(views)], axis=1)


def column_hot(visible_ref, columns):
    ids = visible_row(visible_ref)
    place = lax.broadcasted_iota(jnp.int32, (columns, ids.shape[1]), 0)
    return jnp.where(place == ids, 1.0, 0.0).astype(jnp.bfloat16)


def camera_rows(cameras_ref, own_rows):
    views = cameras_ref.shape[0]
    lane = lax.broadcasted_iota(jnp.int32, (1, views * own_rows), 1)
    rows = []
    for entry in range(11):
        row = jnp.full(lane.shape, cameras_ref[0, entry], jnp.float32)
        for view in range(1, views):
            row = jnp.where(lane >= view * own_rows, cameras_ref[view, entry], row)
        rows.append(row)
    return rows


def down(row, lanes):
    spread_row = jnp.broadcast_to(row.astype(jnp.float32), (lanes, row.shape[1]))
    return jnp.transpose(spread_row)


def list_hot_down(lists, lanes):
    ids = down(lax.bitwise_and(lists, lanes - 1), lanes)
    lane = lax.broadcasted_iota(jnp.int32, ids.shape, 1).astype(jnp.float32)
    return jnp.where(ids == lane, 1.0, 0.0).astype(jnp.bfloat16)


def list_hot(lists, lanes):
    place = lax.broadcasted_iota(jnp.int32, (lanes, lists.shape[1]), 0)
    hot = jnp.where(place == lax.bitwise_and(lists, lanes - 1), 1.0, 0.0).astype(jnp.bfloat16)
    return hot, lax.shift_right_logical(lists, lanes.bit_length() - 1)


def step_kernel(
    views, tiles, params_hbm, visible_hbm, cameras_hbm, lists_hbm, counts_hbm, targets_hbm,
    grad_ref, seen_ref, image_ref,
    params_ref, visible_ref, cameras_ref, lists_ref, counts_ref, targets_ref, picked_ref, outgoing, everyone, hot_back, hots, hots_wide, rows, grads,
    weights, weight_parts, ratios, carried, held, given, landed, slopes_ref,
    load_sem, out_sem, out_recv, back_sem, back_recv
):
    my_view, my_tile = lax.axis_index("view"), lax.axis_index("tile")
    owners = views * tiles
    me = my_tile * views + my_view

    partners = []
    for step_view in range(views):
        view = lax.rem(my_view + step_view, views)
        for step_tile in range(tiles):
            if step_view or step_tile:
                tile = lax.rem(my_tile + step_tile, tiles)
                partners.append((tile * views + view, view, tile))
    pairs = (
        (visible_hbm, visible_ref), (cameras_hbm, cameras_ref), (params_hbm, params_ref),
        (lists_hbm, lists_ref), (counts_hbm, counts_ref), (targets_hbm, targets_ref),
    )
    loads = [
        pltpu.make_async_copy(source, held_at, load_sem.at[place])
        for place, (source, held_at) in enumerate(pairs)
    ]
    for load in loads:
        load.start()
    barrier = pltpu.get_barrier_semaphore()

    for _, view, tile in partners:
        pl.semaphore_signal(barrier, inc=1, device_id=(view, tile), device_id_type=MESH)

    width, columns = params_ref.shape
    own_rows = visible_ref.shape[1]
    wide = 2 * own_rows
    loads[0].wait()
    hot = column_hot(visible_ref, columns)
    loads[1].wait()
    cameras = camera_rows(cameras_ref, own_rows)
    loads[2].wait()
    padded = jnp.concatenate(
        [params_ref[...], jnp.zeros((64 - width, columns), jnp.float32)], axis=0
    )
    found = matmul(jnp.concatenate(three_pieces(padded), axis=0), hot)
    picked_ref[...] = found[0:64] + found[64:128] + found[128:192]
    raw = [picked_ref[row : row + 1, :] for row in range(width)]
    out = project(raw, cameras)
    lower = jnp.concatenate(out[0:4] + [out[8]], axis=0)
    upper = jnp.concatenate(out[4:8] + [jnp.zeros_like(out[8])], axis=0)
    for view in range(views):
        span = slice(view * own_rows, (view + 1) * own_rows)
        outgoing[view] = jnp.concatenate([lower[:, span], upper[:, span]], axis=1)

    def to_owner(source, landing, sends, receives, view, tile):
        return pltpu.make_async_remote_copy(
            src_ref=source, dst_ref=landing, send_sem=sends.at[0], recv_sem=receives.at[0],
            device_id=(view, tile), device_id_type=MESH,
        )

    everyone[me] = outgoing[my_view]
    pl.semaphore_wait(barrier, owners - 1)
    for _, view, tile in partners:
        to_owner(outgoing.at[view], everyone.at[me], out_sem, out_recv, view, tile).start()

    for load in loads[3:]:
        load.wait()
    per_device, entries = lists_ref.shape
    groups, groups_wide = [], []
    for tile in range(per_device):
        ids = lists_ref[tile : tile + 1, :]
        narrow, group = list_hot(ids, own_rows)
        hots[tile] = jnp.concatenate([narrow] * 4, axis=0)
        groups.append(jnp.broadcast_to(group, (SUBS, entries)))
        hots_wide[tile] = list_hot_down(ids, wide)
        group = lax.shift_right_logical(ids, wide.bit_length() - 1)
        groups_wide.append(jnp.broadcast_to(group, (SUBS, entries)))

    ids_down = down(visible_row(visible_ref), BLOCK)
    for start in range(0, columns, BLOCK):
        lane_at = lax.broadcasted_iota(jnp.int32, ids_down.shape, 1).astype(jnp.float32) + start
        hot_back[:, start : start + BLOCK] = jnp.where(ids_down == lane_at, 1.0, 0.0).astype(
            jnp.bfloat16
        )
    rest = pl.ds(0, owners - 1)
    _, next_view, next_tile = partners[0]
    all_rows = to_owner(
        everyone.at[rest], everyone.at[rest], out_sem, out_recv, next_view, next_tile
    )
    all_rows.wait_recv()

    batch = max(1, min(tiles, 32 // views))
    chunk = batch * views
    lane = lax.broadcasted_iota(jnp.int32, (chunk * (SUBS + 1), wide), 1)

    def gather(index, held_rows):
        source = everyone[pl.ds(index * chunk, chunk)]
        last = source[:, 4, :]
        source = jnp.concatenate([source, jnp.zeros((chunk, SUBS - PACK, wide), jnp.float32)], axis=1)
        turned = pltpu.roll(pltpu.roll(source, own_rows, 2), 4, 1)
        source = jnp.where(lax.broadcasted_iota(jnp.int32, source.shape, 1) < 4, source, turned)
        source = jnp.concatenate([source.reshape(chunk * SUBS, wide), last], axis=0)
        high, middle, low = [piece.astype(jnp.float32) for piece in three_pieces(source)]
        source = jnp.concatenate(
            [
                jnp.where(lane < own_rows, high, pltpu.roll(middle, own_rows, 1)),
                jnp.where(lane < own_rows, low, 0.0),
            ],
            axis=1,
        ).astype(jnp.bfloat16)
        new_rows = []
        for tile in range(per_device):
            located = matmul(source, hots[tile])
            first, second = held_rows[tile]
            for owner in range(chunk):
                mine = groups[tile] == index * chunk + owner
                first = first + jnp.where(mine, located[owner * SUBS : (owner + 1) * SUBS], 0.0)
            for start in range(0, chunk, SUBS):
                begin = chunk * SUBS + start
                number = lax.broadcasted_iota(jnp.int32, (SUBS, entries), 0) + (
                    index * chunk + start
                )
                second = second + jnp.where(
                    groups[tile] == number, located[begin : begin + SUBS], 0.0
                )
            new_rows.append((first, second))
        return tuple(new_rows)

    empty = jnp.zeros((SUBS, entries), jnp.float32)
    collected = lax.fori_loop(0, tiles // batch, gather, ((empty, empty),) * per_device)
    for tile in range(per_device):
        rows[tile, 0:SUBS, :] = collected[tile][0]
        rows[tile, SUBS : 2 * SUBS, :] = jnp.broadcast_to(
            jnp.sum(collected[tile][1], axis=0, keepdims=True), (SUBS, entries)
        )

    first_tile = my_tile * per_device
    half = SIDE // 2
    middles = []
    for tile in range(per_device):
        number = first_tile + tile
        middles.append(
            (
                (lax.rem(number, WIN_COLS) * SIDE + half).astype(jnp.float32),
                (lax.div(number, WIN_COLS) * SIDE + half).astype(jnp.float32),
            )
        )
    side_x = lax.broadcasted_iota(jnp.int32, (SIDE, BLOCK), 0).astype(jnp.float32) + (0.5 - half)
    spot = lax.bitwise_and(
        lax.broadcasted_iota(jnp.int32, (2 * BLOCK, 2 * BLOCK), 0), BLOCK - 1
    )
    lane_two = lax.broadcasted_iota(jnp.int32, (2 * BLOCK, 2 * BLOCK), 1)
    ahead = jnp.where((spot < lane_two) | (lane_two >= BLOCK), 1.0, 0.0).astype(jnp.bfloat16)
    behind = jnp.where((spot > lane_two) | (lane_two >= BLOCK), 1.0, 0.0)[0:BLOCK]
    behind = behind.astype(jnp.bfloat16)
    blocks = entries // BLOCK
    stride = 4 if blocks % 4 == 0 else 1

    carried[...] = jnp.zeros_like(carried)
    held[...] = jnp.zeros_like(held)

    def forward(block, _):
        start = pl.multiple_of(block * BLOCK, BLOCK)
        for tile in range(per_device):
            live = (block < counts_ref[0, tile]).astype(jnp.float32)
            low = rows[tile, 0:SUBS, pl.ds(start, BLOCK)]
            up = rows[tile, SUBS : 2 * SUBS, pl.ds(start, BLOCK)]
            mean_x = low[0:1] - middles[tile][0]
            mean_y = low[1:2] - middles[tile][1]
            form_a = -0.5 * low[2:3]
            form_b = -low[3:4]
            form_c = -0.5 * low[4:5]
            opacity = low[5:6] * live
            delta_x = side_x - mean_x
            square = form_a * delta_x * delta_x
            cross = form_b * delta_x
            pieces = []
            for line in range(SIDE):
                delta_y = (line + 0.5 - half) - mean_y
                pieces.append((cross + form_c * delta_y) * delta_y + square)
            alpha = opacity * jnp.exp(jnp.concatenate(pieces, axis=0))
            decay = jnp.log(1.0 - alpha)
            before = matmul(jnp.concatenate(two_pieces(decay), axis=1), ahead)
            past = carried[tile]
            weight = alpha * jnp.exp(before[:, 0:BLOCK] + past)
            carried[tile] = past + before[:, BLOCK:]
            ratios[tile, block] = alpha * jnp.exp(-decay)
            weights[tile, block] = weight
            parts = jnp.concatenate(two_pieces(weight), axis=1)
            weight_parts[tile, block] = parts[:, 0:BLOCK]
            colour = jnp.concatenate([low[6:8], up[0:1], jnp.zeros((5, BLOCK), jnp.float32)], axis=0)
            high = colour.astype(jnp.bfloat16).astype(jnp.float32)
            both = jnp.concatenate([high, colour - high], axis=0).astype(jnp.bfloat16)
            held[tile] += matmul_nt(parts, jnp.concatenate([both, both], axis=1))
        return 0

    def forward_pair(index, _):
        for part in range(stride):
            forward(index * stride + part, 0)
        return 0

    lax.fori_loop(0, blocks // stride, forward_pair, 0)

    slopes, slopes_wide = [], []
    for tile in range(per_device):
        drawn = jnp.transpose(
            jnp.concatenate(
                [held[tile], jnp.zeros((PIX, BLOCK - 2 * SUBS), jnp.float32)], axis=1
            )
        )
        drawn = drawn[0:3] + drawn[SUBS : SUBS + 3]
        image_ref[:, 0, tile * PIX : (tile + 1) * PIX] = drawn
        slope = 2.0 * (drawn - targets_ref[:, 0, tile * PIX : (tile + 1) * PIX])
        high = slope.astype(jnp.bfloat16).astype(jnp.float32)
        stack = jnp.concatenate(
            [high, slope - high, high, jnp.zeros((BLOCK - 9, PIX), jnp.float32)], axis=0
        )
        slopes.append(stack[0 : 2 * SUBS].astype(jnp.bfloat16))
        slopes_wide.append(jnp.transpose(stack).astype(jnp.bfloat16)[:, 0 : 2 * SUBS])

    pixel = lax.broadcasted_iota(jnp.int32, (2 * SUBS, PIX), 1)
    kind = lax.broadcasted_iota(jnp.int32, (2 * SUBS, PIX), 0)
    at_x = lax.bitwise_and(pixel, SIDE - 1).astype(jnp.float32) + (0.5 - half)
    at_y = lax.shift_right_logical(pixel, SIDE.bit_length() - 1).astype(jnp.float32) + (0.5 - half)
    power_x = jnp.where((kind == 1) | (kind == 4), at_x, jnp.where(kind == 3, at_x * at_x, 1.0))
    power_y = jnp.where((kind == 2) | (kind == 4), at_y, jnp.where(kind == 5, at_y * at_y, 1.0))
    basis = jnp.where(kind < 6, power_x * power_y, 0.0).astype(jnp.bfloat16)

    carried[...] = jnp.zeros_like(carried)

    def backward(index, _):
        block = blocks - 1 - index
        start = pl.multiple_of(block * BLOCK, BLOCK)
        for tile in range(per_device):
            low = rows[tile, 0:SUBS, pl.ds(start, BLOCK)]
            up = rows[tile, SUBS : 2 * SUBS, pl.ds(start, BLOCK)]
            colour = jnp.concatenate([low[6:8], up[0:1]], axis=0)
            high = colour.astype(jnp.bfloat16).astype(jnp.float32)
            both = jnp.concatenate(
                [high, high, colour - high, jnp.zeros((7, BLOCK), jnp.float32)], axis=0
            ).astype(jnp.bfloat16)
            pulled = matmul(slopes_wide[tile], both) * weights[tile, block]
            after = matmul(pulled.astype(jnp.bfloat16), behind)
            past = carried[tile]
            inner = pulled - (after[:, 0:BLOCK] + past) * ratios[tile, block]
            carried[tile] = past + after[:, BLOCK:]
            sums = matmul(basis, inner.astype(jnp.bfloat16))
            tint = matmul(slopes[tile], weight_parts[tile, block])
            tint = tint[0:3] + tint[3:6]
            mean_x = low[0:1] - middles[tile][0]
            mean_y = low[1:2] - middles[tile][1]
            form_a, form_b, form_c = low[2:3], low[3:4], low[4:5]
            whole, by_x, by_y = sums[0:1], sums[1:2], sums[2:3]
            sum_x = by_x - mean_x * whole
            sum_y = by_y - mean_y * whole
            sum_xx = sums[3:4] - 2.0 * mean_x * by_x + mean_x * mean_x * whole
            sum_xy = sums[4:5] - mean_x * by_y - mean_y * by_x + mean_x * mean_y * whole
            sum_yy = sums[5:6] - 2.0 * mean_y * by_y + mean_y * mean_y * whole
            grads[tile, 0:SUBS, pl.ds(start, BLOCK)] = jnp.concatenate(
                [
                    form_a * sum_x + form_b * sum_y,
                    form_b * sum_x + form_c * sum_y,
                    -0.5 * sum_xx,
                    -sum_xy,
                    -0.5 * sum_yy,
                    whole / low[5:6],
                    tint[0:2],
                ],
                axis=0,
            )
            grads[tile, SUBS : 2 * SUBS, pl.ds(start, BLOCK)] = jnp.broadcast_to(
                tint[2:3], (SUBS, BLOCK)
            )
        return 0

    def backward_pair(index, _):
        for part in range(stride):
            backward(index * stride + part, 0)
        return 0

    lax.fori_loop(0, blocks // stride, backward_pair, 0)

    pairs = chunk // 2
    lane_pair = lax.broadcasted_iota(jnp.int32, (pairs, SUBS, wide), 2)

    def scatter(index, _):
        total = jnp.zeros((2 * pairs * (SUBS + 1), wide), jnp.float32)
        for tile in range(per_device):
            main = grads[tile, 0:SUBS, :]
            last = grads[tile, SUBS : 2 * SUBS, :]
            parts = [[], [], [], []]
            main_high = main.astype(jnp.bfloat16).astype(jnp.float32)
            last_high = last.astype(jnp.bfloat16).astype(jnp.float32)
            for pair in range(pairs):
                mine = groups_wide[tile] == index * pairs + pair
                parts[0].append(jnp.where(mine, main_high, 0.0))
                parts[1].append(jnp.where(mine, main - main_high, 0.0))
            for start in range(0, pairs, SUBS):
                number = lax.broadcasted_iota(jnp.int32, (SUBS, entries), 0) + (
                    index * pairs + start
                )
                mine = groups_wide[tile] == number
                parts[2].append(jnp.where(mine, last_high, 0.0))
                parts[3].append(jnp.where(mine, last - last_high, 0.0))
            left = jnp.concatenate(parts[0] + parts[1] + parts[2] + parts[3], axis=0)
            total = total + matmul(left.astype(jnp.bfloat16), hots_wide[tile])
        size = pairs * SUBS
        main = (total[0:size] + total[size : 2 * size]).reshape(pairs, SUBS, wide)
        last = total[2 * size : 2 * size + pairs] + total[2 * size + pairs :]
        raised = pltpu.roll(main, 4, 1)
        row_pair = lax.broadcasted_iota(jnp.int32, main.shape, 1)
        last_turned = pltpu.roll(last, own_rows, 1)
        low_lane = lane_pair < own_rows
        even = jnp.where(
            row_pair < 4,
            jnp.where(low_lane, main, pltpu.roll(raised, own_rows, 2)),
            jnp.broadcast_to(last[:, None, :], main.shape),
        )
        odd = jnp.where(
            row_pair < 4,
            jnp.where(low_lane, pltpu.roll(main, own_rows, 2), raised),
            jnp.broadcast_to(last_turned[:, None, :], main.shape),
        )
        for pair in range(pairs):
            given[index * chunk + 2 * pair] = even[pair, 0:PACK]
            given[index * chunk + 2 * pair + 1] = odd[pair, 0:PACK]
        return 0

    lax.fori_loop(0, tiles // batch, scatter, 0)

    for other, view, tile in partners:
        to_owner(given.at[other], landed.at[me], back_sem, back_recv, view, tile).start()
    landed[me] = given[me]
    _, pullback = jax.vjp(lambda source: project(source, cameras), raw)
    all_back = to_owner(
        given.at[rest], landed.at[rest], back_sem, back_recv, next_view, next_tile
    )
    all_back.wait_recv()
    arrived = landed[pl.ds(0, views)]
    for tile in range(1, tiles):
        arrived = arrived + landed[pl.ds(tile * views, views)]
    lower = jnp.concatenate([arrived[view][:, 0:own_rows] for view in range(views)], axis=1)
    upper = jnp.concatenate([arrived[view][:, own_rows:] for view in range(views)], axis=1)
    (returned,) = pullback(
        [lower[row : row + 1] for row in range(4)]
        + [upper[row : row + 1] for row in range(4)]
        + [lower[4:5]]
    )
    slopes_ref[...] = jnp.ones_like(slopes_ref)
    for row in range(width):
        slopes_ref[row : row + 1, :] = returned[row]
    found = matmul(jnp.concatenate(three_pieces(slopes_ref[...]), axis=0), hot_back[...])
    found = found[0:64] + found[64:128] + found[128:192]
    grad_ref[...] = found[0:width]
    seen_ref[...] = found[width : width + 1]

    all_rows.wait_send()
    all_back.wait_send()


def update_kernel(
    params_ref, first_ref, second_ref, grad_ref, seen_ref, drawn_ref,
    new_params_ref, new_first_ref, new_second_ref, image_ref
):
    grad = grad_ref[...]
    seen = seen_ref[...] > 0.5
    first, second, params = first_ref[...], second_ref[...], params_ref[...]
    moved_first = beta_first * first + (1.0 - beta_first) * grad
    moved_second = beta_second * second + (1.0 - beta_second) * grad * grad
    moved_params = params - learn_rate * moved_first / (jnp.sqrt(moved_second) + adam_eps)
    new_first_ref[...] = jnp.where(seen, moved_first, first)
    new_second_ref[...] = jnp.where(seen, moved_second, second)
    new_params_ref[...] = jnp.where(seen, moved_params, params)
    image_ref[...] = drawn_ref[...]


def shards(views, tiles, params, first, second, visible, cameras, tile_lists, tile_blocks, targets):
    own_rows = visible.shape[1]
    per_device, entries = tile_lists.shape[1:]
    blocks = entries // BLOCK
    packet = (PACK, 2 * own_rows)
    f32 = jnp.float32
    dma = pltpu.SemaphoreType.DMA
    owners = views * tiles
    image_shape = jax.ShapeDtypeStruct((3, 1, per_device * PIX), f32)
    grad, seen, drawn = pl.pallas_call(
        functools.partial(step_kernel, views, tiles),
        out_shape=[
            jax.ShapeDtypeStruct(params.shape, f32),
            jax.ShapeDtypeStruct((1, params.shape[1]), f32),
            image_shape,
        ],
        in_specs=[ANY] * 6,
        out_specs=[VMEM, VMEM, VMEM],
        scratch_shapes=[
            pltpu.VMEM(params.shape, f32),
            pltpu.VMEM(visible.shape, jnp.int32),
            pltpu.SMEM(cameras.shape, f32),
            pltpu.VMEM((per_device, entries), jnp.int32),
            pltpu.SMEM(tile_blocks.shape, jnp.int32),
            pltpu.VMEM((3, 1, per_device * PIX), f32),
            pltpu.VMEM((64, views * own_rows), f32),
            pltpu.VMEM((views,) + packet, f32),
            pltpu.VMEM((owners,) + packet, f32),
            pltpu.VMEM((views * own_rows, params.shape[1]), jnp.bfloat16),
            pltpu.VMEM((per_device, 4 * own_rows, entries), jnp.bfloat16),
            pltpu.VMEM((per_device, entries, 2 * own_rows), jnp.bfloat16),
            pltpu.VMEM((per_device, 2 * SUBS, entries), f32),
            pltpu.VMEM((per_device, 2 * SUBS, entries), f32),
            pltpu.VMEM((per_device, blocks, PIX, BLOCK), f32),
            pltpu.VMEM((per_device, blocks, PIX, BLOCK), jnp.bfloat16),
            pltpu.VMEM((per_device, blocks, PIX, BLOCK), f32),
            pltpu.VMEM((per_device, PIX, BLOCK), f32),
            pltpu.VMEM((per_device, PIX, 2 * SUBS), f32),
            pltpu.VMEM((owners,) + packet, f32),
            pltpu.VMEM((owners,) + packet, f32),
            pltpu.VMEM((64, views * own_rows), f32),
            dma((6,)),
            dma((1,)), dma((1,)), dma((1,)), dma((1,)),
        ],
        compiler_params=pltpu.CompilerParams(
            collective_id=0, has_side_effects=True, vmem_limit_bytes=LIMIT
        ),
        name="render_step",
    )(params, visible, cameras, tile_lists[0], tile_blocks, jnp.transpose(targets, (1, 0, 2)))
    like = jax.ShapeDtypeStruct(params.shape, f32)
    new_params, new_first, new_second, rendered = pl.pallas_call(
        update_kernel,
        out_shape=[like, like, like, image_shape],
        in_specs=[VMEM] * 6,
        out_specs=[VMEM] * 4,
        compiler_params=pltpu.CompilerParams(vmem_limit_bytes=LIMIT),
        name="update",
    )(params, first, second, grad, seen, drawn)
    return (new_params, new_first, new_second, jnp.transpose(rendered, (1, 0, 2)))


def solution(mesh):
    in_specs = (
        P(None, ("view", "tile")),
        P(None, ("view", "tile")),
        P(None, ("view", "tile")),
        P(None, ("view", "tile")),
        P(),
        P("view", "tile", None),
        P("view", "tile"),
        P("view", None, "tile"),
    )
    out_specs = (
        P(None, ("view", "tile")),
        P(None, ("view", "tile")),
        P(None, ("view", "tile")),
        P("view", None, "tile"),
    )
    body = functools.partial(shards, mesh.shape["view"], mesh.shape["tile"])
    return jax.shard_map(body, mesh=mesh, in_specs=in_specs, out_specs=out_specs, check_vma=False)
```

```python
import functools

import jax
import jax.numpy as jnp
from jax import lax
from jax.experimental import pallas as pl
from jax.experimental.pallas import tpu as pltpu
from jax.sharding import PartitionSpec as P

SIDE = 16
PIX = 256
BLOCK = 128
WIN_COLS = 8
SUBS = 8
PACK = 5
MESH = pl.DeviceIdType.MESH
VMEM = pl.BlockSpec(memory_space=pltpu.VMEM)
ANY = pl.BlockSpec(memory_space=pl.ANY)
SMEM = pl.BlockSpec(memory_space=pltpu.SMEM)
LIMIT = 62 * 1024 * 1024


harm_zero = 0.28209479177387814
harm_one = 0.4886025119029199
harm_two = (
    1.0925484305920792,
    -1.0925484305920792,
    0.31539156525252005,
    -1.0925484305920792,
    0.5462742152960396,
)
harm_three = (
    -0.5900435899266435,
    2.890611442640554,
    -0.4570457994644658,
    0.3731763325901154,
    -0.4570457994644658,
    1.445305721320277,
    -0.5900435899266435,
)
learn_rate = 0.05
beta_first = 0.9
beta_second = 0.999
adam_eps = 1e-08
blur_add = 0.3


def rotation(real_part, axis_one, axis_two, axis_three):
    inverse = lax.rsqrt(
        real_part * real_part + axis_one * axis_one + axis_two * axis_two + axis_three * axis_three
    )
    real_unit = real_part * inverse
    unit_one = axis_one * inverse
    unit_two = axis_two * inverse
    unit_three = axis_three * inverse
    return (
        (
            1.0 - 2.0 * (unit_two * unit_two + unit_three * unit_three),
            2.0 * (unit_one * unit_two - real_unit * unit_three),
            2.0 * (unit_one * unit_three + real_unit * unit_two),
        ),
        (
            2.0 * (unit_one * unit_two + real_unit * unit_three),
            1.0 - 2.0 * (unit_one * unit_one + unit_three * unit_three),
            2.0 * (unit_two * unit_three - real_unit * unit_one),
        ),
        (
            2.0 * (unit_one * unit_three - real_unit * unit_two),
            2.0 * (unit_two * unit_three + real_unit * unit_one),
            1.0 - 2.0 * (unit_one * unit_one + unit_two * unit_two),
        ),
    )


def harmonics(first_dir, second_dir, third_dir):
    sq_first = first_dir * first_dir
    sq_second = second_dir * second_dir
    sq_third = third_dir * third_dir
    return [
        harm_zero,
        -harm_one * second_dir,
        harm_one * third_dir,
        -harm_one * first_dir,
        harm_two[0] * first_dir * second_dir,
        harm_two[1] * second_dir * third_dir,
        harm_two[2] * (2.0 * sq_third - sq_first - sq_second),
        harm_two[3] * first_dir * third_dir,
        harm_two[4] * (sq_first - sq_second),
        harm_three[0] * second_dir * (3.0 * sq_first - sq_second),
        harm_three[1] * first_dir * second_dir * third_dir,
        harm_three[2] * second_dir * (4.0 * sq_third - sq_first - sq_second),
        harm_three[3] * third_dir * (2.0 * sq_third - 3.0 * sq_first - 3.0 * sq_second),
        harm_three[4] * first_dir * (4.0 * sq_third - sq_first - sq_second),
        harm_three[5] * third_dir * (sq_first - sq_second),
        harm_three[6] * first_dir * (sq_first - 3.0 * sq_second),
    ]


def project(raw, camera):
    camera_turn = rotation(camera[0], camera[1], camera[2], camera[3])
    shift_vec = (camera[4], camera[5], camera[6])
    focal_x = camera[7]
    focal_y = camera[8]
    position = (raw[0], raw[1], raw[2])
    viewed = [
        camera_turn[across][0] * position[0]
        + camera_turn[across][1] * position[1]
        + camera_turn[across][2] * position[2]
        + shift_vec[across]
        for across in range(3)
    ]
    inverse = 1.0 / viewed[2]
    mean_x = focal_x * viewed[0] * inverse + camera[9]
    mean_y = focal_y * viewed[1] * inverse + camera[10]
    gauss_turn = rotation(raw[6], raw[7], raw[8], raw[9])
    stretch = [jnp.exp(raw[3 + column]) for column in range(3)]
    jac_xx = focal_x * inverse
    jac_xz = -focal_x * viewed[0] * inverse * inverse
    jac_yy = focal_y * inverse
    jac_yz = -focal_y * viewed[1] * inverse * inverse
    leading_x = [
        jac_xx * camera_turn[0][column] + jac_xz * camera_turn[2][column] for column in range(3)
    ]
    leading_y = [
        jac_yy * camera_turn[1][column] + jac_yz * camera_turn[2][column] for column in range(3)
    ]
    axes_x = [
        (
            leading_x[0] * gauss_turn[0][column]
            + leading_x[1] * gauss_turn[1][column]
            + leading_x[2] * gauss_turn[2][column]
        )
        * stretch[column]
        for column in range(3)
    ]
    axes_y = [
        (
            leading_y[0] * gauss_turn[0][column]
            + leading_y[1] * gauss_turn[1][column]
            + leading_y[2] * gauss_turn[2][column]
        )
        * stretch[column]
        for column in range(3)
    ]
    cov_xx = axes_x[0] * axes_x[0] + axes_x[1] * axes_x[1] + axes_x[2] * axes_x[2] + blur_add
    cov_xy = axes_x[0] * axes_y[0] + axes_x[1] * axes_y[1] + axes_x[2] * axes_y[2]
    cov_yy = axes_y[0] * axes_y[0] + axes_y[1] * axes_y[1] + axes_y[2] * axes_y[2] + blur_add
    determ = cov_xx * cov_yy - cov_xy * cov_xy
    opacity = 1.0 / (1.0 + jnp.exp(-raw[10]))
    camera_eye = [
        -(
            camera_turn[0][column] * shift_vec[0]
            + camera_turn[1][column] * shift_vec[1]
            + camera_turn[2][column] * shift_vec[2]
        )
        for column in range(3)
    ]
    offset = [position[column] - camera_eye[column] for column in range(3)]
    length = lax.rsqrt(offset[0] * offset[0] + offset[1] * offset[1] + offset[2] * offset[2])
    harmonic_terms = harmonics(offset[0] * length, offset[1] * length, offset[2] * length)
    colours = []
    for channel in range(3):
        total = 0.5 + jnp.zeros_like(opacity)
        for harmonic in range(16):
            total = total + raw[11 + 16 * channel + harmonic] * harmonic_terms[harmonic]
        colours.append(total)
    return [mean_x, mean_y, cov_yy / determ, -cov_xy / determ, cov_xx / determ, opacity] + colours


def three_pieces(value):
    high = value.astype(jnp.bfloat16)
    rest = value - high.astype(jnp.float32)
    middle = rest.astype(jnp.bfloat16)
    low = (rest - middle.astype(jnp.float32)).astype(jnp.bfloat16)
    return high, middle, low


def two_pieces(value):
    high = value.astype(jnp.bfloat16)
    return high, (value - high.astype(jnp.float32)).astype(jnp.bfloat16)


def matmul(left, right):
    return jnp.dot(left, right, preferred_element_type=jnp.float32)


def matmul_nt(left, right):
    return lax.dot_general(
        left, right, (((1,), (1,)), ((), ())), preferred_element_type=jnp.float32
    )


def visible_row(visible_ref):
    views = visible_ref.shape[0]
    return jnp.concatenate([visible_ref[view : view + 1, :] for view in range(views)], axis=1)


def column_hot(visible_ref, columns):
    ids = visible_row(visible_ref)
    place = lax.broadcasted_iota(jnp.int32, (columns, ids.shape[1]), 0)
    return jnp.where(place == ids, 1.0, 0.0).astype(jnp.bfloat16)


def camera_rows(cameras_ref, own_rows):
    views = cameras_ref.shape[0]
    shape = (views // 2, 2 * own_rows)
    number = 2 * lax.broadcasted_iota(jnp.int32, shape, 0) + jnp.where(
        lax.broadcasted_iota(jnp.int32, shape, 1) >= own_rows, 1, 0
    )
    rows = []
    for entry in range(11):
        row = jnp.full(shape, cameras_ref[0, entry], jnp.float32)
        for view in range(1, views):
            row = jnp.where(number >= view, cameras_ref[view, entry], row)
        rows.append(row)
    return rows


def down(row, lanes):
    spread_row = jnp.broadcast_to(row.astype(jnp.float32), (lanes, row.shape[1]))
    return jnp.transpose(spread_row)


def list_hot_down(lists, lanes):
    ids = down(lax.bitwise_and(lists, lanes - 1), lanes)
    lane = lax.broadcasted_iota(jnp.int32, ids.shape, 1).astype(jnp.float32)
    return jnp.where(ids == lane, 1.0, 0.0).astype(jnp.bfloat16)


def list_hot(lists, lanes):
    place = lax.broadcasted_iota(jnp.int32, (lanes, lists.shape[1]), 0)
    hot = jnp.where(place == lax.bitwise_and(lists, lanes - 1), 1.0, 0.0).astype(jnp.bfloat16)
    return hot, lax.shift_right_logical(lists, lanes.bit_length() - 1)


def step_kernel(
    views, tiles, params_hbm, visible_hbm, cameras_hbm, lists_hbm, counts_hbm, targets_hbm,
    grad_ref, seen_ref, image_ref,
    params_ref, visible_ref, cameras_ref, lists_ref, counts_ref, targets_ref, picked_ref, outgoing, everyone, hot_back, hots, hots_wide, rows, grads,
    weights, weight_parts, ratios, carried, held, given, landed, slopes_ref, folded,
    load_sem, out_sem, out_recv, back_sem, back_recv
):
    my_view, my_tile = lax.axis_index("view"), lax.axis_index("tile")
    owners = views * tiles
    me = my_tile * views + my_view

    partners = []
    for step_view in range(views):
        view = lax.rem(my_view + step_view, views)
        for step_tile in range(tiles):
            if step_view or step_tile:
                tile = lax.rem(my_tile + step_tile, tiles)
                partners.append((tile * views + view, view, tile))
    pairs = (
        (visible_hbm, visible_ref), (cameras_hbm, cameras_ref), (params_hbm, params_ref),
        (lists_hbm, lists_ref), (counts_hbm, counts_ref), (targets_hbm, targets_ref),
    )
    loads = [
        pltpu.make_async_copy(source, held_at, load_sem.at[place])
        for place, (source, held_at) in enumerate(pairs)
    ]
    for load in loads:
        load.start()
    barrier = pltpu.get_barrier_semaphore()

    for _, view, tile in partners:
        pl.semaphore_signal(barrier, inc=1, device_id=(view, tile), device_id_type=MESH)

    width, columns = params_ref.shape
    own_rows = visible_ref.shape[1]
    wide = 2 * own_rows
    loads[0].wait()
    hot = column_hot(visible_ref, columns)
    loads[1].wait()
    cameras = camera_rows(cameras_ref, own_rows)
    loads[2].wait()
    padded = jnp.concatenate(
        [params_ref[...], jnp.zeros((64 - width, columns), jnp.float32)], axis=0
    )
    found = matmul(jnp.concatenate(three_pieces(padded), axis=0), hot)
    found = found[0:64] + found[64:128] + found[128:192]
    folds = views // 2
    for fold in range(folds):
        picked_ref[fold * 64 : (fold + 1) * 64, :] = found[:, fold * wide : (fold + 1) * wide]
    raw = [picked_ref[pl.ds(row, folds, stride=64), :] for row in range(width)]
    out = project(raw, cameras)
    for row in range(9):
        folded[pl.ds(row, folds, stride=2 * SUBS), :] = out[row]
    low_lane = lax.broadcasted_iota(jnp.int32, (4, wide), 1) < own_rows
    for fold in range(folds):
        first = folded[fold * 2 * SUBS : fold * 2 * SUBS + 4, :]
        second = folded[fold * 2 * SUBS + 4 : fold * 2 * SUBS + 8, :]
        last = folded[fold * 2 * SUBS + 8 : fold * 2 * SUBS + 9, :]
        outgoing[2 * fold, 0:4] = jnp.where(low_lane, first, pltpu.roll(second, own_rows, 1))
        outgoing[2 * fold, 4:5] = last
        outgoing[2 * fold + 1, 0:4] = jnp.where(low_lane, pltpu.roll(first, own_rows, 1), second)
        outgoing[2 * fold + 1, 4:5] = pltpu.roll(last, own_rows, 1)

    def to_owner(source, landing, sends, receives, view, tile):
        return pltpu.make_async_remote_copy(
            src_ref=source, dst_ref=landing, send_sem=sends.at[0], recv_sem=receives.at[0],
            device_id=(view, tile), device_id_type=MESH,
        )

    everyone[me] = outgoing[my_view]
    pl.semaphore_wait(barrier, owners - 1)
    for _, view, tile in partners:
        to_owner(outgoing.at[view], everyone.at[me], out_sem, out_recv, view, tile).start()

    for load in loads[3:]:
        load.wait()
    per_device, entries = lists_ref.shape
    groups, groups_wide = [], []
    for tile in range(per_device):
        ids = lists_ref[tile : tile + 1, :]
        narrow, group = list_hot(ids, own_rows)
        hots[tile] = jnp.concatenate([narrow] * 4, axis=0)
        groups.append(jnp.broadcast_to(group, (SUBS, entries)))
        hots_wide[tile] = list_hot_down(ids, wide)
        group = lax.shift_right_logical(ids, wide.bit_length() - 1)
        groups_wide.append(jnp.broadcast_to(group, (SUBS, entries)))

    ids_down = down(visible_row(visible_ref), BLOCK)
    for start in range(0, columns, BLOCK):
        lane_at = lax.broadcasted_iota(jnp.int32, ids_down.shape, 1).astype(jnp.float32) + start
        hot_back[:, start : start + BLOCK] = jnp.where(ids_down == lane_at, 1.0, 0.0).astype(
            jnp.bfloat16
        )
    rest = pl.ds(0, owners - 1)
    _, next_view, next_tile = partners[0]
    all_rows = to_owner(
        everyone.at[rest], everyone.at[rest], out_sem, out_recv, next_view, next_tile
    )
    all_rows.wait_recv()

    batch = max(1, min(tiles, 32 // views))
    chunk = batch * views
    lane = lax.broadcasted_iota(jnp.int32, (chunk * (SUBS + 1), wide), 1)

    def gather(index, held_rows):
        source = everyone[pl.ds(index * chunk, chunk)]
        last = source[:, 4, :]
        source = jnp.concatenate([source, jnp.zeros((chunk, SUBS - PACK, wide), jnp.float32)], axis=1)
        turned = pltpu.roll(pltpu.roll(source, own_rows, 2), 4, 1)
        source = jnp.where(lax.broadcasted_iota(jnp.int32, source.shape, 1) < 4, source, turned)
        source = jnp.concatenate([source.reshape(chunk * SUBS, wide), last], axis=0)
        high, middle, low = [piece.astype(jnp.float32) for piece in three_pieces(source)]
        source = jnp.concatenate(
            [
                jnp.where(lane < own_rows, high, pltpu.roll(middle, own_rows, 1)),
                jnp.where(lane < own_rows, low, 0.0),
            ],
            axis=1,
        ).astype(jnp.bfloat16)
        new_rows = []
        for tile in range(per_device):
            located = matmul(source, hots[tile])
            first, second = held_rows[tile]
            for owner in range(chunk):
                mine = groups[tile] == index * chunk + owner
                first = first + jnp.where(mine, located[owner * SUBS : (owner + 1) * SUBS], 0.0)
            for start in range(0, chunk, SUBS):
                begin = chunk * SUBS + start
                number = lax.broadcasted_iota(jnp.int32, (SUBS, entries), 0) + (
                    index * chunk + start
                )
                second = second + jnp.where(
                    groups[tile] == number, located[begin : begin + SUBS], 0.0
                )
            new_rows.append((first, second))
        return tuple(new_rows)

    empty = jnp.zeros((SUBS, entries), jnp.float32)
    collected = lax.fori_loop(0, tiles // batch, gather, ((empty, empty),) * per_device)
    for tile in range(per_device):
        rows[tile, 0:SUBS, :] = collected[tile][0]
        rows[tile, SUBS : 2 * SUBS, :] = jnp.broadcast_to(
            jnp.sum(collected[tile][1], axis=0, keepdims=True), (SUBS, entries)
        )

    first_tile = my_tile * per_device
    half = SIDE // 2
    middles = []
    for tile in range(per_device):
        number = first_tile + tile
        middles.append(
            (
                (lax.rem(number, WIN_COLS) * SIDE + half).astype(jnp.float32),
                (lax.div(number, WIN_COLS) * SIDE + half).astype(jnp.float32),
            )
        )
    side_x = lax.broadcasted_iota(jnp.int32, (SIDE, BLOCK), 0).astype(jnp.float32) + (0.5 - half)
    spot = lax.bitwise_and(
        lax.broadcasted_iota(jnp.int32, (2 * BLOCK, 2 * BLOCK), 0), BLOCK - 1
    )
    lane_two = lax.broadcasted_iota(jnp.int32, (2 * BLOCK, 2 * BLOCK), 1)
    ahead = jnp.where((spot < lane_two) | (lane_two >= BLOCK), 1.0, 0.0).astype(jnp.bfloat16)
    behind = jnp.where((spot > lane_two) | (lane_two >= BLOCK), 1.0, 0.0)[0:BLOCK]
    behind = behind.astype(jnp.bfloat16)
    blocks = entries // BLOCK
    stride = 4 if blocks % 4 == 0 else 1

    carried[...] = jnp.zeros_like(carried)
    held[...] = jnp.zeros_like(held)

    def forward(block, _):
        start = pl.multiple_of(block * BLOCK, BLOCK)
        for tile in range(per_device):
            live = (block < counts_ref[0, tile]).astype(jnp.float32)
            low = rows[tile, 0:SUBS, pl.ds(start, BLOCK)]
            up = rows[tile, SUBS : 2 * SUBS, pl.ds(start, BLOCK)]
            mean_x = low[0:1] - middles[tile][0]
            mean_y = low[1:2] - middles[tile][1]
            form_a = -0.5 * low[2:3]
            form_b = -low[3:4]
            form_c = -0.5 * low[4:5]
            opacity = low[5:6] * live
            delta_x = side_x - mean_x
            square = form_a * delta_x * delta_x
            cross = form_b * delta_x
            pieces = []
            for line in range(SIDE):
                delta_y = (line + 0.5 - half) - mean_y
                pieces.append((cross + form_c * delta_y) * delta_y + square)
            alpha = opacity * jnp.exp(jnp.concatenate(pieces, axis=0))
            decay = jnp.log(1.0 - alpha)
            before = matmul(jnp.concatenate(two_pieces(decay), axis=1), ahead)
            past = carried[tile]
            weight = alpha * jnp.exp(before[:, 0:BLOCK] + past)
            carried[tile] = past + before[:, BLOCK:]
            ratios[tile, block] = alpha * jnp.exp(-decay)
            weights[tile, block] = weight
            parts = jnp.concatenate(two_pieces(weight), axis=1)
            weight_parts[tile, block] = parts[:, 0:BLOCK]
            colour = jnp.concatenate([low[6:8], up[0:1], jnp.zeros((5, BLOCK), jnp.float32)], axis=0)
            high = colour.astype(jnp.bfloat16).astype(jnp.float32)
            both = jnp.concatenate([high, colour - high], axis=0).astype(jnp.bfloat16)
            held[tile] += matmul_nt(parts, jnp.concatenate([both, both], axis=1))
        return 0

    def forward_pair(index, _):
        for part in range(stride):
            forward(index * stride + part, 0)
        return 0

    lax.fori_loop(0, blocks // stride, forward_pair, 0)

    slopes, slopes_wide = [], []
    for tile in range(per_device):
        drawn = jnp.transpose(
            jnp.concatenate(
                [held[tile], jnp.zeros((PIX, BLOCK - 2 * SUBS), jnp.float32)], axis=1
            )
        )
        drawn = drawn[0:3] + drawn[SUBS : SUBS + 3]
        image_ref[:, 0, tile * PIX : (tile + 1) * PIX] = drawn
        slope = 2.0 * (drawn - targets_ref[:, 0, tile * PIX : (tile + 1) * PIX])
        high = slope.astype(jnp.bfloat16).astype(jnp.float32)
        stack = jnp.concatenate(
            [high, slope - high, high, jnp.zeros((BLOCK - 9, PIX), jnp.float32)], axis=0
        )
        slopes.append(stack[0 : 2 * SUBS].astype(jnp.bfloat16))
        slopes_wide.append(jnp.transpose(stack).astype(jnp.bfloat16)[:, 0 : 2 * SUBS])

    pixel = lax.broadcasted_iota(jnp.int32, (2 * SUBS, PIX), 1)
    kind = lax.broadcasted_iota(jnp.int32, (2 * SUBS, PIX), 0)
    at_x = lax.bitwise_and(pixel, SIDE - 1).astype(jnp.float32) + (0.5 - half)
    at_y = lax.shift_right_logical(pixel, SIDE.bit_length() - 1).astype(jnp.float32) + (0.5 - half)
    power_x = jnp.where((kind == 1) | (kind == 4), at_x, jnp.where(kind == 3, at_x * at_x, 1.0))
    power_y = jnp.where((kind == 2) | (kind == 4), at_y, jnp.where(kind == 5, at_y * at_y, 1.0))
    basis = jnp.where(kind < 6, power_x * power_y, 0.0).astype(jnp.bfloat16)

    carried[...] = jnp.zeros_like(carried)

    def backward(index, _):
        block = blocks - 1 - index
        start = pl.multiple_of(block * BLOCK, BLOCK)
        for tile in range(per_device):
            low = rows[tile, 0:SUBS, pl.ds(start, BLOCK)]
            up = rows[tile, SUBS : 2 * SUBS, pl.ds(start, BLOCK)]
            colour = jnp.concatenate([low[6:8], up[0:1]], axis=0)
            high = colour.astype(jnp.bfloat16).astype(jnp.float32)
            both = jnp.concatenate(
                [high, high, colour - high, jnp.zeros((7, BLOCK), jnp.float32)], axis=0
            ).astype(jnp.bfloat16)
            pulled = matmul(slopes_wide[tile], both) * weights[tile, block]
            after = matmul(pulled.astype(jnp.bfloat16), behind)
            past = carried[tile]
            inner = pulled - (after[:, 0:BLOCK] + past) * ratios[tile, block]
            carried[tile] = past + after[:, BLOCK:]
            sums = matmul(basis, inner.astype(jnp.bfloat16))
            tint = matmul(slopes[tile], weight_parts[tile, block])
            tint = tint[0:3] + tint[3:6]
            mean_x = low[0:1] - middles[tile][0]
            mean_y = low[1:2] - middles[tile][1]
            form_a, form_b, form_c = low[2:3], low[3:4], low[4:5]
            whole, by_x, by_y = sums[0:1], sums[1:2], sums[2:3]
            sum_x = by_x - mean_x * whole
            sum_y = by_y - mean_y * whole
            sum_xx = sums[3:4] - 2.0 * mean_x * by_x + mean_x * mean_x * whole
            sum_xy = sums[4:5] - mean_x * by_y - mean_y * by_x + mean_x * mean_y * whole
            sum_yy = sums[5:6] - 2.0 * mean_y * by_y + mean_y * mean_y * whole
            grads[tile, 0:SUBS, pl.ds(start, BLOCK)] = jnp.concatenate(
                [
                    form_a * sum_x + form_b * sum_y,
                    form_b * sum_x + form_c * sum_y,
                    -0.5 * sum_xx,
                    -sum_xy,
                    -0.5 * sum_yy,
                    whole / low[5:6],
                    tint[0:2],
                ],
                axis=0,
            )
            grads[tile, SUBS : 2 * SUBS, pl.ds(start, BLOCK)] = jnp.broadcast_to(
                tint[2:3], (SUBS, BLOCK)
            )
        return 0

    def backward_pair(index, _):
        for part in range(stride):
            backward(index * stride + part, 0)
        return 0

    lax.fori_loop(0, blocks // stride, backward_pair, 0)

    pairs = chunk // 2
    lane_pair = lax.broadcasted_iota(jnp.int32, (pairs, SUBS, wide), 2)

    def scatter(index, _):
        total = jnp.zeros((2 * pairs * (SUBS + 1), wide), jnp.float32)
        for tile in range(per_device):
            main = grads[tile, 0:SUBS, :]
            last = grads[tile, SUBS : 2 * SUBS, :]
            parts = [[], [], [], []]
            main_high = main.astype(jnp.bfloat16).astype(jnp.float32)
            last_high = last.astype(jnp.bfloat16).astype(jnp.float32)
            for pair in range(pairs):
                mine = groups_wide[tile] == index * pairs + pair
                parts[0].append(jnp.where(mine, main_high, 0.0))
                parts[1].append(jnp.where(mine, main - main_high, 0.0))
            for start in range(0, pairs, SUBS):
                number = lax.broadcasted_iota(jnp.int32, (SUBS, entries), 0) + (
                    index * pairs + start
                )
                mine = groups_wide[tile] == number
                parts[2].append(jnp.where(mine, last_high, 0.0))
                parts[3].append(jnp.where(mine, last - last_high, 0.0))
            left = jnp.concatenate(parts[0] + parts[1] + parts[2] + parts[3], axis=0)
            total = total + matmul(left.astype(jnp.bfloat16), hots_wide[tile])
        size = pairs * SUBS
        main = (total[0:size] + total[size : 2 * size]).reshape(pairs, SUBS, wide)
        last = total[2 * size : 2 * size + pairs] + total[2 * size + pairs :]
        raised = pltpu.roll(main, 4, 1)
        row_pair = lax.broadcasted_iota(jnp.int32, main.shape, 1)
        last_turned = pltpu.roll(last, own_rows, 1)
        low_pair = lane_pair < own_rows
        even = jnp.where(
            row_pair < 4,
            jnp.where(low_pair, main, pltpu.roll(raised, own_rows, 2)),
            jnp.broadcast_to(last[:, None, :], main.shape),
        )
        odd = jnp.where(
            row_pair < 4,
            jnp.where(low_pair, pltpu.roll(main, own_rows, 2), raised),
            jnp.broadcast_to(last_turned[:, None, :], main.shape),
        )
        for pair in range(pairs):
            given[index * chunk + 2 * pair] = even[pair, 0:PACK]
            given[index * chunk + 2 * pair + 1] = odd[pair, 0:PACK]
        return 0

    lax.fori_loop(0, tiles // batch, scatter, 0)

    for other, view, tile in partners:
        to_owner(given.at[other], landed.at[me], back_sem, back_recv, view, tile).start()
    landed[me] = given[me]
    _, pullback = jax.vjp(lambda source: project(source, cameras), raw)
    all_back = to_owner(
        given.at[rest], landed.at[rest], back_sem, back_recv, next_view, next_tile
    )
    all_back.wait_recv()
    arrived = landed[pl.ds(0, views)]
    for tile in range(1, tiles):
        arrived = arrived + landed[pl.ds(tile * views, views)]
    for fold in range(folds):
        even, odd = arrived[2 * fold], arrived[2 * fold + 1]
        odd_turned = pltpu.roll(odd, own_rows, 1)
        even_turned = pltpu.roll(even, own_rows, 1)
        begin = fold * 2 * SUBS
        folded[begin : begin + 4, :] = jnp.where(low_lane, even[0:4], odd_turned[0:4])
        folded[begin + 4 : begin + 8, :] = jnp.where(low_lane, even_turned[0:4], odd[0:4])
        folded[begin + 8 : begin + 9, :] = jnp.where(low_lane[0:1], even[4:5], odd_turned[4:5])
    (returned,) = pullback([folded[pl.ds(row, folds, stride=2 * SUBS), :] for row in range(9)])
    slopes_ref[...] = jnp.ones_like(slopes_ref)
    for row in range(width):
        slopes_ref[pl.ds(row, folds, stride=64), :] = returned[row]
    slopes = jnp.concatenate(
        [slopes_ref[fold * 64 : (fold + 1) * 64, :] for fold in range(folds)], axis=1
    )
    found = matmul(jnp.concatenate(two_pieces(slopes), axis=0), hot_back[...])
    found = found[0:64] + found[64:128]
    grad_ref[...] = found[0:width]
    seen_ref[...] = found[width : width + 1]

    all_rows.wait_send()
    all_back.wait_send()


def update_kernel(
    params_ref, first_ref, second_ref, grad_ref, seen_ref, drawn_ref,
    new_params_ref, new_first_ref, new_second_ref, image_ref
):
    grad = grad_ref[...]
    seen = seen_ref[...] > 0.5
    first, second, params = first_ref[...], second_ref[...], params_ref[...]
    moved_first = beta_first * first + (1.0 - beta_first) * grad
    moved_second = beta_second * second + (1.0 - beta_second) * grad * grad
    moved_params = params - learn_rate * moved_first / (jnp.sqrt(moved_second) + adam_eps)
    new_first_ref[...] = jnp.where(seen, moved_first, first)
    new_second_ref[...] = jnp.where(seen, moved_second, second)
    new_params_ref[...] = jnp.where(seen, moved_params, params)
    image_ref[...] = drawn_ref[...]


def shards(views, tiles, params, first, second, visible, cameras, tile_lists, tile_blocks, targets):
    own_rows = visible.shape[1]
    per_device, entries = tile_lists.shape[1:]
    blocks = entries // BLOCK
    packet = (PACK, 2 * own_rows)
    f32 = jnp.float32
    dma = pltpu.SemaphoreType.DMA
    owners = views * tiles
    image_shape = jax.ShapeDtypeStruct((3, 1, per_device * PIX), f32)
    grad, seen, drawn = pl.pallas_call(
        functools.partial(step_kernel, views, tiles),
        out_shape=[
            jax.ShapeDtypeStruct(params.shape, f32),
            jax.ShapeDtypeStruct((1, params.shape[1]), f32),
            image_shape,
        ],
        in_specs=[ANY] * 6,
        out_specs=[VMEM, VMEM, VMEM],
        scratch_shapes=[
            pltpu.VMEM(params.shape, f32),
            pltpu.VMEM(visible.shape, jnp.int32),
            pltpu.SMEM(cameras.shape, f32),
            pltpu.VMEM((per_device, entries), jnp.int32),
            pltpu.SMEM(tile_blocks.shape, jnp.int32),
            pltpu.VMEM((3, 1, per_device * PIX), f32),
            pltpu.VMEM((64 * views // 2, 2 * own_rows), f32),
            pltpu.VMEM((views,) + packet, f32),
            pltpu.VMEM((owners,) + packet, f32),
            pltpu.VMEM((views * own_rows, params.shape[1]), jnp.bfloat16),
            pltpu.VMEM((per_device, 4 * own_rows, entries), jnp.bfloat16),
            pltpu.VMEM((per_device, entries, 2 * own_rows), jnp.bfloat16),
            pltpu.VMEM((per_device, 2 * SUBS, entries), f32),
            pltpu.VMEM((per_device, 2 * SUBS, entries), f32),
            pltpu.VMEM((per_device, blocks, PIX, BLOCK), f32),
            pltpu.VMEM((per_device, blocks, PIX, BLOCK), jnp.bfloat16),
            pltpu.VMEM((per_device, blocks, PIX, BLOCK), f32),
            pltpu.VMEM((per_device, PIX, BLOCK), f32),
            pltpu.VMEM((per_device, PIX, 2 * SUBS), f32),
            pltpu.VMEM((owners,) + packet, f32),
            pltpu.VMEM((owners,) + packet, f32),
            pltpu.VMEM((64 * views // 2, 2 * own_rows), f32),
            pltpu.VMEM((SUBS * views, 2 * own_rows), f32),
            dma((6,)),
            dma((1,)), dma((1,)), dma((1,)), dma((1,)),
        ],
        compiler_params=pltpu.CompilerParams(
            collective_id=0, has_side_effects=True, vmem_limit_bytes=LIMIT
        ),
        name="render_step",
    )(params, visible, cameras, tile_lists[0], tile_blocks, jnp.transpose(targets, (1, 0, 2)))
    like = jax.ShapeDtypeStruct(params.shape, f32)
    new_params, new_first, new_second, rendered = pl.pallas_call(
        update_kernel,
        out_shape=[like, like, like, image_shape],
        in_specs=[VMEM] * 6,
        out_specs=[VMEM] * 4,
        compiler_params=pltpu.CompilerParams(vmem_limit_bytes=LIMIT),
        name="update",
    )(params, first, second, grad, seen, drawn)
    return (new_params, new_first, new_second, jnp.transpose(rendered, (1, 0, 2)))


def solution(mesh):
    in_specs = (
        P(None, ("view", "tile")),
        P(None, ("view", "tile")),
        P(None, ("view", "tile")),
        P(None, ("view", "tile")),
        P(),
        P("view", "tile", None),
        P("view", "tile"),
        P("view", None, "tile"),
    )
    out_specs = (
        P(None, ("view", "tile")),
        P(None, ("view", "tile")),
        P(None, ("view", "tile")),
        P("view", None, "tile"),
    )
    body = functools.partial(shards, mesh.shape["view"], mesh.shape["tile"])
    return jax.shard_map(body, mesh=mesh, in_specs=in_specs, out_specs=out_specs, check_vma=False)
```

```python
import functools

import jax
import jax.numpy as jnp
from jax import lax
from jax.experimental import pallas as pl
from jax.experimental.pallas import tpu as pltpu
from jax.sharding import PartitionSpec as P

SIDE = 16
PIX = 256
BLOCK = 128
WIN_COLS = 8
SUBS = 8
PACK = 5
MESH = pl.DeviceIdType.MESH
VMEM = pl.BlockSpec(memory_space=pltpu.VMEM)
ANY = pl.BlockSpec(memory_space=pl.ANY)
SMEM = pl.BlockSpec(memory_space=pltpu.SMEM)
LIMIT = 62 * 1024 * 1024


harm_zero = 0.28209479177387814
harm_one = 0.4886025119029199
harm_two = (
    1.0925484305920792,
    -1.0925484305920792,
    0.31539156525252005,
    -1.0925484305920792,
    0.5462742152960396,
)
harm_three = (
    -0.5900435899266435,
    2.890611442640554,
    -0.4570457994644658,
    0.3731763325901154,
    -0.4570457994644658,
    1.445305721320277,
    -0.5900435899266435,
)
learn_rate = 0.05
beta_first = 0.9
beta_second = 0.999
adam_eps = 1e-08
blur_add = 0.3


def rotation(real_part, axis_one, axis_two, axis_three):
    inverse = lax.rsqrt(
        real_part * real_part + axis_one * axis_one + axis_two * axis_two + axis_three * axis_three
    )
    real_unit = real_part * inverse
    unit_one = axis_one * inverse
    unit_two = axis_two * inverse
    unit_three = axis_three * inverse
    return (
        (
            1.0 - 2.0 * (unit_two * unit_two + unit_three * unit_three),
            2.0 * (unit_one * unit_two - real_unit * unit_three),
            2.0 * (unit_one * unit_three + real_unit * unit_two),
        ),
        (
            2.0 * (unit_one * unit_two + real_unit * unit_three),
            1.0 - 2.0 * (unit_one * unit_one + unit_three * unit_three),
            2.0 * (unit_two * unit_three - real_unit * unit_one),
        ),
        (
            2.0 * (unit_one * unit_three - real_unit * unit_two),
            2.0 * (unit_two * unit_three + real_unit * unit_one),
            1.0 - 2.0 * (unit_one * unit_one + unit_two * unit_two),
        ),
    )


def harmonics(first_dir, second_dir, third_dir):
    sq_first = first_dir * first_dir
    sq_second = second_dir * second_dir
    sq_third = third_dir * third_dir
    return [
        harm_zero,
        -harm_one * second_dir,
        harm_one * third_dir,
        -harm_one * first_dir,
        harm_two[0] * first_dir * second_dir,
        harm_two[1] * second_dir * third_dir,
        harm_two[2] * (2.0 * sq_third - sq_first - sq_second),
        harm_two[3] * first_dir * third_dir,
        harm_two[4] * (sq_first - sq_second),
        harm_three[0] * second_dir * (3.0 * sq_first - sq_second),
        harm_three[1] * first_dir * second_dir * third_dir,
        harm_three[2] * second_dir * (4.0 * sq_third - sq_first - sq_second),
        harm_three[3] * third_dir * (2.0 * sq_third - 3.0 * sq_first - 3.0 * sq_second),
        harm_three[4] * first_dir * (4.0 * sq_third - sq_first - sq_second),
        harm_three[5] * third_dir * (sq_first - sq_second),
        harm_three[6] * first_dir * (sq_first - 3.0 * sq_second),
    ]


def project(raw, camera):
    camera_turn = rotation(camera[0], camera[1], camera[2], camera[3])
    shift_vec = (camera[4], camera[5], camera[6])
    focal_x = camera[7]
    focal_y = camera[8]
    position = (raw[0], raw[1], raw[2])
    viewed = [
        camera_turn[across][0] * position[0]
        + camera_turn[across][1] * position[1]
        + camera_turn[across][2] * position[2]
        + shift_vec[across]
        for across in range(3)
    ]
    inverse = 1.0 / viewed[2]
    mean_x = focal_x * viewed[0] * inverse + camera[9]
    mean_y = focal_y * viewed[1] * inverse + camera[10]
    gauss_turn = rotation(raw[6], raw[7], raw[8], raw[9])
    stretch = [jnp.exp(raw[3 + column]) for column in range(3)]
    jac_xx = focal_x * inverse
    jac_xz = -focal_x * viewed[0] * inverse * inverse
    jac_yy = focal_y * inverse
    jac_yz = -focal_y * viewed[1] * inverse * inverse
    leading_x = [
        jac_xx * camera_turn[0][column] + jac_xz * camera_turn[2][column] for column in range(3)
    ]
    leading_y = [
        jac_yy * camera_turn[1][column] + jac_yz * camera_turn[2][column] for column in range(3)
    ]
    axes_x = [
        (
            leading_x[0] * gauss_turn[0][column]
            + leading_x[1] * gauss_turn[1][column]
            + leading_x[2] * gauss_turn[2][column]
        )
        * stretch[column]
        for column in range(3)
    ]
    axes_y = [
        (
            leading_y[0] * gauss_turn[0][column]
            + leading_y[1] * gauss_turn[1][column]
            + leading_y[2] * gauss_turn[2][column]
        )
        * stretch[column]
        for column in range(3)
    ]
    cov_xx = axes_x[0] * axes_x[0] + axes_x[1] * axes_x[1] + axes_x[2] * axes_x[2] + blur_add
    cov_xy = axes_x[0] * axes_y[0] + axes_x[1] * axes_y[1] + axes_x[2] * axes_y[2]
    cov_yy = axes_y[0] * axes_y[0] + axes_y[1] * axes_y[1] + axes_y[2] * axes_y[2] + blur_add
    determ = cov_xx * cov_yy - cov_xy * cov_xy
    opacity = 1.0 / (1.0 + jnp.exp(-raw[10]))
    camera_eye = [
        -(
            camera_turn[0][column] * shift_vec[0]
            + camera_turn[1][column] * shift_vec[1]
            + camera_turn[2][column] * shift_vec[2]
        )
        for column in range(3)
    ]
    offset = [position[column] - camera_eye[column] for column in range(3)]
    length = lax.rsqrt(offset[0] * offset[0] + offset[1] * offset[1] + offset[2] * offset[2])
    harmonic_terms = harmonics(offset[0] * length, offset[1] * length, offset[2] * length)
    colours = []
    for channel in range(3):
        total = 0.5 + jnp.zeros_like(opacity)
        for harmonic in range(16):
            total = total + raw[11 + 16 * channel + harmonic] * harmonic_terms[harmonic]
        colours.append(total)
    return [mean_x, mean_y, cov_yy / determ, -cov_xy / determ, cov_xx / determ, opacity] + colours


def three_pieces(value):
    high = value.astype(jnp.bfloat16)
    rest = value - high.astype(jnp.float32)
    middle = rest.astype(jnp.bfloat16)
    low = (rest - middle.astype(jnp.float32)).astype(jnp.bfloat16)
    return high, middle, low


def two_pieces(value):
    high = value.astype(jnp.bfloat16)
    return high, (value - high.astype(jnp.float32)).astype(jnp.bfloat16)


def matmul(left, right):
    return jnp.dot(left, right, preferred_element_type=jnp.float32)


def matmul_nt(left, right):
    return lax.dot_general(
        left, right, (((1,), (1,)), ((), ())), preferred_element_type=jnp.float32
    )


def visible_row(visible_ref):
    views = visible_ref.shape[0]
    return jnp.concatenate([visible_ref[view : view + 1, :] for view in range(views)], axis=1)


def column_hot(visible_ref, columns):
    ids = visible_row(visible_ref)
    place = lax.broadcasted_iota(jnp.int32, (columns, ids.shape[1]), 0)
    return jnp.where(place == ids, 1.0, 0.0).astype(jnp.bfloat16)


def camera_rows(cameras_ref, own_rows):
    views = cameras_ref.shape[0]
    shape = (views // 2, 2 * own_rows)
    number = 2 * lax.broadcasted_iota(jnp.int32, shape, 0) + jnp.where(
        lax.broadcasted_iota(jnp.int32, shape, 1) >= own_rows, 1, 0
    )
    rows = []
    for entry in range(11):
        row = jnp.full(shape, cameras_ref[0, entry], jnp.float32)
        for view in range(1, views):
            row = jnp.where(number >= view, cameras_ref[view, entry], row)
        rows.append(row)
    return rows


def down(row, lanes):
    spread_row = jnp.broadcast_to(row.astype(jnp.float32), (lanes, row.shape[1]))
    return jnp.transpose(spread_row)


def list_hot_down(lists, lanes):
    ids = down(lax.bitwise_and(lists, lanes - 1), lanes)
    lane = lax.broadcasted_iota(jnp.int32, ids.shape, 1).astype(jnp.float32)
    return jnp.where(ids == lane, 1.0, 0.0).astype(jnp.bfloat16)


def list_hot(lists, lanes):
    place = lax.broadcasted_iota(jnp.int32, (lanes, lists.shape[1]), 0)
    hot = jnp.where(place == lax.bitwise_and(lists, lanes - 1), 1.0, 0.0).astype(jnp.bfloat16)
    return hot, lax.shift_right_logical(lists, lanes.bit_length() - 1)


def step_kernel(
    views, tiles, params_hbm, visible_hbm, cameras_hbm, lists_hbm, counts_hbm, targets_hbm,
    grad_ref, seen_ref, image_ref,
    params_ref, visible_ref, cameras_ref, lists_ref, counts_ref, targets_ref, picked_ref, outgoing, everyone, hot_back, hots, hots_wide, rows, grads,
    weights, weight_parts, ratios, carried, held, given, landed, slopes_ref, folded,
    load_sem, out_sem, out_recv, back_sem, back_recv
):
    my_view, my_tile = lax.axis_index("view"), lax.axis_index("tile")
    owners = views * tiles
    me = my_tile * views + my_view

    partners = []
    for step_view in range(views):
        view = lax.rem(my_view + step_view, views)
        for step_tile in range(tiles):
            if step_view or step_tile:
                tile = lax.rem(my_tile + step_tile, tiles)
                partners.append((tile * views + view, view, tile))
    pairs = (
        (visible_hbm, visible_ref), (cameras_hbm, cameras_ref), (params_hbm, params_ref),
        (lists_hbm, lists_ref), (counts_hbm, counts_ref), (targets_hbm, targets_ref),
    )
    loads = [
        pltpu.make_async_copy(source, held_at, load_sem.at[place])
        for place, (source, held_at) in enumerate(pairs)
    ]
    for load in loads:
        load.start()
    barrier = pltpu.get_barrier_semaphore()

    for _, view, tile in partners:
        pl.semaphore_signal(barrier, inc=1, device_id=(view, tile), device_id_type=MESH)

    width, columns = params_ref.shape
    own_rows = visible_ref.shape[1]
    wide = 2 * own_rows
    loads[0].wait()
    hot = column_hot(visible_ref, columns)
    loads[1].wait()
    cameras = camera_rows(cameras_ref, own_rows)
    loads[2].wait()
    padded = jnp.concatenate(
        [params_ref[...], jnp.zeros((64 - width, columns), jnp.float32)], axis=0
    )
    found = matmul(jnp.concatenate(three_pieces(padded), axis=0), hot)
    found = found[0:64] + found[64:128] + found[128:192]
    folds = views // 2
    for fold in range(folds):
        picked_ref[fold * 64 : (fold + 1) * 64, :] = found[:, fold * wide : (fold + 1) * wide]
    raw = [picked_ref[pl.ds(row, folds, stride=64), :] for row in range(width)]
    out = project(raw, cameras)
    for row in range(9):
        folded[pl.ds(row, folds, stride=2 * SUBS), :] = out[row]
    low_lane = lax.broadcasted_iota(jnp.int32, (4, wide), 1) < own_rows
    for fold in range(folds):
        first = folded[fold * 2 * SUBS : fold * 2 * SUBS + 4, :]
        second = folded[fold * 2 * SUBS + 4 : fold * 2 * SUBS + 8, :]
        last = folded[fold * 2 * SUBS + 8 : fold * 2 * SUBS + 9, :]
        outgoing[2 * fold, 0:4] = jnp.where(low_lane, first, pltpu.roll(second, own_rows, 1))
        outgoing[2 * fold, 4:5] = last
        outgoing[2 * fold + 1, 0:4] = jnp.where(low_lane, pltpu.roll(first, own_rows, 1), second)
        outgoing[2 * fold + 1, 4:5] = pltpu.roll(last, own_rows, 1)

    def to_owner(source, landing, sends, receives, view, tile):
        return pltpu.make_async_remote_copy(
            src_ref=source, dst_ref=landing, send_sem=sends.at[0], recv_sem=receives.at[0],
            device_id=(view, tile), device_id_type=MESH,
        )

    everyone[me] = outgoing[my_view]
    pl.semaphore_wait(barrier, owners - 1)
    for _, view, tile in partners:
        to_owner(outgoing.at[view], everyone.at[me], out_sem, out_recv, view, tile).start()

    for load in loads[3:]:
        load.wait()
    per_device, entries = lists_ref.shape
    groups, groups_wide = [], []
    for tile in range(per_device):
        ids = lists_ref[tile : tile + 1, :]
        narrow, group = list_hot(ids, own_rows)
        hots[tile] = jnp.concatenate([narrow] * 4, axis=0)
        groups.append(jnp.broadcast_to(group, (SUBS, entries)))
        hots_wide[tile] = list_hot_down(ids, wide)
        group = lax.shift_right_logical(ids, wide.bit_length() - 1)
        groups_wide.append(jnp.broadcast_to(group, (SUBS, entries)))

    ids_down = down(visible_row(visible_ref), BLOCK)
    for start in range(0, columns, BLOCK):
        lane_at = lax.broadcasted_iota(jnp.int32, ids_down.shape, 1).astype(jnp.float32) + start
        hot_back[:, start : start + BLOCK] = jnp.where(ids_down == lane_at, 1.0, 0.0).astype(
            jnp.bfloat16
        )
    rest = pl.ds(0, owners - 1)
    _, next_view, next_tile = partners[0]
    all_rows = to_owner(
        everyone.at[rest], everyone.at[rest], out_sem, out_recv, next_view, next_tile
    )
    all_rows.wait_recv()

    batch = max(1, min(tiles, 32 // views))
    chunk = batch * views
    lane = lax.broadcasted_iota(jnp.int32, (chunk * (SUBS + 1), wide), 1)

    def gather(index, held_rows):
        source = everyone[pl.ds(index * chunk, chunk)]
        last = source[:, 4, :]
        source = jnp.concatenate([source, jnp.zeros((chunk, SUBS - PACK, wide), jnp.float32)], axis=1)
        turned = pltpu.roll(pltpu.roll(source, own_rows, 2), 4, 1)
        source = jnp.where(lax.broadcasted_iota(jnp.int32, source.shape, 1) < 4, source, turned)
        source = jnp.concatenate([source.reshape(chunk * SUBS, wide), last], axis=0)
        high, middle, low = [piece.astype(jnp.float32) for piece in three_pieces(source)]
        source = jnp.concatenate(
            [
                jnp.where(lane < own_rows, high, pltpu.roll(middle, own_rows, 1)),
                jnp.where(lane < own_rows, low, 0.0),
            ],
            axis=1,
        ).astype(jnp.bfloat16)
        new_rows = []
        for tile in range(per_device):
            located = matmul(source, hots[tile])
            first, second = held_rows[tile]
            for owner in range(chunk):
                mine = groups[tile] == index * chunk + owner
                first = first + jnp.where(mine, located[owner * SUBS : (owner + 1) * SUBS], 0.0)
            for start in range(0, chunk, SUBS):
                begin = chunk * SUBS + start
                number = lax.broadcasted_iota(jnp.int32, (SUBS, entries), 0) + (
                    index * chunk + start
                )
                second = second + jnp.where(
                    groups[tile] == number, located[begin : begin + SUBS], 0.0
                )
            new_rows.append((first, second))
        return tuple(new_rows)

    empty = jnp.zeros((SUBS, entries), jnp.float32)
    collected = lax.fori_loop(0, tiles // batch, gather, ((empty, empty),) * per_device)
    for tile in range(per_device):
        rows[tile, 0:SUBS, :] = collected[tile][0]
        rows[tile, SUBS : 2 * SUBS, :] = jnp.broadcast_to(
            jnp.sum(collected[tile][1], axis=0, keepdims=True), (SUBS, entries)
        )

    first_tile = my_tile * per_device
    half = SIDE // 2
    middles = []
    for tile in range(per_device):
        number = first_tile + tile
        middles.append(
            (
                (lax.rem(number, WIN_COLS) * SIDE + half).astype(jnp.float32),
                (lax.div(number, WIN_COLS) * SIDE + half).astype(jnp.float32),
            )
        )
    side_x = lax.broadcasted_iota(jnp.int32, (SIDE, BLOCK), 0).astype(jnp.float32) + (0.5 - half)
    spot = lax.bitwise_and(
        lax.broadcasted_iota(jnp.int32, (2 * BLOCK, 2 * BLOCK), 0), BLOCK - 1
    )
    lane_two = lax.broadcasted_iota(jnp.int32, (2 * BLOCK, 2 * BLOCK), 1)
    ahead = jnp.where((spot < lane_two) | (lane_two >= BLOCK), 1.0, 0.0).astype(jnp.bfloat16)
    behind = jnp.where((spot > lane_two) | (lane_two >= BLOCK), 1.0, 0.0)[0:BLOCK]
    behind = behind.astype(jnp.bfloat16)
    blocks = entries // BLOCK
    stride = 8 if blocks % 8 == 0 else 1

    carried[...] = jnp.zeros_like(carried)
    held[...] = jnp.zeros_like(held)

    def forward(block, _):
        start = pl.multiple_of(block * BLOCK, BLOCK)
        for tile in range(per_device):
            live = (block < counts_ref[0, tile]).astype(jnp.float32)
            low = rows[tile, 0:SUBS, pl.ds(start, BLOCK)]
            up = rows[tile, SUBS : 2 * SUBS, pl.ds(start, BLOCK)]
            mean_x = low[0:1] - middles[tile][0]
            mean_y = low[1:2] - middles[tile][1]
            form_a = -0.5 * low[2:3]
            form_b = -low[3:4]
            form_c = -0.5 * low[4:5]
            opacity = low[5:6] * live
            delta_x = side_x - mean_x
            square = form_a * delta_x * delta_x
            cross = form_b * delta_x
            pieces = []
            for line in range(SIDE):
                delta_y = (line + 0.5 - half) - mean_y
                pieces.append((cross + form_c * delta_y) * delta_y + square)
            alpha = opacity * jnp.exp(jnp.concatenate(pieces, axis=0))
            decay = jnp.log(1.0 - alpha)
            before = matmul(jnp.concatenate(two_pieces(decay), axis=1), ahead)
            past = carried[tile]
            weight = alpha * jnp.exp(before[:, 0:BLOCK] + past)
            carried[tile] = past + before[:, BLOCK:]
            ratios[tile, block] = alpha * jnp.exp(-decay)
            weights[tile, block] = weight
            parts = jnp.concatenate(two_pieces(weight), axis=1)
            weight_parts[tile, block] = parts[:, 0:BLOCK]
            colour = jnp.concatenate([low[6:8], up[0:1], jnp.zeros((5, BLOCK), jnp.float32)], axis=0)
            high = colour.astype(jnp.bfloat16).astype(jnp.float32)
            both = jnp.concatenate([high, colour - high], axis=0).astype(jnp.bfloat16)
            held[tile] += matmul_nt(parts, jnp.concatenate([both, both], axis=1))
        return 0

    def forward_pair(index, _):
        for part in range(stride):
            forward(index * stride + part, 0)
        return 0

    lax.fori_loop(0, blocks // stride, forward_pair, 0)

    slopes, slopes_wide = [], []
    for tile in range(per_device):
        drawn = jnp.transpose(
            jnp.concatenate(
                [held[tile], jnp.zeros((PIX, BLOCK - 2 * SUBS), jnp.float32)], axis=1
            )
        )
        drawn = drawn[0:3] + drawn[SUBS : SUBS + 3]
        image_ref[:, 0, tile * PIX : (tile + 1) * PIX] = drawn
        slope = 2.0 * (drawn - targets_ref[:, 0, tile * PIX : (tile + 1) * PIX])
        high = slope.astype(jnp.bfloat16).astype(jnp.float32)
        stack = jnp.concatenate(
            [high, slope - high, high, jnp.zeros((BLOCK - 9, PIX), jnp.float32)], axis=0
        )
        slopes.append(stack[0 : 2 * SUBS].astype(jnp.bfloat16))
        slopes_wide.append(jnp.transpose(stack).astype(jnp.bfloat16)[:, 0 : 2 * SUBS])

    pixel = lax.broadcasted_iota(jnp.int32, (2 * SUBS, PIX), 1)
    kind = lax.broadcasted_iota(jnp.int32, (2 * SUBS, PIX), 0)
    at_x = lax.bitwise_and(pixel, SIDE - 1).astype(jnp.float32) + (0.5 - half)
    at_y = lax.shift_right_logical(pixel, SIDE.bit_length() - 1).astype(jnp.float32) + (0.5 - half)
    power_x = jnp.where((kind == 1) | (kind == 4), at_x, jnp.where(kind == 3, at_x * at_x, 1.0))
    power_y = jnp.where((kind == 2) | (kind == 4), at_y, jnp.where(kind == 5, at_y * at_y, 1.0))
    basis = jnp.where(kind < 6, power_x * power_y, 0.0).astype(jnp.bfloat16)

    carried[...] = jnp.zeros_like(carried)

    def backward(index, _):
        block = blocks - 1 - index
        start = pl.multiple_of(block * BLOCK, BLOCK)
        for tile in range(per_device):
            low = rows[tile, 0:SUBS, pl.ds(start, BLOCK)]
            up = rows[tile, SUBS : 2 * SUBS, pl.ds(start, BLOCK)]
            colour = jnp.concatenate([low[6:8], up[0:1]], axis=0)
            high = colour.astype(jnp.bfloat16).astype(jnp.float32)
            both = jnp.concatenate(
                [high, high, colour - high, jnp.zeros((7, BLOCK), jnp.float32)], axis=0
            ).astype(jnp.bfloat16)
            pulled = matmul(slopes_wide[tile], both) * weights[tile, block]
            after = matmul(pulled.astype(jnp.bfloat16), behind)
            past = carried[tile]
            inner = pulled - (after[:, 0:BLOCK] + past) * ratios[tile, block]
            carried[tile] = past + after[:, BLOCK:]
            sums = matmul(basis, inner.astype(jnp.bfloat16))
            tint = matmul(slopes[tile], weight_parts[tile, block])
            tint = tint[0:3] + tint[3:6]
            mean_x = low[0:1] - middles[tile][0]
            mean_y = low[1:2] - middles[tile][1]
            form_a, form_b, form_c = low[2:3], low[3:4], low[4:5]
            whole, by_x, by_y = sums[0:1], sums[1:2], sums[2:3]
            sum_x = by_x - mean_x * whole
            sum_y = by_y - mean_y * whole
            sum_xx = sums[3:4] - 2.0 * mean_x * by_x + mean_x * mean_x * whole
            sum_xy = sums[4:5] - mean_x * by_y - mean_y * by_x + mean_x * mean_y * whole
            sum_yy = sums[5:6] - 2.0 * mean_y * by_y + mean_y * mean_y * whole
            grads[tile, 0:SUBS, pl.ds(start, BLOCK)] = jnp.concatenate(
                [
                    form_a * sum_x + form_b * sum_y,
                    form_b * sum_x + form_c * sum_y,
                    -0.5 * sum_xx,
                    -sum_xy,
                    -0.5 * sum_yy,
                    whole / low[5:6],
                    tint[0:2],
                ],
                axis=0,
            )
            grads[tile, SUBS : 2 * SUBS, pl.ds(start, BLOCK)] = jnp.broadcast_to(
                tint[2:3], (SUBS, BLOCK)
            )
        return 0

    def backward_pair(index, _):
        for part in range(stride):
            backward(index * stride + part, 0)
        return 0

    lax.fori_loop(0, blocks // stride, backward_pair, 0)

    pairs = chunk // 2
    lane_pair = lax.broadcasted_iota(jnp.int32, (pairs, SUBS, wide), 2)

    def scatter(index, _):
        total = jnp.zeros((2 * pairs * (SUBS + 1), wide), jnp.float32)
        for tile in range(per_device):
            main = grads[tile, 0:SUBS, :]
            last = grads[tile, SUBS : 2 * SUBS, :]
            parts = [[], [], [], []]
            main_high = main.astype(jnp.bfloat16).astype(jnp.float32)
            last_high = last.astype(jnp.bfloat16).astype(jnp.float32)
            for pair in range(pairs):
                mine = groups_wide[tile] == index * pairs + pair
                parts[0].append(jnp.where(mine, main_high, 0.0))
                parts[1].append(jnp.where(mine, main - main_high, 0.0))
            for start in range(0, pairs, SUBS):
                number = lax.broadcasted_iota(jnp.int32, (SUBS, entries), 0) + (
                    index * pairs + start
                )
                mine = groups_wide[tile] == number
                parts[2].append(jnp.where(mine, last_high, 0.0))
                parts[3].append(jnp.where(mine, last - last_high, 0.0))
            left = jnp.concatenate(parts[0] + parts[1] + parts[2] + parts[3], axis=0)
            total = total + matmul(left.astype(jnp.bfloat16), hots_wide[tile])
        size = pairs * SUBS
        main = (total[0:size] + total[size : 2 * size]).reshape(pairs, SUBS, wide)
        last = total[2 * size : 2 * size + pairs] + total[2 * size + pairs :]
        raised = pltpu.roll(main, 4, 1)
        row_pair = lax.broadcasted_iota(jnp.int32, main.shape, 1)
        last_turned = pltpu.roll(last, own_rows, 1)
        low_pair = lane_pair < own_rows
        even = jnp.where(
            row_pair < 4,
            jnp.where(low_pair, main, pltpu.roll(raised, own_rows, 2)),
            jnp.broadcast_to(last[:, None, :], main.shape),
        )
        odd = jnp.where(
            row_pair < 4,
            jnp.where(low_pair, pltpu.roll(main, own_rows, 2), raised),
            jnp.broadcast_to(last_turned[:, None, :], main.shape),
        )
        for pair in range(pairs):
            given[index * chunk + 2 * pair] = even[pair, 0:PACK]
            given[index * chunk + 2 * pair + 1] = odd[pair, 0:PACK]
        return 0

    lax.fori_loop(0, tiles // batch, scatter, 0)

    for other, view, tile in partners:
        to_owner(given.at[other], landed.at[me], back_sem, back_recv, view, tile).start()
    landed[me] = given[me]
    _, pullback = jax.vjp(lambda source: project(source, cameras), raw)
    all_back = to_owner(
        given.at[rest], landed.at[rest], back_sem, back_recv, next_view, next_tile
    )
    all_back.wait_recv()
    arrived = landed[pl.ds(0, views)]
    for tile in range(1, tiles):
        arrived = arrived + landed[pl.ds(tile * views, views)]
    for fold in range(folds):
        even, odd = arrived[2 * fold], arrived[2 * fold + 1]
        odd_turned = pltpu.roll(odd, own_rows, 1)
        even_turned = pltpu.roll(even, own_rows, 1)
        begin = fold * 2 * SUBS
        folded[begin : begin + 4, :] = jnp.where(low_lane, even[0:4], odd_turned[0:4])
        folded[begin + 4 : begin + 8, :] = jnp.where(low_lane, even_turned[0:4], odd[0:4])
        folded[begin + 8 : begin + 9, :] = jnp.where(low_lane[0:1], even[4:5], odd_turned[4:5])
    (returned,) = pullback([folded[pl.ds(row, folds, stride=2 * SUBS), :] for row in range(9)])
    slopes_ref[...] = jnp.ones_like(slopes_ref)
    for row in range(width):
        slopes_ref[pl.ds(row, folds, stride=64), :] = returned[row]
    slopes = jnp.concatenate(
        [slopes_ref[fold * 64 : (fold + 1) * 64, :] for fold in range(folds)], axis=1
    )
    found = matmul(jnp.concatenate(two_pieces(slopes), axis=0), hot_back[...])
    found = found[0:64] + found[64:128]
    grad_ref[...] = found[0:width]
    seen_ref[...] = found[width : width + 1]

    all_rows.wait_send()
    all_back.wait_send()


def update_kernel(
    params_ref, first_ref, second_ref, grad_ref, seen_ref, drawn_ref,
    new_params_ref, new_first_ref, new_second_ref, image_ref
):
    grad = grad_ref[...]
    seen = seen_ref[...] > 0.5
    first, second, params = first_ref[...], second_ref[...], params_ref[...]
    moved_first = beta_first * first + (1.0 - beta_first) * grad
    moved_second = beta_second * second + (1.0 - beta_second) * grad * grad
    moved_params = params - learn_rate * moved_first / (jnp.sqrt(moved_second) + adam_eps)
    new_first_ref[...] = jnp.where(seen, moved_first, first)
    new_second_ref[...] = jnp.where(seen, moved_second, second)
    new_params_ref[...] = jnp.where(seen, moved_params, params)
    image_ref[...] = drawn_ref[...]


def shards(views, tiles, params, first, second, visible, cameras, tile_lists, tile_blocks, targets):
    own_rows = visible.shape[1]
    per_device, entries = tile_lists.shape[1:]
    blocks = entries // BLOCK
    packet = (PACK, 2 * own_rows)
    f32 = jnp.float32
    dma = pltpu.SemaphoreType.DMA
    owners = views * tiles
    image_shape = jax.ShapeDtypeStruct((3, 1, per_device * PIX), f32)
    grad, seen, drawn = pl.pallas_call(
        functools.partial(step_kernel, views, tiles),
        out_shape=[
            jax.ShapeDtypeStruct(params.shape, f32),
            jax.ShapeDtypeStruct((1, params.shape[1]), f32),
            image_shape,
        ],
        in_specs=[ANY] * 6,
        out_specs=[VMEM, VMEM, VMEM],
        scratch_shapes=[
            pltpu.VMEM(params.shape, f32),
            pltpu.VMEM(visible.shape, jnp.int32),
            pltpu.SMEM(cameras.shape, f32),
            pltpu.VMEM((per_device, entries), jnp.int32),
            pltpu.SMEM(tile_blocks.shape, jnp.int32),
            pltpu.VMEM((3, 1, per_device * PIX), f32),
            pltpu.VMEM((64 * views // 2, 2 * own_rows), f32),
            pltpu.VMEM((views,) + packet, f32),
            pltpu.VMEM((owners,) + packet, f32),
            pltpu.VMEM((views * own_rows, params.shape[1]), jnp.bfloat16),
            pltpu.VMEM((per_device, 4 * own_rows, entries), jnp.bfloat16),
            pltpu.VMEM((per_device, entries, 2 * own_rows), jnp.bfloat16),
            pltpu.VMEM((per_device, 2 * SUBS, entries), f32),
            pltpu.VMEM((per_device, 2 * SUBS, entries), f32),
            pltpu.VMEM((per_device, blocks, PIX, BLOCK), f32),
            pltpu.VMEM((per_device, blocks, PIX, BLOCK), jnp.bfloat16),
            pltpu.VMEM((per_device, blocks, PIX, BLOCK), f32),
            pltpu.VMEM((per_device, PIX, BLOCK), f32),
            pltpu.VMEM((per_device, PIX, 2 * SUBS), f32),
            pltpu.VMEM((owners,) + packet, f32),
            pltpu.VMEM((owners,) + packet, f32),
            pltpu.VMEM((64 * views // 2, 2 * own_rows), f32),
            pltpu.VMEM((SUBS * views, 2 * own_rows), f32),
            dma((6,)),
            dma((1,)), dma((1,)), dma((1,)), dma((1,)),
        ],
        compiler_params=pltpu.CompilerParams(
            collective_id=0, has_side_effects=True, vmem_limit_bytes=LIMIT
        ),
        name="render_step",
    )(params, visible, cameras, tile_lists[0], tile_blocks, jnp.transpose(targets, (1, 0, 2)))
    like = jax.ShapeDtypeStruct(params.shape, f32)
    new_params, new_first, new_second, rendered = pl.pallas_call(
        update_kernel,
        out_shape=[like, like, like, image_shape],
        in_specs=[VMEM] * 6,
        out_specs=[VMEM] * 4,
        compiler_params=pltpu.CompilerParams(vmem_limit_bytes=LIMIT),
        name="update",
    )(params, first, second, grad, seen, drawn)
    return (new_params, new_first, new_second, jnp.transpose(rendered, (1, 0, 2)))


def solution(mesh):
    in_specs = (
        P(None, ("view", "tile")),
        P(None, ("view", "tile")),
        P(None, ("view", "tile")),
        P(None, ("view", "tile")),
        P(),
        P("view", "tile", None),
        P("view", "tile"),
        P("view", None, "tile"),
    )
    out_specs = (
        P(None, ("view", "tile")),
        P(None, ("view", "tile")),
        P(None, ("view", "tile")),
        P("view", None, "tile"),
    )
    body = functools.partial(shards, mesh.shape["view"], mesh.shape["tile"])
    return jax.shard_map(body, mesh=mesh, in_specs=in_specs, out_specs=out_specs, check_vma=False)
```
